512 devices in a mesh: pool: 64 (over z, y), tp: 8 (over x, core).
Axes of the slice: x: 4, y: 4, z: 16, core: 2. Of those that a mesh axis runs over, the one named last changes fastest.
Arguments:
- query: bfloat16 [512, 2, 32, 128], P('pool', None, 'tp'), may hold values from -6 to 6
- new_kv: bfloat16 [512, 2, 2, 8, 128], P('pool', None, None, 'tp'), may hold values from -6 to 6
- kv_store: bfloat16 [16384, 2, 8, 16, 128], P('pool', None, 'tp'), may hold values from -6 to 6
- prefix_pages: int32 [256, 8], P('pool'), may hold values from 0 to 16383, as said below
- fork_of: int32 [512], P('pool'), may hold values from 0 to 3, as said below
- own_pages: int32 [512, 24], P('pool'), may hold values from 0 to 16383, as said below
- lengths: int32 [512], P('pool'), may hold values from 129 to 512
- o_weight: bfloat16 [4096, 2560], P('tp'), may hold values from -1.5 to 1.5
Outputs:
- projected: bfloat16 [512, 2, 2560], P('pool', None, 'tp')
The draws below stay inside these ranges and needn't reach their ends.
Inputs may be any that keep to these rules, and one draw needn't show every extreme that they name: `prefix_pages`: page id g lies in the store of instance g // 256, at place g % 256; a page may be named more than once. `own_pages`: ids as for prefix_pages. The own pages of branches 4 to 7 of an instance lie in that instance's store, at distinct places. Of the 128 ids named by an instance's prefixes and by the own pages of its first 4 branches, at most 4 lie in any one store, and exactly 4 in one store, the same store for every instance. `fork_of`: each of an instance's 4 prefixes is named by at least one of its branches.
All inputs are finite; a program needn't handle non-finite values.
Results may differ from the reference program's by a relative error of at most 0.019.
Values may be sent and summed in bfloat16 or wider, within the bound.
No kernel may reach another device: no remote copies, remote signals or barrier semaphores. Data moves between devices by JAX's collectives and lax.ppermute only.
A program may use at most 64 MiB of HBM per device.

```python
import math
import jax
import jax.numpy as jnp
from jax import lax

HD = 128
KVH = 8
QH = 32
DW = 2560
PAGE = 16
NPRE = 8
NOWN = 24
STEPS = 2
B_DEV = 8
MIG = 4
ROOTS = 4
NP = 32
P_DEV = 256
BRANCHES = 512
STORE = 16384
REMOTE = 128
CAP = 4


def query_values(key):
    array_shape = (BRANCHES, STEPS, QH, HD)
    key_a = jax.random.fold_in(jax.random.fold_in(key, 11), 0)
    drawn = jax.random.truncated_normal(key_a, -6.0, 6.0, array_shape, jnp.float32)
    return drawn


def draw_query(key, part):
    return query_values(key).astype(jnp.bfloat16)


def draw_new_kv(key, part):
    queries = query_values(key).reshape(BRANCHES, STEPS, KVH, QH // KVH, HD)
    key_a, key_b = jax.random.split(jax.random.fold_in(key, 12), 2)
    array_shape = (BRANCHES, STEPS, KVH, HD)
    noise = 0.8 * jax.random.truncated_normal(key_a, -4.0, 4.0, array_shape, jnp.float32)
    value_rows = jax.random.truncated_normal(key_b, -6.0, 6.0, array_shape, jnp.float32)
    key_rows = jnp.clip(0.6 * jnp.sum(queries, 3) / math.sqrt(QH // KVH) + noise, -6.0, 6.0)
    return jnp.stack([key_rows, value_rows], 2).astype(jnp.bfloat16)


def draw_kv_store(key, part):
    array_shape = (STORE, 2, KVH, PAGE, HD)
    key_a = jax.random.fold_in(jax.random.fold_in(key, 13), 0)
    drawn = jax.random.truncated_normal(key_a, -6.0, 6.0, array_shape, jnp.float32)
    return drawn.astype(jnp.bfloat16)


def layout(key):
    instances = BRANCHES // B_DEV
    base_key = jax.random.fold_in(key, 5)
    hot_store = jax.random.randint(jax.random.fold_in(base_key, 1), (), 0, instances).astype(jnp.int32)

    def one_instance(inst_key, instance):
        key_a, key_b, key_c, key_d, key_e, key_f = jax.random.split(inst_key, 6)
        cells = jax.random.permutation(key_b, (instances - 1) * CAP)[:REMOTE - CAP].astype(jnp.int32)
        bin_of = jnp.concatenate([jnp.zeros((CAP,), jnp.int32), 1 + cells // CAP])
        bin_of = jax.random.permutation(key_a, bin_of)
        others = jax.random.permutation(key_c, instances - 1).astype(jnp.int32)
        holder = jnp.where(bin_of == 0, hot_store, (hot_store + 1 + others[jnp.maximum(bin_of - 1, 0)]) % instances)
        offset = jax.random.randint(key_d, (REMOTE,), 0, P_DEV).astype(jnp.int32)
        remote = holder * P_DEV + offset
        prefix = remote[:ROOTS * NPRE].reshape(ROOTS, NPRE)
        moved_ids = remote[ROOTS * NPRE:].reshape(MIG, NOWN)
        resident = instance * P_DEV + jax.random.permutation(key_e, P_DEV).astype(jnp.int32)[:(B_DEV - MIG) * NOWN]
        own_ids = jnp.concatenate([moved_ids, resident.reshape(B_DEV - MIG, NOWN)], 0)
        extra = jax.random.randint(jax.random.fold_in(key_f, 1), (B_DEV - ROOTS,), 0, ROOTS).astype(jnp.int32)
        fork_ids = jax.random.permutation(key_f, jnp.concatenate([jnp.arange(ROOTS, dtype=jnp.int32), extra]))
        return (prefix, own_ids, fork_ids)
    inst_keys = jax.random.split(jax.random.fold_in(base_key, 2), instances)
    prefix, own_ids, fork_ids = jax.vmap(one_instance)(inst_keys, jnp.arange(instances, dtype=jnp.int32))
    return (prefix.reshape(instances * ROOTS, NPRE).astype(jnp.int32), own_ids.reshape(BRANCHES, NOWN).astype(jnp.int32), fork_ids.reshape(BRANCHES).astype(jnp.int32))


def draw_prefix_pages(key, part):
    return layout(key)[0]


def draw_own_pages(key, part):
    return layout(key)[1]


def draw_fork_of(key, part):
    return layout(key)[2]


def plant(values, own_key, smallest, top_value):
    spot = [jax.random.randint(jax.random.fold_in(own_key, axis), (), 0, length) for axis, length in enumerate(values.shape)]
    main_axis = values.shape.index(max(values.shape))
    beside = spot[:main_axis] + [(spot[main_axis] + 1) % values.shape[main_axis]] + spot[main_axis + 1:]
    return values.at[tuple(spot)].set(smallest).at[tuple(beside)].set(top_value)


def shard_levels(stream_key, dims, cuts, low, largest):
    loudness, own = 1.0, jax.random.fold_in(stream_key, 6)
    for dim, parts in cuts:
        heights = jnp.exp(jax.random.uniform(jax.random.fold_in(own, dim), (parts,), jnp.float32, low / len(cuts), largest / len(cuts)))
        loudness = loudness * jnp.repeat(heights, dims[dim] // parts).reshape([-1 if axis == dim else 1 for axis in range(len(dims))])
    return loudness


def centred(stream_key, extent, scale, reach, cuts=(), kind=jnp.bfloat16):
    values = scale * jax.random.normal(stream_key, extent, jnp.float32)
    if cuts:
        values = values * shard_levels(stream_key, extent, cuts, -0.22, 0.18)
    return jnp.clip(values, -reach, reach).astype(kind)


def setup_inputs(seed: int = 0) -> dict:
    key_of = jax.random.split(jax.random.key(seed), 9)
    return {
        "query": draw_query(jax.random.fold_in(key_of[8], 71), 0),
        "new_kv": draw_new_kv(jax.random.fold_in(key_of[8], 71), 0),
        "kv_store": draw_kv_store(jax.random.fold_in(key_of[8], 71), 0),
        "prefix_pages": draw_prefix_pages(jax.random.fold_in(key_of[8], 71), 0),
        "fork_of": draw_fork_of(jax.random.fold_in(key_of[8], 71), 0),
        "own_pages": draw_own_pages(jax.random.fold_in(key_of[8], 71), 0),
        "lengths": plant(jax.random.randint(key_of[6], (BRANCHES,), NPRE * PAGE + 1, NP * PAGE + 1), jax.random.fold_in(key_of[6], 1), NPRE * PAGE + 1, NP * PAGE).astype(jnp.int32),
        "o_weight": centred(key_of[7], (QH * HD, DW), 16 ** -0.5, 1.5, ((0, 8),)),
    }


def block_parts(queries, key_rows, value_rows, allowed, contract, apply):
    scores = jnp.einsum(contract, queries.astype(jnp.float32), key_rows.astype(jnp.float32)) * (1.0 / math.sqrt(HD))
    scores = jnp.where(allowed, scores, -1e+30)
    block_top = lax.optimization_barrier(jnp.max(scores, -1))
    weights = jnp.where(allowed, jnp.exp(scores - block_top[..., None]), 0.0).astype(jnp.bfloat16)
    totals = lax.optimization_barrier(jnp.sum(weights.astype(jnp.float32), -1))
    weighted = jnp.einsum(apply, weights.astype(jnp.float32), value_rows.astype(jnp.float32))
    return (block_top, totals, weighted)

def attend(query_rows, fresh_kv, page_set, length_row):
    branch_count = query_rows.shape[0]
    queries = query_rows.reshape(branch_count, STEPS, KVH, QH // KVH, HD)
    position = jnp.arange(NP * PAGE, dtype=jnp.int32).reshape(NP, PAGE)
    usable = (position[None] < length_row[:, None, None])[:, None, None, None]
    block_top, totals, weighted = block_parts(queries, page_set[:, :, 0], page_set[:, :, 1], usable, 'btkgd,bpkjd->btkgpj', 'btkgpj,bpkjd->btkgpd')
    steps_row = jnp.arange(STEPS, dtype=jnp.int32)
    causal = (steps_row[None, :] <= steps_row[:, None])[None, :, None, None, :]
    new_top, new_total, new_weighted = block_parts(queries, fresh_kv[:, :, 0], fresh_kv[:, :, 1], causal, 'btkgd,bnkd->btkgn', 'btkgn,bnkd->btkgd')
    row_top = jnp.maximum(lax.optimization_barrier(jnp.max(block_top, -1)), new_top)
    factor = jnp.exp(block_top - row_top[..., None])
    new_factor = jnp.exp(new_top - row_top)
    numerator = lax.optimization_barrier(jnp.sum(factor[..., None] * weighted, -2)) + new_factor[..., None] * new_weighted
    denominator = lax.optimization_barrier(jnp.sum(factor * totals, -1)) + new_factor * new_total
    attended = (numerator / denominator[..., None]).astype(jnp.bfloat16)
    return attended.reshape(branch_count, STEPS, QH * HD)

def reference(query, new_kv, kv_store, prefix_pages, fork_of, own_pages, lengths, o_weight):
    instances = BRANCHES // B_DEV

    def one_instance(pieces):
        query_rows, fresh_kv, prefix_rows, fork_row, own_rows, length_row = pieces
        prefix_ids = jnp.take(prefix_rows, fork_row, axis=0)
        page_ids = jnp.concatenate([prefix_ids, own_rows], 1).astype(jnp.int32)
        page_set = jnp.take(kv_store, page_ids.reshape(-1), axis=0).reshape(B_DEV, NP, 2, KVH, PAGE, HD)
        return attend(query_rows, fresh_kv, page_set, length_row)
    attended = lax.map(one_instance, (query.reshape(instances, B_DEV, STEPS, QH, HD), new_kv.reshape(instances, B_DEV, STEPS, 2, KVH, HD), prefix_pages.reshape(instances, ROOTS, NPRE), fork_of.reshape(instances, B_DEV), own_pages.reshape(instances, B_DEV, NOWN), lengths.reshape(instances, B_DEV)))
    flattened = attended.reshape(BRANCHES * STEPS, QH * HD)
    projected = jnp.dot(flattened, o_weight, preferred_element_type=jnp.float32).astype(jnp.bfloat16)
    return projected.reshape(BRANCHES, STEPS, DW)
```

```python
import math

import jax
import jax.numpy as jnp
from jax import lax
from jax.experimental import pallas as pl
from jax.experimental.pallas import tpu as pltpu
from jax.sharding import Mesh
from jax.sharding import PartitionSpec as P

F32 = jnp.float32
BF16 = jnp.bfloat16
I32 = jnp.int32

HD = 128
PAGE = 16
NPRE = 8
NOWN = 24
ROOTS = 4
B = 8
MIG = 4
STEPS = 2
GROUP = 4
ROWS = B * STEPS * GROUP
SLOTS = 4
P_DEV = 256
NEG = -(2.0**100)
SCALE = 1.0 / math.sqrt(HD)
ZN, YN, XN, CN = 16, 4, 4, 2
POOL = ZN * YN
TPN = XN * CN
PREFIX_IDS = ROOTS * NPRE
KEYS = SLOTS * PAGE
PAGE_ROWS = ZN * KEYS
CHUNK = 2 * PAGE_ROWS + ZN
RES = ROWS + 16

VMEM = pl.BlockSpec(memory_space=pltpu.VMEM)
SMEM = pl.BlockSpec(memory_space=pltpu.SMEM)
NT = (((1,), (1,)), ((), ()))
NN = (((1,), (0,)), ((), ()))


def iota(shape, dim):
    return lax.broadcasted_iota(I32, shape, dim)


def dot(a, b, dims=NN):
    return lax.dot_general(a, b, dims, preferred_element_type=F32)


def request_kernel(prefix, own, fork, length, req):
    lane = iota((8, HD), 1)
    row = iota((8, HD), 0)
    ids = jnp.zeros((8, HD), I32)
    for r in range(ROOTS):
        for c in range(NPRE):
            ids = jnp.where(lane == r * NPRE + c, prefix[r, c], ids)
    for r in range(MIG):
        for c in range(NOWN):
            ids = jnp.where(lane == PREFIX_IDS + r * NOWN + c, own[r, c], ids)
    forks = jnp.zeros((8, HD), I32)
    lens = jnp.zeros((8, HD), I32)
    for b in range(B):
        forks = jnp.where(row == b, fork[b], forks)
        lens = jnp.where(row == b, length[b], lens)
    is_prefix = lane < PREFIX_IDS
    moved = jnp.maximum(lane - PREFIX_IDS, 0)
    chunk = jnp.where(is_prefix, lane % NPRE, NPRE + moved % NOWN)
    wanted = (is_prefix & (forks == lane // NPRE)) | (~is_prefix & (row == moved // NOWN))
    tokens = jnp.where(wanted, jnp.clip(lens - PAGE * chunk, 0, PAGE), 0)
    place = jnp.where(row == 0, ids % P_DEV, 0)
    table = jnp.concatenate([tokens, place], 0).astype(F32).astype(BF16)
    holder = jnp.broadcast_to((ids // P_DEV)[0:1], (POOL, HD))
    member = holder == iota((POOL, HD), 0)
    earlier = (iota((HD, HD), 0) < iota((HD, HD), 1)).astype(F32).astype(BF16)
    rank = dot(member.astype(F32).astype(BF16), earlier)
    out = jnp.zeros((POOL, HD), F32)
    for s in range(SLOTS):
        chosen = jnp.where(member & (rank == float(s)), 1.0, 0.0).astype(BF16)
        parts = [table if k == s else jnp.zeros((16, HD), BF16) for k in range(HD // 16)]
        out = out + dot(chosen, jnp.concatenate(parts, 0), NT)
    req[...] = out.astype(I32)


def spread_kernel(q, out):
    out[...] = jnp.broadcast_to(q[...][None], (ZN, ROWS, HD))


def gather_kernel(places, req, store, out):
    def instance(i, carry):
        y = i % YN
        z = i // YN
        for s in range(SLOTS):
            at = places[i, 16 * s + 8]
            start = pl.multiple_of(z * KEYS + s * PAGE, PAGE)
            out[y, pl.ds(start, PAGE), :] = store[at, 0]
            out[y, pl.ds(PAGE_ROWS + start, PAGE), :] = store[at, 1]
        return carry

    lax.fori_loop(0, POOL, instance, 0, unroll=8)
    rows = req[...].astype(F32)
    for y in range(YN):
        tile = jnp.zeros((ZN, HD), F32)
        for z in range(ZN):
            i = z * YN + y
            tile = jnp.where(iota((ZN, HD), 0) == z, rows[i : i + 1], tile)
        out[y, pl.ds(2 * PAGE_ROWS, ZN), :] = tile.astype(BF16)


def local_kernel(own, length, q, fresh_k, fresh_v, store, sums, top, total, keys, values):
    branches = B - MIG
    span = NOWN * PAGE
    for b in range(branches):
        for p in range(NOWN):
            at = own[MIG + b, p] % P_DEV
            start = b * span + p * PAGE
            keys[pl.ds(start, PAGE), :] = store[at, 0]
            values[pl.ds(start, PAGE), :] = store[at, 1]
    rows = q[...]
    branch_of = (iota((ROWS, 1), 0) % 16) // STEPS
    step_of = iota((ROWS, 1), 0) % STEPS
    lane16 = iota((ROWS, 16), 1)
    score = dot(rows, fresh_k[...], NT) * SCALE
    ok = (lane16 // STEPS == branch_of) & (lane16 % STEPS <= step_of)
    blocks = [(jnp.where(ok, score, NEG), ok, fresh_v[...])]
    position = iota((ROWS, span), 1) + NPRE * PAGE
    for b in range(branches):
        score = dot(rows, keys[pl.ds(b * span, span), :], NT) * SCALE
        ok = (branch_of == MIG + b) & (position < length[MIG + b])
        blocks.append((jnp.where(ok, score, NEG), ok, values[pl.ds(b * span, span), :]))
    best = jnp.max(blocks[0][0], 1, keepdims=True)
    for score, _, _ in blocks[1:]:
        best = jnp.maximum(best, jnp.max(score, 1, keepdims=True))
    acc = jnp.zeros((ROWS, HD), F32)
    count = jnp.zeros((ROWS, 1), F32)
    for score, ok, value in blocks:
        weight = jnp.where(ok, jnp.exp(score - best), 0.0).astype(BF16)
        count = count + jnp.sum(weight.astype(F32), 1, keepdims=True)
        acc = acc + dot(weight, value)
    sums[...] = acc
    top[...] = jnp.broadcast_to(best, (ROWS, HD))
    total[...] = jnp.broadcast_to(count, (ROWS, HD))


def partial_kernel(pages, queries, out):
    lane = iota((16, HD), 1)
    branch = iota((16, HD), 0) // STEPS
    pick = lane % 16 == branch
    blocks = []
    for y in range(YN):
        tile = pages[y, pl.ds(2 * PAGE_ROWS, ZN), :].astype(F32)
        blocks.append(
            jnp.concatenate(
                [jnp.where(pick, jnp.broadcast_to(tile[z : z + 1], (16, HD)), 0.0).astype(BF16) for z in range(ZN)], 0
            )
        )
    width = YN * KEYS
    shape = (YN * HD, width)
    source, key = iota(shape, 0), iota(shape, 1)
    expand = (source // HD == key // KEYS) & ((source % HD) // 16 == (key % KEYS) // PAGE)
    tokens = dot(jnp.concatenate(blocks, 1), expand.astype(F32).astype(BF16))
    slot_token = (iota((16, width), 1) % PAGE).astype(F32)
    column = iota((ROWS, HD), 1)
    stats = jnp.zeros((ROWS, HD), F32)
    for z in range(ZN):
        ok = slot_token < tokens[z * 16 : (z + 1) * 16]
        ok = jnp.concatenate([jnp.where(ok, 1.0, 0.0)] * GROUP, 0) > 0.5
        keys = jnp.concatenate([pages[y, pl.ds(z * KEYS, KEYS), :] for y in range(YN)], 0)
        values = jnp.concatenate([pages[y, pl.ds(PAGE_ROWS + z * KEYS, KEYS), :] for y in range(YN)], 0)
        score = jnp.where(ok, dot(queries[z], keys, NT) * SCALE, NEG)
        best = jnp.max(score, 1, keepdims=True).astype(BF16).astype(F32)
        weight = jnp.where(ok, jnp.exp(score - best), 0.0).astype(BF16)
        count = jnp.sum(weight.astype(F32), 1, keepdims=True)
        out[z, pl.ds(0, ROWS), :] = dot(weight, values).astype(BF16)
        stats = jnp.where(column == z, best, jnp.where(column == ZN + z, count, stats))
    turned = jnp.transpose(stats)
    tops = turned[0:ZN]
    counts = turned[ZN : 2 * ZN]
    high = counts.astype(BF16).astype(F32)
    low = counts - high
    row = iota((16, ROWS), 0)
    for z in range(ZN):
        tile = jnp.where(row == 1, high[z : z + 1], jnp.where(row == 2, low[z : z + 1], 0.0))
        tile = jnp.where(row == 0, tops[z : z + 1], tile).astype(BF16)
        out[z, pl.ds(ROWS, 16), :] = jnp.concatenate([tile, jnp.zeros((16, HD - ROWS), BF16)], 1)


def finish_kernel(parts, sums, top, total, weight, out):
    row = iota((ZN, HD), 0)
    tops = jnp.full((ZN, HD), NEG, F32)
    counts = jnp.zeros((ZN, HD), F32)
    for z in range(ZN):
        tile = parts[z, pl.ds(ROWS, 16), :].astype(F32)
        tops = jnp.where(row == z, tile[0:1], tops)
        counts = jnp.where(row == z, tile[1:2] + tile[2:3], counts)
    tops = jnp.concatenate([tops, jnp.full((HD - ZN, HD), NEG, F32)], 0)
    counts = jnp.concatenate([counts, jnp.zeros((HD - ZN, HD), F32)], 0)
    tops = jnp.transpose(tops)[0:ROWS]
    counts = jnp.transpose(counts)[0:ROWS]
    own_top = top[...]
    best = jnp.maximum(jnp.max(tops, 1, keepdims=True), own_top)
    factor = jnp.exp(tops - best)
    own_factor = jnp.exp(own_top - best)
    denominator = jnp.sum(factor * counts, 1, keepdims=True) + own_factor * total[...]
    numerator = own_factor * sums[...]
    for z in range(ZN):
        numerator = numerator + factor[:, z : z + 1] * parts[z, pl.ds(0, ROWS), :].astype(F32)
    attended = (numerator / denominator).astype(BF16)
    attended = jnp.concatenate([attended[16 * g : 16 * (g + 1)] for g in range(GROUP)], 1)
    result = dot(attended, weight[...]).astype(BF16).astype(F32)
    width = out.shape[2]
    for k in range(TPN):
        out[k] = result[:, k * width : (k + 1) * width].astype(BF16)


def call(kernel, out_shape, in_specs, name, scratch=(), cost=None):
    return pl.pallas_call(
        kernel,
        out_shape=out_shape,
        in_specs=in_specs,
        out_specs=jax.tree.map(lambda _: VMEM, out_shape),
        scratch_shapes=scratch,
        cost_estimate=cost,
        compiler_params=pltpu.CompilerParams(vmem_limit_bytes=40 * 2**20),
        name=name,
    )


def swap(x, axes):
    return lax.all_to_all(x, axes, split_axis=0, concat_axis=0, tiled=True)


def shards(query, new_kv, kv_store, prefix_pages, fork_of, own_pages, lengths, o_weight):
    shape = jax.ShapeDtypeStruct
    store = kv_store.reshape(P_DEV, 2, PAGE, HD)
    request = call(request_kernel, shape((POOL, HD), I32), [SMEM] * 4, "request")(
        prefix_pages, own_pages, fork_of, lengths
    )
    request = swap(request, ("z", "y"))
    q = query.transpose(2, 0, 1, 3).reshape(ROWS, HD)
    queries = call(spread_kernel, shape((ZN, ROWS, HD), BF16), [VMEM], "spread")(q)
    queries = swap(queries, "z")
    fresh_k = new_kv[:, :, 0, 0].reshape(B * STEPS, HD)
    fresh_v = new_kv[:, :, 1, 0].reshape(B * STEPS, HD)
    local = call(
        local_kernel,
        [shape((ROWS, HD), F32)] * 3,
        [SMEM, SMEM, VMEM, VMEM, VMEM, VMEM],
        "resident",
        [pltpu.VMEM(((B - MIG) * NOWN * PAGE, HD), BF16)] * 2,
        pl.CostEstimate(flops=10**8, bytes_accessed=3 * 2**20, transcendentals=10**5),
    )(own_pages, lengths, q, fresh_k, fresh_v, store)
    pages = call(gather_kernel, shape((YN, CHUNK, HD), BF16), [SMEM, VMEM, VMEM], "gather_pages")(
        request, request, store
    )
    pages = swap(pages, "y")
    parts = call(partial_kernel, shape((ZN, RES, HD), BF16), [VMEM, VMEM], "partials")(pages, queries)
    parts = swap(parts, "z")
    width = o_weight.shape[1] // TPN
    shares = call(finish_kernel, shape((TPN, 16, width), BF16), [VMEM] * 5, "finish")(parts, *local, o_weight)
    shares = swap(shares, ("x", "c"))
    return jnp.sum(shares.astype(F32), 0).astype(BF16).reshape(B, STEPS, width)


def solution(mesh):
    fine = Mesh(mesh.devices.reshape(ZN, YN, XN, CN), ("z", "y", "x", "c"))
    pool, tp = ("z", "y"), ("x", "c")
    return jax.shard_map(
        shards,
        mesh=fine,
        in_specs=(
            P(pool, None, tp, None),
            P(pool, None, None, tp, None),
            P(pool, None, tp, None, None),
            P(pool, None),
            P(pool),
            P(pool, None),
            P(pool),
            P(tp, None),
        ),
        out_specs=P(pool, None, tp),
        check_vma=False,
    )
```

```python
import math

import jax
import jax.numpy as jnp
from jax import lax
from jax.experimental import pallas as pl
from jax.experimental.pallas import tpu as pltpu
from jax.sharding import Mesh
from jax.sharding import PartitionSpec as P

F32 = jnp.float32
BF16 = jnp.bfloat16
I32 = jnp.int32

HD = 128
PAGE = 16
NPRE = 8
NOWN = 24
ROOTS = 4
B = 8
MIG = 4
STEPS = 2
GROUP = 4
ROWS = B * STEPS * GROUP
SLOTS = 4
P_DEV = 256
NEG = -(2.0**100)
SCALE = 1.0 / math.sqrt(HD)
ZN, YN, XN, CN = 16, 4, 4, 2
POOL = ZN * YN
TPN = XN * CN
PREFIX_IDS = ROOTS * NPRE
KEYS = SLOTS * PAGE
PAGE_ROWS = ZN * KEYS
CHUNK = 2 * PAGE_ROWS + ZN
RES = ROWS + 16

VMEM = pl.BlockSpec(memory_space=pltpu.VMEM)
SMEM = pl.BlockSpec(memory_space=pltpu.SMEM)
HBM = pl.BlockSpec(memory_space=pltpu.HBM)
NT = (((1,), (1,)), ((), ()))
NN = (((1,), (0,)), ((), ()))


def iota(shape, dim):
    return lax.broadcasted_iota(I32, shape, dim)


def dot(a, b, dims=NN):
    return lax.dot_general(a, b, dims, preferred_element_type=F32)


def request_kernel(prefix_hbm, own_hbm, fork_hbm, length_hbm, req, prefix, own, fork, length, sems):
    pairs = ((prefix_hbm, prefix), (own_hbm, own), (fork_hbm, fork), (length_hbm, length))
    copies = [pltpu.make_async_copy(a, b, sems.at[n]) for n, (a, b) in enumerate(pairs)]
    for copy in copies:
        copy.start()
    for copy in copies:
        copy.wait()
    lane = iota((8, HD), 1)
    row = iota((8, HD), 0)
    ids = jnp.zeros((8, HD), I32)
    for r in range(ROOTS):
        for c in range(NPRE):
            ids = jnp.where(lane == r * NPRE + c, prefix[r, c], ids)
    for r in range(MIG):
        for c in range(NOWN):
            ids = jnp.where(lane == PREFIX_IDS + r * NOWN + c, own[r, c], ids)
    forks = jnp.zeros((8, HD), I32)
    lens = jnp.zeros((8, HD), I32)
    for b in range(B):
        forks = jnp.where(row == b, fork[b], forks)
        lens = jnp.where(row == b, length[b], lens)
    is_prefix = lane < PREFIX_IDS
    moved = jnp.maximum(lane - PREFIX_IDS, 0)
    chunk = jnp.where(is_prefix, lane % NPRE, NPRE + moved % NOWN)
    wanted = (is_prefix & (forks == lane // NPRE)) | (~is_prefix & (row == moved // NOWN))
    tokens = jnp.where(wanted, jnp.clip(lens - PAGE * chunk, 0, PAGE), 0)
    place = jnp.where(row == 0, ids % P_DEV, 0)
    table = jnp.concatenate([tokens, place], 0).astype(F32).astype(BF16)
    holder = ids // P_DEV
    holder = (holder % YN) * ZN + holder // YN
    member = jnp.broadcast_to(holder[0:1], (POOL, HD)) == iota((POOL, HD), 0)
    earlier = (iota((HD, HD), 0) < iota((HD, HD), 1)).astype(F32).astype(BF16)
    rank = dot(member.astype(F32).astype(BF16), earlier)
    out = jnp.zeros((POOL, HD), F32)
    for s in range(SLOTS):
        chosen = jnp.where(member & (rank == float(s)), 1.0, 0.0).astype(BF16)
        parts = [table if k == s else jnp.zeros((16, HD), BF16) for k in range(HD // 16)]
        out = out + dot(chosen, jnp.concatenate(parts, 0), NT)
    req[...] = out.astype(I32)


def spread_kernel(q, out):
    out[...] = jnp.broadcast_to(q[...][None], (ZN, ROWS, HD))


def prefetch_kernel(source, out, sem):
    copy = pltpu.make_async_copy(source, out, sem)
    copy.start()
    copy.wait()


def gather_kernel(column, places, req, store, *refs):
    outs, stages, sems = refs[:YN], refs[YN : 2 * YN], refs[2 * YN]
    copies = []
    for k, stage in enumerate(stages):
        base = ((column[0] + k) % YN) * ZN
        for z in range(ZN):
            for s in range(SLOTS):
                at = places[base + z, 16 * s + 8]
                start = z * KEYS + s * PAGE
                stage[pl.ds(start, PAGE), :] = store[at, 0]
                stage[pl.ds(PAGE_ROWS + start, PAGE), :] = store[at, 1]
        rows = req[pl.ds(pl.multiple_of(base, ZN), ZN), :]
        stage[pl.ds(2 * PAGE_ROWS, ZN), :] = rows.astype(F32).astype(BF16)
        copy = pltpu.make_async_copy(stage, outs[k], sems.at[k])
        copy.start()
        copies.append(copy)
    for copy in copies:
        copy.wait()


def local_kernel(own, length, q, fresh_k, fresh_v, store, sums, top, total, keys, values):
    branches = B - MIG
    span = NOWN * PAGE
    for b in range(branches):
        for p in range(NOWN):
            at = own[MIG + b, p] % P_DEV
            start = b * span + p * PAGE
            keys[pl.ds(start, PAGE), :] = store[at, 0]
            values[pl.ds(start, PAGE), :] = store[at, 1]
    rows = q[...]
    branch_of = (iota((ROWS, 1), 0) % 16) // STEPS
    step_of = iota((ROWS, 1), 0) % STEPS
    lane16 = iota((ROWS, 16), 1)
    score = dot(rows, fresh_k[...], NT) * SCALE
    ok = (lane16 // STEPS == branch_of) & (lane16 % STEPS <= step_of)
    blocks = [(jnp.where(ok, score, NEG), ok, fresh_v[...])]
    position = iota((ROWS, span), 1) + NPRE * PAGE
    for b in range(branches):
        score = dot(rows, keys[pl.ds(b * span, span), :], NT) * SCALE
        ok = (branch_of == MIG + b) & (position < length[MIG + b])
        blocks.append((jnp.where(ok, score, NEG), ok, values[pl.ds(b * span, span), :]))
    best = jnp.max(blocks[0][0], 1, keepdims=True)
    for score, _, _ in blocks[1:]:
        best = jnp.maximum(best, jnp.max(score, 1, keepdims=True))
    acc = jnp.zeros((ROWS, HD), F32)
    count = jnp.zeros((ROWS, 1), F32)
    for score, ok, value in blocks:
        weight = jnp.where(ok, jnp.exp(score - best), 0.0).astype(BF16)
        count = count + jnp.sum(weight.astype(F32), 1, keepdims=True)
        acc = acc + dot(weight, value)
    sums[...] = acc
    top[...] = jnp.broadcast_to(best, (ROWS, HD))
    total[...] = jnp.broadcast_to(count, (ROWS, HD))


def partial_kernel(own, p1, p2, p3, queries, out, p0, sem):
    copy = pltpu.make_async_copy(own, p0, sem)
    copy.start()
    pages = (p0, p1, p2, p3)
    copy.wait()
    lane = iota((16, HD), 1)
    branch = iota((16, HD), 0) // STEPS
    pick = lane % 16 == branch
    blocks = []
    for y in range(YN):
        tile = pages[y][pl.ds(2 * PAGE_ROWS, ZN), :].astype(F32)
        blocks.append(
            jnp.concatenate(
                [jnp.where(pick, jnp.broadcast_to(tile[z : z + 1], (16, HD)), 0.0).astype(BF16) for z in range(ZN)], 0
            )
        )
    width = YN * KEYS
    shape = (YN * HD, width)
    source, key = iota(shape, 0), iota(shape, 1)
    expand = (source // HD == key // KEYS) & ((source % HD) // 16 == (key % KEYS) // PAGE)
    tokens = dot(jnp.concatenate(blocks, 1), expand.astype(F32).astype(BF16))
    slot_token = (iota((16, width), 1) % PAGE).astype(F32)
    column = iota((ROWS, HD), 1)
    stats = jnp.zeros((ROWS, HD), F32)
    for z in range(ZN):
        ok = slot_token < tokens[z * 16 : (z + 1) * 16]
        ok = jnp.concatenate([jnp.where(ok, 1.0, 0.0)] * GROUP, 0) > 0.5
        keys = jnp.concatenate([pages[y][pl.ds(z * KEYS, KEYS), :] for y in range(YN)], 0)
        values = jnp.concatenate([pages[y][pl.ds(PAGE_ROWS + z * KEYS, KEYS), :] for y in range(YN)], 0)
        score = jnp.where(ok, dot(queries[z], keys, NT) * SCALE, NEG)
        best = jnp.max(score, 1, keepdims=True).astype(BF16).astype(F32)
        weight = jnp.where(ok, jnp.exp(score - best), 0.0).astype(BF16)
        count = jnp.sum(weight.astype(F32), 1, keepdims=True)
        out[z, pl.ds(0, ROWS), :] = dot(weight, values).astype(BF16)
        stats = jnp.where(column == z, best, jnp.where(column == ZN + z, count, stats))
    turned = jnp.transpose(stats)
    tops = turned[0:ZN]
    counts = turned[ZN : 2 * ZN]
    high = counts.astype(BF16).astype(F32)
    low = counts - high
    row = iota((16, ROWS), 0)
    for z in range(ZN):
        tile = jnp.where(row == 1, high[z : z + 1], jnp.where(row == 2, low[z : z + 1], 0.0))
        tile = jnp.where(row == 0, tops[z : z + 1], tile).astype(BF16)
        out[z, pl.ds(ROWS, 16), :] = jnp.concatenate([tile, jnp.zeros((16, HD - ROWS), BF16)], 1)


def finish_kernel(parts, sums, top, total, weight_hbm, out, weight, sem):
    copy = pltpu.make_async_copy(weight_hbm, weight, sem)
    copy.start()
    row = iota((ZN, HD), 0)
    tops = jnp.full((ZN, HD), NEG, F32)
    counts = jnp.zeros((ZN, HD), F32)
    for z in range(ZN):
        tile = parts[z, pl.ds(ROWS, 16), :].astype(F32)
        tops = jnp.where(row == z, tile[0:1], tops)
        counts = jnp.where(row == z, tile[1:2] + tile[2:3], counts)
    tops = jnp.concatenate([tops, jnp.full((HD - ZN, HD), NEG, F32)], 0)
    counts = jnp.concatenate([counts, jnp.zeros((HD - ZN, HD), F32)], 0)
    tops = jnp.transpose(tops)[0:ROWS]
    counts = jnp.transpose(counts)[0:ROWS]
    own_top = top[...]
    best = jnp.maximum(jnp.max(tops, 1, keepdims=True), own_top)
    factor = jnp.exp(tops - best)
    own_factor = jnp.exp(own_top - best)
    denominator = jnp.sum(factor * counts, 1, keepdims=True) + own_factor * total[...]
    numerator = own_factor * sums[...]
    for z in range(ZN):
        numerator = numerator + factor[:, z : z + 1] * parts[z, pl.ds(0, ROWS), :].astype(F32)
    attended = (numerator / denominator).astype(BF16)
    attended = jnp.concatenate([attended[16 * g : 16 * (g + 1)] for g in range(GROUP)], 1)
    copy.wait()
    result = dot(attended, weight[...]).astype(BF16).astype(F32)
    width = out.shape[2]
    for k in range(TPN):
        out[k] = result[:, k * width : (k + 1) * width].astype(BF16)


def total_kernel(shares, out):
    total = shares[0].astype(F32)
    for k in range(1, TPN):
        total = total + shares[k].astype(F32)
    total = total.astype(BF16).astype(F32)
    for b in range(B):
        out[b] = total[STEPS * b : STEPS * (b + 1)].astype(BF16)


def call(kernel, out_shape, in_specs, name, scratch=(), cost=None, mib=12, out_specs=None):
    return pl.pallas_call(
        kernel,
        out_shape=out_shape,
        in_specs=in_specs,
        out_specs=jax.tree.map(lambda _: VMEM, out_shape) if out_specs is None else out_specs,
        scratch_shapes=scratch,
        cost_estimate=cost,
        compiler_params=pltpu.CompilerParams(vmem_limit_bytes=mib * 2**20),
        name=name,
    )


def hbm(x):
    return pltpu.with_memory_space_constraint(x, pltpu.HBM)


def vmem(x):
    return pltpu.with_memory_space_constraint(x, pltpu.VMEM)


def prefetch(x, name):
    return call(
        prefetch_kernel, pltpu.VMEM(x.shape, x.dtype), [HBM], name, [pltpu.SemaphoreType.DMA(())], out_specs=VMEM
    )(hbm(x))


def swap(x, axes):
    return lax.all_to_all(x, axes, split_axis=0, concat_axis=0, tiled=True)


def shards(query, new_kv, kv_store, prefix_pages, fork_of, own_pages, lengths, o_weight):
    shape = jax.ShapeDtypeStruct
    store = kv_store.reshape(P_DEV, 2, PAGE, HD)
    request = call(
        request_kernel,
        shape((POOL, HD), I32),
        [HBM] * 4,
        "request",
        [
            pltpu.SMEM(prefix_pages.shape, I32),
            pltpu.SMEM(own_pages.shape, I32),
            pltpu.SMEM(fork_of.shape, I32),
            pltpu.SMEM(lengths.shape, I32),
            pltpu.SemaphoreType.DMA((4,)),
        ],
    )(hbm(prefix_pages), hbm(own_pages), hbm(fork_of), hbm(lengths))
    request = swap(request, ("y", "z"))
    column = lax.axis_index("y").astype(I32).reshape(1)
    store = prefetch(store, "store_ahead")
    pages = call(
        gather_kernel,
        [pltpu.HBM((CHUNK, HD), BF16)] * YN,
        [SMEM, SMEM, VMEM, VMEM],
        "gather_pages",
        [pltpu.VMEM((CHUNK, HD), BF16)] * YN + [pltpu.SemaphoreType.DMA((YN,))],
        out_specs=[HBM] * YN,
    )(column, request, request, vmem(store))
    arrived = [pages[0]]
    for k in (2, 1, 3):
        arrived.append(lax.ppermute(pages[k], "y", [(y, (y + k) % YN) for y in range(YN)]))
    q = query.transpose(2, 0, 1, 3).reshape(ROWS, HD)
    queries = call(spread_kernel, shape((ZN, ROWS, HD), BF16), [VMEM], "spread")(q)
    queries, _ = lax.optimization_barrier((queries, pages[0]))
    queries = swap(queries, "z")
    fresh_k = new_kv[:, :, 0, 0].reshape(B * STEPS, HD)
    fresh_v = new_kv[:, :, 1, 0].reshape(B * STEPS, HD)
    local = call(
        local_kernel,
        [shape((ROWS, HD), F32)] * 3,
        [SMEM, SMEM, VMEM, VMEM, VMEM, VMEM],
        "resident",
        [pltpu.VMEM(((B - MIG) * NOWN * PAGE, HD), BF16)] * 2,
        pl.CostEstimate(flops=10**8, bytes_accessed=3 * 2**20, transcendentals=10**5),
    )(own_pages, lengths, q, fresh_k, fresh_v, store)
    parts = call(partial_kernel, shape((ZN, RES, HD), BF16), [HBM] + [VMEM] * 4, "partials", [
        pltpu.VMEM((CHUNK, HD), BF16), pltpu.SemaphoreType.DMA(())
    ])(hbm(arrived[0]), *[vmem(x) for x in arrived[1:]], queries)
    parts = swap(parts, "z")
    width = o_weight.shape[1] // TPN
    shares = call(finish_kernel, shape((TPN, 16, width), BF16), [VMEM] * 4 + [HBM], "finish", [
        pltpu.VMEM(o_weight.shape, BF16), pltpu.SemaphoreType.DMA(())
    ])(
        parts, *local, hbm(o_weight)
    )
    shares = swap(shares, ("x", "c"))
    return call(total_kernel, shape((B, STEPS, width), BF16), [VMEM], "total")(shares)


def solution(mesh):
    fine = Mesh(mesh.devices.reshape(ZN, YN, XN, CN), ("z", "y", "x", "c"))
    pool, tp = ("z", "y"), ("x", "c")
    return jax.shard_map(
        shards,
        mesh=fine,
        in_specs=(
            P(pool, None, tp, None),
            P(pool, None, None, tp, None),
            P(pool, None, tp, None, None),
            P(pool, None),
            P(pool),
            P(pool, None),
            P(pool),
            P(tp, None),
        ),
        out_specs=P(pool, None, tp),
        check_vma=False,
    )
```

```python
import math

import jax
import jax.numpy as jnp
from jax import lax
from jax.experimental import pallas as pl
from jax.experimental.pallas import tpu as pltpu
from jax.sharding import Mesh
from jax.sharding import PartitionSpec as P

F32 = jnp.float32
BF16 = jnp.bfloat16
I32 = jnp.int32

HD = 128
PAGE = 16
NPRE = 8
NOWN = 24
ROOTS = 4
B = 8
MIG = 4
STEPS = 2
GROUP = 4
ROWS = B * STEPS * GROUP
SLOTS = 4
P_DEV = 256
NEG = -(2.0**100)
SCALE = 1.0 / math.sqrt(HD)
ZN, YN, XN, CN = 16, 4, 4, 2
POOL = ZN * YN
TPN = XN * CN
PREFIX_IDS = ROOTS * NPRE
KEYS = SLOTS * PAGE
PAGE_ROWS = ZN * KEYS
CHUNK = 2 * PAGE_ROWS + ZN
RES = ROWS + 8

VMEM = pl.BlockSpec(memory_space=pltpu.VMEM)
SMEM = pl.BlockSpec(memory_space=pltpu.SMEM)
HBM = pl.BlockSpec(memory_space=pltpu.HBM)
ANY = pl.BlockSpec(memory_space=pl.ANY)
NT = (((1,), (1,)), ((), ()))
NN = (((1,), (0,)), ((), ()))


def iota(shape, dim):
    return lax.broadcasted_iota(I32, shape, dim)


def dot(a, b, dims=NN):
    return lax.dot_general(a, b, dims, preferred_element_type=F32)


def request_kernel(prefix_hbm, own_hbm, fork_hbm, length_hbm, req, prefix, own, fork, length, sems):
    pairs = ((prefix_hbm, prefix), (own_hbm, own), (fork_hbm, fork), (length_hbm, length))
    copies = [pltpu.make_async_copy(a, b, sems.at[n]) for n, (a, b) in enumerate(pairs)]
    for copy in copies:
        copy.start()
    for copy in copies:
        copy.wait()
    lane = iota((8, HD), 1)
    row = iota((8, HD), 0)
    ids = jnp.zeros((8, HD), I32)
    for r in range(ROOTS):
        for c in range(NPRE):
            ids = jnp.where(lane == r * NPRE + c, prefix[r, c], ids)
    for r in range(MIG):
        for c in range(NOWN):
            ids = jnp.where(lane == PREFIX_IDS + r * NOWN + c, own[r, c], ids)
    forks = jnp.zeros((8, HD), I32)
    lens = jnp.zeros((8, HD), I32)
    for b in range(B):
        forks = jnp.where(row == b, fork[b], forks)
        lens = jnp.where(row == b, length[b], lens)
    is_prefix = lane < PREFIX_IDS
    moved = jnp.maximum(lane - PREFIX_IDS, 0)
    chunk = jnp.where(is_prefix, lane % NPRE, NPRE + moved % NOWN)
    wanted = (is_prefix & (forks == lane // NPRE)) | (~is_prefix & (row == moved // NOWN))
    tokens = jnp.where(wanted, jnp.clip(lens - PAGE * chunk, 0, PAGE), 0)
    place = jnp.where(row == 0, ids % P_DEV, 0)
    table = jnp.concatenate([tokens, place], 0).astype(F32).astype(BF16)
    holder = ids // P_DEV
    holder = (holder % YN) * ZN + holder // YN
    member = jnp.broadcast_to(holder[0:1], (POOL, HD)) == iota((POOL, HD), 0)
    earlier = (iota((HD, HD), 0) < iota((HD, HD), 1)).astype(F32).astype(BF16)
    rank = dot(member.astype(F32).astype(BF16), earlier)
    out = jnp.zeros((POOL, HD), F32)
    for s in range(SLOTS):
        chosen = jnp.where(member & (rank == float(s)), 1.0, 0.0).astype(BF16)
        parts = [table if k == s else jnp.zeros((16, HD), BF16) for k in range(HD // 16)]
        out = out + dot(chosen, jnp.concatenate(parts, 0), NT)
    req[...] = out.astype(I32)


def prefetch_kernel(source, out, sem):
    copy = pltpu.make_async_copy(source, out, sem)
    copy.start()
    copy.wait()


def gather_kernel(column, places, req, store, *refs):
    outs, stages, sems = refs[:YN], refs[YN : 2 * YN], refs[2 * YN]
    copies = []
    for k, stage in enumerate(stages):
        base = ((column[0] + k) % YN) * ZN
        for z in range(ZN):
            for s in range(SLOTS):
                at = places[base + z, 16 * s + 8]
                start = z * KEYS + s * PAGE
                stage[pl.ds(start, PAGE), :] = store[at, 0]
                stage[pl.ds(PAGE_ROWS + start, PAGE), :] = store[at, 1]
        rows = req[pl.ds(pl.multiple_of(base, ZN), ZN), :]
        stage[pl.ds(2 * PAGE_ROWS, ZN), :] = rows.astype(F32).astype(BF16)
        copy = pltpu.make_async_copy(stage, outs[k], sems.at[k])
        copy.start()
        copies.append(copy)
    for copy in copies:
        copy.wait()


def local_kernel(own, length, q, fresh_k, fresh_v, store, sums, top, total, keys, values):
    branches = B - MIG
    span = NOWN * PAGE
    for b in range(branches):
        for p in range(NOWN):
            at = own[MIG + b, p] % P_DEV
            start = b * span + p * PAGE
            keys[pl.ds(start, PAGE), :] = store[at, 0]
            values[pl.ds(start, PAGE), :] = store[at, 1]
    rows = q[...]
    branch_of = (iota((ROWS, 1), 0) % 16) // STEPS
    step_of = iota((ROWS, 1), 0) % STEPS
    lane16 = iota((ROWS, 16), 1)
    score = dot(rows, fresh_k[...], NT) * SCALE
    ok = (lane16 // STEPS == branch_of) & (lane16 % STEPS <= step_of)
    blocks = [(jnp.where(ok, score, NEG), ok, fresh_v[...])]
    position = iota((ROWS, span), 1) + NPRE * PAGE
    for b in range(branches):
        score = dot(rows, keys[pl.ds(b * span, span), :], NT) * SCALE
        ok = (branch_of == MIG + b) & (position < length[MIG + b])
        blocks.append((jnp.where(ok, score, NEG), ok, values[pl.ds(b * span, span), :]))
    best = jnp.max(blocks[0][0], 1, keepdims=True)
    for score, _, _ in blocks[1:]:
        best = jnp.maximum(best, jnp.max(score, 1, keepdims=True))
    acc = jnp.zeros((ROWS, HD), F32)
    count = jnp.zeros((ROWS, 1), F32)
    for score, ok, value in blocks:
        weight = jnp.where(ok, jnp.exp(score - best), 0.0).astype(BF16)
        count = count + jnp.sum(weight.astype(F32), 1, keepdims=True)
        acc = acc + dot(weight, value)
    sums[...] = acc
    top[...] = jnp.broadcast_to(best, (ROWS, HD))
    total[...] = jnp.broadcast_to(count, (ROWS, HD))


def mask_kernel(c0, c1, c2, c3, out, tiles, sems):
    chunks = (c0, c1, c2, c3)
    copies = [
        pltpu.make_async_copy(c.at[pl.ds(2 * PAGE_ROWS, ZN), :], tiles.at[k], sems.at[k]) for k, c in enumerate(chunks)
    ]
    for copy in copies:
        copy.start()
    for copy in copies:
        copy.wait()
    pick = iota((16, HD), 1) % 16 == iota((16, HD), 0) // STEPS
    blocks = []
    for k in range(YN):
        tile = tiles[k].astype(F32)
        rows = [jnp.where(pick, jnp.broadcast_to(tile[z : z + 1], (16, HD)), 0.0).astype(BF16) for z in range(ZN)]
        blocks.append(jnp.concatenate(rows, 0))
    width = YN * KEYS
    shape = (YN * HD, width)
    source, key = iota(shape, 0), iota(shape, 1)
    expand = (source // HD == key // KEYS) & ((source % HD) // 16 == (key % KEYS) // PAGE)
    tokens = dot(jnp.concatenate(blocks, 1), expand.astype(F32).astype(BF16))
    number = (iota((ZN * 16, width), 1) % PAGE).astype(F32)
    out[...] = jnp.where(number < tokens, 0.0, NEG)


def partial_kernel(mask, c0, c1, c2, c3, queries, out, pages, sems):
    half = PAGE_ROWS // 2
    copies = []
    for part in range(2):
        for k, chunk in enumerate((c0, c1, c2, c3)):
            for kv in range(2):
                rows = pl.ds(kv * PAGE_ROWS + part * half, half)
                copy = pltpu.make_async_copy(chunk.at[rows, :], pages.at[k, rows, :], sems.at[part, k, kv])
                copy.start()
                copies.append(copy)
    column = iota((ROWS, HD), 1)
    stats = jnp.zeros((ROWS, HD), F32)
    sums = []
    for z in range(ZN):
        if z % (ZN // 2) == 0:
            first = (z // (ZN // 2)) * 2 * YN
            for copy in copies[first : first + 2 * YN]:
                copy.wait()
        bias = jnp.concatenate([mask[pl.ds(z * 16, 16), :]] * GROUP, 0)
        keys = jnp.concatenate([pages[k, pl.ds(z * KEYS, KEYS), :] for k in range(YN)], 0)
        values = jnp.concatenate([pages[k, pl.ds(PAGE_ROWS + z * KEYS, KEYS), :] for k in range(YN)], 0)
        score = jnp.where(bias < 0.0, NEG, dot(queries[z], keys, NT) * SCALE)
        best = jnp.max(score, 1, keepdims=True).astype(BF16).astype(F32)
        weight = jnp.where(bias < 0.0, 0.0, jnp.exp(score - best)).astype(BF16)
        count = jnp.sum(weight.astype(F32), 1, keepdims=True)
        sums.append(dot(weight, values))
        stats = jnp.where(column == z, best, jnp.where(column == ZN + z, count, stats))
    turned = jnp.transpose(stats)
    turned = jnp.concatenate([turned, jnp.zeros((HD, HD - ROWS), F32)], 1)
    tops = turned[0:ZN]
    counts = turned[ZN : 2 * ZN]
    high = counts.astype(BF16).astype(F32)
    low = counts - high
    row = iota((8, HD), 0)
    tiles = []
    for z in range(ZN):
        tile = jnp.where(row == 1, high[z : z + 1], jnp.where(row == 2, low[z : z + 1], 0.0))
        tiles.append(jnp.where(row == 0, tops[z : z + 1], tile))
    for z in range(0, ZN, 2):
        pair = jnp.concatenate([sums[z], tiles[z], sums[z + 1], tiles[z + 1]], 0)
        out[pl.ds(z * RES, 2 * RES), :] = pair.astype(BF16)


def finish_kernel(parts, sums, top, total, weight_hbm, out, weight, sem):
    copy = pltpu.make_async_copy(weight_hbm, weight, sem)
    copy.start()
    row = iota((ZN, HD), 0)
    tops = jnp.full((ZN, HD), NEG, F32)
    counts = jnp.zeros((ZN, HD), F32)
    received = []
    for z in range(0, ZN, 2):
        pair = parts[pl.ds(z * RES, 2 * RES), :].astype(F32)
        received += [pair[0:RES], pair[RES : 2 * RES]]
    for z in range(ZN):
        tile = received[z][ROWS:RES]
        tops = jnp.where(row == z, tile[0:1], tops)
        counts = jnp.where(row == z, tile[1:2] + tile[2:3], counts)
    tops = jnp.concatenate([tops, jnp.full((HD - ZN, HD), NEG, F32)], 0)
    counts = jnp.concatenate([counts, jnp.zeros((HD - ZN, HD), F32)], 0)
    tops = jnp.transpose(tops)[0:ROWS]
    counts = jnp.transpose(counts)[0:ROWS]
    own_top = top[...]
    best = jnp.maximum(jnp.max(tops, 1, keepdims=True), own_top)
    factor = jnp.exp(tops - best)
    own_factor = jnp.exp(own_top - best)
    denominator = jnp.sum(factor * counts, 1, keepdims=True) + own_factor * total[...]
    numerator = own_factor * sums[...]
    for z in range(ZN):
        numerator = numerator + factor[:, z : z + 1] * received[z][0:ROWS]
    attended = (numerator / denominator).astype(BF16)
    attended = jnp.concatenate([attended[16 * g : 16 * (g + 1)] for g in range(GROUP)], 1)
    copy.wait()
    result = dot(attended, weight[...]).astype(BF16).astype(F32)
    width = out.shape[2]
    for k in range(TPN):
        out[k] = result[:, k * width : (k + 1) * width].astype(BF16)


def total_kernel(shares, out):
    total = shares[0].astype(F32)
    for k in range(1, TPN):
        total = total + shares[k].astype(F32)
    total = total.astype(BF16).astype(F32)
    for b in range(B):
        out[b] = total[STEPS * b : STEPS * (b + 1)].astype(BF16)


def call(kernel, out_shape, in_specs, name, scratch=(), cost=None, mib=12, out_specs=None):
    return pl.pallas_call(
        kernel,
        out_shape=out_shape,
        in_specs=in_specs,
        out_specs=jax.tree.map(lambda _: VMEM, out_shape) if out_specs is None else out_specs,
        scratch_shapes=scratch,
        cost_estimate=cost,
        compiler_params=pltpu.CompilerParams(vmem_limit_bytes=mib * 2**20),
        name=name,
    )


def hbm(x):
    return pltpu.with_memory_space_constraint(x, pltpu.HBM)


def vmem(x):
    return pltpu.with_memory_space_constraint(x, pltpu.VMEM)


def prefetch(x, name):
    return call(
        prefetch_kernel, pltpu.VMEM(x.shape, x.dtype), [HBM], name, [pltpu.SemaphoreType.DMA(())], out_specs=VMEM
    )(hbm(x))


def swap(x, axes):
    return lax.all_to_all(x, axes, split_axis=0, concat_axis=0, tiled=True)


def shards(query, new_kv, kv_store, prefix_pages, fork_of, own_pages, lengths, o_weight):
    shape = jax.ShapeDtypeStruct
    store = kv_store.reshape(P_DEV, 2, PAGE, HD)
    request = call(
        request_kernel,
        shape((POOL, HD), I32),
        [HBM] * 4,
        "request",
        [
            pltpu.SMEM(prefix_pages.shape, I32),
            pltpu.SMEM(own_pages.shape, I32),
            pltpu.SMEM(fork_of.shape, I32),
            pltpu.SMEM(lengths.shape, I32),
            pltpu.SemaphoreType.DMA((4,)),
        ],
    )(hbm(prefix_pages), hbm(own_pages), hbm(fork_of), hbm(lengths))
    request = swap(request, ("y", "z"))
    column = lax.axis_index("y").astype(I32).reshape(1)
    store = prefetch(store, "store_ahead")
    pages = call(
        gather_kernel,
        [pltpu.HBM((CHUNK, HD), BF16)] * YN,
        [SMEM, SMEM, VMEM, VMEM],
        "gather_pages",
        [pltpu.VMEM((CHUNK, HD), BF16)] * YN + [pltpu.SemaphoreType.DMA((YN,))],
        out_specs=[HBM] * YN,
    )(column, request, request, vmem(store))
    arrived = [pages[0]]
    for k in (2, 1, 3):
        arrived.append(lax.ppermute(pages[k], "y", [(y, (y + k) % YN) for y in range(YN)]))
    q = query.transpose(2, 0, 1, 3).reshape(ROWS, HD)
    queries = lax.all_gather(q, "z")
    fresh_k = new_kv[:, :, 0, 0].reshape(B * STEPS, HD)
    fresh_v = new_kv[:, :, 1, 0].reshape(B * STEPS, HD)
    local = call(
        local_kernel,
        [shape((ROWS, HD), F32)] * 3,
        [SMEM, SMEM, VMEM, VMEM, VMEM, VMEM],
        "resident",
        [pltpu.VMEM(((B - MIG) * NOWN * PAGE, HD), BF16)] * 2,
        pl.CostEstimate(flops=10**8, bytes_accessed=3 * 2**20, transcendentals=10**5),
    )(own_pages, lengths, q, fresh_k, fresh_v, store)
    mask = call(
        mask_kernel,
        shape((ZN * 16, YN * KEYS), F32),
        [ANY] * YN,
        "token_masks",
        [pltpu.VMEM((YN, ZN, HD), BF16), pltpu.SemaphoreType.DMA((YN,))],
    )(*arrived)
    parts = call(
        partial_kernel,
        shape((ZN * RES, HD), BF16),
        [VMEM] + [ANY] * YN + [VMEM],
        "partials",
        [pltpu.VMEM((YN, CHUNK, HD), BF16), pltpu.SemaphoreType.DMA((2, YN, 2))],
    )(mask, *arrived, queries)
    parts = swap(parts.reshape(ZN, RES, HD), "z").reshape(ZN * RES, HD)
    width = o_weight.shape[1] // TPN
    shares = call(finish_kernel, shape((TPN, 16, width), BF16), [VMEM] * 4 + [HBM], "finish", [
        pltpu.VMEM(o_weight.shape, BF16), pltpu.SemaphoreType.DMA(())
    ])(
        parts, *local, hbm(o_weight)
    )
    shares = swap(shares, ("x", "c"))
    return call(total_kernel, shape((B, STEPS, width), BF16), [VMEM], "total")(shares)


def solution(mesh):
    fine = Mesh(mesh.devices.reshape(ZN, YN, XN, CN), ("z", "y", "x", "c"))
    pool, tp = ("z", "y"), ("x", "c")
    return jax.shard_map(
        shards,
        mesh=fine,
        in_specs=(
            P(pool, None, tp, None),
            P(pool, None, None, tp, None),
            P(pool, None, tp, None, None),
            P(pool, None),
            P(pool),
            P(pool, None),
            P(pool),
            P(tp, None),
        ),
        out_specs=P(pool, None, tp),
        check_vma=False,
    )
```

```python
import math

import jax
import jax.numpy as jnp
from jax import lax
from jax.experimental import pallas as pl
from jax.experimental.pallas import tpu as pltpu
from jax.sharding import Mesh
from jax.sharding import PartitionSpec as P

F32 = jnp.float32
BF16 = jnp.bfloat16
I32 = jnp.int32

HD = 128
PAGE = 16
NPRE = 8
NOWN = 24
ROOTS = 4
B = 8
MIG = 4
STEPS = 2
GROUP = 4
ROWS = B * STEPS * GROUP
SLOTS = 4
P_DEV = 256
NEG = -(2.0**100)
SCALE = 1.0 / math.sqrt(HD)
ZN, YN, XN, CN = 16, 4, 4, 2
ZL = 4
Z = ("zh", "zl")
POOL = ZN * YN
TPN = XN * CN
PREFIX_IDS = ROOTS * NPRE
KEYS = SLOTS * PAGE
PAGE_ROWS = ZN * KEYS
CHUNK = 2 * PAGE_ROWS + ZN
RES = ROWS + 8

VMEM = pl.BlockSpec(memory_space=pltpu.VMEM)
SMEM = pl.BlockSpec(memory_space=pltpu.SMEM)
HBM = pl.BlockSpec(memory_space=pltpu.HBM)
ANY = pl.BlockSpec(memory_space=pl.ANY)
NT = (((1,), (1,)), ((), ()))
NN = (((1,), (0,)), ((), ()))


def iota(shape, dim):
    return lax.broadcasted_iota(I32, shape, dim)


def dot(a, b, dims=NN):
    return lax.dot_general(a, b, dims, preferred_element_type=F32)


def request_kernel(prefix_hbm, own_hbm, fork_hbm, length_hbm, req, prefix, own, fork, length, sems):
    pairs = ((prefix_hbm, prefix), (own_hbm, own), (fork_hbm, fork), (length_hbm, length))
    copies = [pltpu.make_async_copy(a, b, sems.at[n]) for n, (a, b) in enumerate(pairs)]
    for copy in copies:
        copy.start()
    for copy in copies:
        copy.wait()
    lane = iota((8, HD), 1)
    row = iota((8, HD), 0)
    ids = jnp.zeros((8, HD), I32)
    for r in range(ROOTS):
        for c in range(NPRE):
            ids = jnp.where(lane == r * NPRE + c, prefix[r, c], ids)
    for r in range(MIG):
        for c in range(NOWN):
            ids = jnp.where(lane == PREFIX_IDS + r * NOWN + c, own[r, c], ids)
    forks = jnp.zeros((8, HD), I32)
    lens = jnp.zeros((8, HD), I32)
    for b in range(B):
        forks = jnp.where(row == b, fork[b], forks)
        lens = jnp.where(row == b, length[b], lens)
    is_prefix = lane < PREFIX_IDS
    moved = jnp.maximum(lane - PREFIX_IDS, 0)
    chunk = jnp.where(is_prefix, lane % NPRE, NPRE + moved % NOWN)
    wanted = (is_prefix & (forks == lane // NPRE)) | (~is_prefix & (row == moved // NOWN))
    tokens = jnp.where(wanted, jnp.clip(lens - PAGE * chunk, 0, PAGE), 0)
    place = jnp.where(row == 0, ids % P_DEV, 0)
    table = jnp.concatenate([tokens, place], 0).astype(F32).astype(BF16)
    holder = ids // P_DEV
    holder = (holder % YN) * ZN + holder // YN
    member = jnp.broadcast_to(holder[0:1], (POOL, HD)) == iota((POOL, HD), 0)
    earlier = (iota((HD, HD), 0) < iota((HD, HD), 1)).astype(F32).astype(BF16)
    rank = dot(member.astype(F32).astype(BF16), earlier)
    out = jnp.zeros((POOL, HD), F32)
    for s in range(SLOTS):
        chosen = jnp.where(member & (rank == float(s)), 1.0, 0.0).astype(BF16)
        parts = [table if k == s else jnp.zeros((16, HD), BF16) for k in range(HD // 16)]
        out = out + dot(chosen, jnp.concatenate(parts, 0), NT)
    req[...] = out.astype(I32)


def prefetch_kernel(source, out, sem):
    copy = pltpu.make_async_copy(source, out, sem)
    copy.start()
    copy.wait()


def gather_kernel(places, req, store, out, stage, sems):
    copies = []
    for y in range(YN):
        for z in range(ZN):
            for s in range(SLOTS):
                at = places[y * ZN + z, 16 * s + 8]
                start = z * KEYS + s * PAGE
                stage[y, pl.ds(start, PAGE), :] = store[at, 0]
                stage[y, pl.ds(PAGE_ROWS + start, PAGE), :] = store[at, 1]
        stage[y, pl.ds(2 * PAGE_ROWS, ZN), :] = req[pl.ds(y * ZN, ZN), :].astype(F32).astype(BF16)
        copy = pltpu.make_async_copy(stage.at[y], out.at[y], sems.at[y])
        copy.start()
        copies.append(copy)
    for copy in copies:
        copy.wait()


def local_kernel(own, length, q, fresh_k, fresh_v, store, sums, top, total, keys, values):
    branches = B - MIG
    span = NOWN * PAGE
    for b in range(branches):
        for p in range(NOWN):
            at = own[MIG + b, p] % P_DEV
            start = b * span + p * PAGE
            keys[pl.ds(start, PAGE), :] = store[at, 0]
            values[pl.ds(start, PAGE), :] = store[at, 1]
    rows = q[...]
    branch_of = (iota((ROWS, 1), 0) % 16) // STEPS
    step_of = iota((ROWS, 1), 0) % STEPS
    lane16 = iota((ROWS, 16), 1)
    score = dot(rows, fresh_k[...], NT) * SCALE
    ok = (lane16 // STEPS == branch_of) & (lane16 % STEPS <= step_of)
    blocks = [(jnp.where(ok, score, NEG), ok, fresh_v[...])]
    position = iota((ROWS, span), 1) + NPRE * PAGE
    for b in range(branches):
        score = dot(rows, keys[pl.ds(b * span, span), :], NT) * SCALE
        ok = (branch_of == MIG + b) & (position < length[MIG + b])
        blocks.append((jnp.where(ok, score, NEG), ok, values[pl.ds(b * span, span), :]))
    best = jnp.max(blocks[0][0], 1, keepdims=True)
    for score, _, _ in blocks[1:]:
        best = jnp.maximum(best, jnp.max(score, 1, keepdims=True))
    acc = jnp.zeros((ROWS, HD), F32)
    count = jnp.zeros((ROWS, 1), F32)
    for score, ok, value in blocks:
        weight = jnp.where(ok, jnp.exp(score - best), 0.0).astype(BF16)
        count = count + jnp.sum(weight.astype(F32), 1, keepdims=True)
        acc = acc + dot(weight, value)
    sums[...] = acc
    top[...] = jnp.broadcast_to(best, (ROWS, HD))
    total[...] = jnp.broadcast_to(count, (ROWS, HD))


def partial_kernel(pages, queries, out):
    pick = iota((16, HD), 1) % 16 == iota((16, HD), 0) // STEPS
    blocks = []
    for k in range(YN):
        tile = pages[k, pl.ds(2 * PAGE_ROWS, ZN), :].astype(F32)
        rows = [jnp.where(pick, jnp.broadcast_to(tile[z : z + 1], (16, HD)), 0.0).astype(BF16) for z in range(ZN)]
        blocks.append(jnp.concatenate(rows, 0))
    width = YN * KEYS
    shape = (YN * HD, width)
    source, key = iota(shape, 0), iota(shape, 1)
    expand = (source // HD == key // KEYS) & ((source % HD) // 16 == (key % KEYS) // PAGE)
    tokens = dot(jnp.concatenate(blocks, 1), expand.astype(F32).astype(BF16))
    number = (iota((ZN * 16, width), 1) % PAGE).astype(F32)
    mask = jnp.where(number < tokens, 0.0, NEG)
    column = iota((ROWS, HD), 1)
    stats = jnp.zeros((ROWS, HD), F32)
    sums = []
    for z in range(ZN):
        bias = jnp.concatenate([mask[z * 16 : (z + 1) * 16]] * GROUP, 0)
        keys = jnp.concatenate([pages[k, pl.ds(z * KEYS, KEYS), :] for k in range(YN)], 0)
        values = jnp.concatenate([pages[k, pl.ds(PAGE_ROWS + z * KEYS, KEYS), :] for k in range(YN)], 0)
        score = jnp.where(bias < 0.0, NEG, dot(queries[z], keys, NT) * SCALE)
        best = jnp.max(score, 1, keepdims=True).astype(BF16).astype(F32)
        weight = jnp.where(bias < 0.0, 0.0, jnp.exp(score - best)).astype(BF16)
        count = jnp.sum(weight.astype(F32), 1, keepdims=True)
        sums.append(dot(weight, values))
        stats = jnp.where(column == z, best, jnp.where(column == ZN + z, count, stats))
    turned = jnp.transpose(stats)
    turned = jnp.concatenate([turned, jnp.zeros((HD, HD - ROWS), F32)], 1)
    tops = turned[0:ZN]
    counts = turned[ZN : 2 * ZN]
    high = counts.astype(BF16).astype(F32)
    low = counts - high
    row = iota((8, HD), 0)
    tiles = []
    for z in range(ZN):
        tile = jnp.where(row == 1, high[z : z + 1], jnp.where(row == 2, low[z : z + 1], 0.0))
        tiles.append(jnp.where(row == 0, tops[z : z + 1], tile))
    for z in range(0, ZN, 2):
        pair = jnp.concatenate([sums[z], tiles[z], sums[z + 1], tiles[z + 1]], 0)
        out[pl.ds(z * RES, 2 * RES), :] = pair.astype(BF16)


def finish_kernel(parts, sums, top, total, weight_hbm, out, weight, sem):
    copy = pltpu.make_async_copy(weight_hbm, weight, sem)
    copy.start()
    row = iota((ZN, HD), 0)
    tops = jnp.full((ZN, HD), NEG, F32)
    counts = jnp.zeros((ZN, HD), F32)
    received = []
    for z in range(0, ZN, 2):
        pair = parts[pl.ds(z * RES, 2 * RES), :].astype(F32)
        received += [pair[0:RES], pair[RES : 2 * RES]]
    for z in range(ZN):
        tile = received[z][ROWS:RES]
        tops = jnp.where(row == z, tile[0:1], tops)
        counts = jnp.where(row == z, tile[1:2] + tile[2:3], counts)
    tops = jnp.concatenate([tops, jnp.full((HD - ZN, HD), NEG, F32)], 0)
    counts = jnp.concatenate([counts, jnp.zeros((HD - ZN, HD), F32)], 0)
    tops = jnp.transpose(tops)[0:ROWS]
    counts = jnp.transpose(counts)[0:ROWS]
    own_top = top[...]
    best = jnp.maximum(jnp.max(tops, 1, keepdims=True), own_top)
    factor = jnp.exp(tops - best)
    own_factor = jnp.exp(own_top - best)
    denominator = jnp.sum(factor * counts, 1, keepdims=True) + own_factor * total[...]
    numerator = own_factor * sums[...]
    for z in range(ZN):
        numerator = numerator + factor[:, z : z + 1] * received[z][0:ROWS]
    attended = (numerator / denominator).astype(BF16)
    attended = jnp.concatenate([attended[16 * g : 16 * (g + 1)] for g in range(GROUP)], 1)
    copy.wait()
    result = dot(attended, weight[...]).astype(BF16).astype(F32)
    width = out.shape[2]
    for k in range(TPN):
        out[k] = result[:, k * width : (k + 1) * width].astype(BF16)


def total_kernel(shares, out):
    total = shares[0].astype(F32)
    for k in range(1, TPN):
        total = total + shares[k].astype(F32)
    total = total.astype(BF16).astype(F32)
    for b in range(B):
        out[b] = total[STEPS * b : STEPS * (b + 1)].astype(BF16)


def call(kernel, out_shape, in_specs, name, scratch=(), cost=None, mib=12, out_specs=None):
    return pl.pallas_call(
        kernel,
        out_shape=out_shape,
        in_specs=in_specs,
        out_specs=jax.tree.map(lambda _: VMEM, out_shape) if out_specs is None else out_specs,
        scratch_shapes=scratch,
        cost_estimate=cost,
        compiler_params=pltpu.CompilerParams(vmem_limit_bytes=mib * 2**20),
        name=name,
    )


def hbm(x):
    return pltpu.with_memory_space_constraint(x, pltpu.HBM)


def vmem(x):
    return pltpu.with_memory_space_constraint(x, pltpu.VMEM)


def prefetch(x, name):
    return call(
        prefetch_kernel, pltpu.VMEM(x.shape, x.dtype), [HBM], name, [pltpu.SemaphoreType.DMA(())], out_specs=VMEM
    )(hbm(x))


def swap(x, axes):
    return lax.all_to_all(x, axes, split_axis=0, concat_axis=0, tiled=True)


def shards(query, new_kv, kv_store, prefix_pages, fork_of, own_pages, lengths, o_weight):
    shape = jax.ShapeDtypeStruct
    store = kv_store.reshape(P_DEV, 2, PAGE, HD)
    request = call(
        request_kernel,
        shape((POOL, HD), I32),
        [HBM] * 4,
        "request",
        [
            pltpu.SMEM(prefix_pages.shape, I32),
            pltpu.SMEM(own_pages.shape, I32),
            pltpu.SMEM(fork_of.shape, I32),
            pltpu.SMEM(lengths.shape, I32),
            pltpu.SemaphoreType.DMA((4,)),
        ],
    )(hbm(prefix_pages), hbm(own_pages), hbm(fork_of), hbm(lengths))
    request = swap(request, ("y", *Z))
    q = query.transpose(2, 0, 1, 3).reshape(ROWS, HD)
    near = lax.all_gather(q, "zl")
    request, near = lax.optimization_barrier((request, near))
    store = prefetch(store, "store_ahead")
    pages = call(
        gather_kernel,
        pltpu.HBM((YN, CHUNK, HD), BF16),
        [SMEM, VMEM, VMEM],
        "gather_pages",
        [pltpu.VMEM((YN, CHUNK, HD), BF16), pltpu.SemaphoreType.DMA((YN,))],
        out_specs=HBM,
    )(request, request, vmem(store))
    near, pages = lax.optimization_barrier((near, pages))
    pages = swap(pages, "y")
    queries = lax.all_gather(near, "zh").reshape(ZN, ROWS, HD)
    fresh_k = new_kv[:, :, 0, 0].reshape(B * STEPS, HD)
    fresh_v = new_kv[:, :, 1, 0].reshape(B * STEPS, HD)
    local = call(
        local_kernel,
        [shape((ROWS, HD), F32)] * 3,
        [SMEM, SMEM, VMEM, VMEM, VMEM, VMEM],
        "resident",
        [pltpu.VMEM(((B - MIG) * NOWN * PAGE, HD), BF16)] * 2,
        pl.CostEstimate(flops=10**8, bytes_accessed=3 * 2**20, transcendentals=10**5),
    )(own_pages, lengths, q, fresh_k, fresh_v, store)
    parts = call(partial_kernel, shape((ZN * RES, HD), BF16), [VMEM] * 2, "partials")(pages, queries)
    parts = swap(parts.reshape(ZN, RES, HD), Z).reshape(ZN * RES, HD)
    width = o_weight.shape[1] // TPN
    shares = call(finish_kernel, shape((TPN, 16, width), BF16), [VMEM] * 4 + [HBM], "finish", [
        pltpu.VMEM(o_weight.shape, BF16), pltpu.SemaphoreType.DMA(())
    ])(
        parts, *local, hbm(o_weight)
    )
    shares = swap(shares, ("x", "c"))
    return call(total_kernel, shape((B, STEPS, width), BF16), [VMEM], "total")(shares)


def solution(mesh):
    fine = Mesh(mesh.devices.reshape(ZN // ZL, ZL, YN, XN, CN), ("zh", "zl", "y", "x", "c"))
    pool, tp = ("zh", "zl", "y"), ("x", "c")
    return jax.shard_map(
        shards,
        mesh=fine,
        in_specs=(
            P(pool, None, tp, None),
            P(pool, None, None, tp, None),
            P(pool, None, tp, None, None),
            P(pool, None),
            P(pool),
            P(pool, None),
            P(pool),
            P(tp, None),
        ),
        out_specs=P(pool, None, tp),
        check_vma=False,
    )
```

```python
import math

import jax
import jax.numpy as jnp
from jax import lax
from jax.experimental import pallas as pl
from jax.experimental.pallas import tpu as pltpu
from jax.sharding import Mesh
from jax.sharding import PartitionSpec as P

F32 = jnp.float32
BF16 = jnp.bfloat16
I32 = jnp.int32

HD = 128
PAGE = 16
NPRE = 8
NOWN = 24
ROOTS = 4
B = 8
MIG = 4
STEPS = 2
GROUP = 4
ROWS = B * STEPS * GROUP
SLOTS = 4
P_DEV = 256
NEG = -(2.0**100)
SCALE = 1.0 / math.sqrt(HD)
ZN, YN, XN, CN = 16, 4, 4, 2
ZL = 4
PARTS = 2
AHEAD = 2
Z = ("zh", "zl")
POOL = ZN * YN
TPN = XN * CN
PREFIX_IDS = ROOTS * NPRE
KEYS = SLOTS * PAGE
PAGE_ROWS = ZN * KEYS
CHUNK = 2 * PAGE_ROWS + ZN
RES = ROWS + 8

VMEM = pl.BlockSpec(memory_space=pltpu.VMEM)
SMEM = pl.BlockSpec(memory_space=pltpu.SMEM)
HBM = pl.BlockSpec(memory_space=pltpu.HBM)
ANY = pl.BlockSpec(memory_space=pl.ANY)
NT = (((1,), (1,)), ((), ()))
NN = (((1,), (0,)), ((), ()))


def iota(shape, dim):
    return lax.broadcasted_iota(I32, shape, dim)


def dot(a, b, dims=NN):
    return lax.dot_general(a, b, dims, preferred_element_type=F32)


def request_kernel(prefix_hbm, own_hbm, fork_hbm, length_hbm, req, prefix, own, fork, length, sems):
    pairs = ((prefix_hbm, prefix), (own_hbm, own), (fork_hbm, fork), (length_hbm, length))
    copies = [pltpu.make_async_copy(a, b, sems.at[n]) for n, (a, b) in enumerate(pairs)]
    for copy in copies:
        copy.start()
    for copy in copies:
        copy.wait()
    lane = iota((8, HD), 1)
    row = iota((8, HD), 0)
    ids = jnp.zeros((8, HD), I32)
    for r in range(ROOTS):
        for c in range(NPRE):
            ids = jnp.where(lane == r * NPRE + c, prefix[r, c], ids)
    for r in range(MIG):
        for c in range(NOWN):
            ids = jnp.where(lane == PREFIX_IDS + r * NOWN + c, own[r, c], ids)
    forks = jnp.zeros((8, HD), I32)
    lens = jnp.zeros((8, HD), I32)
    for b in range(B):
        forks = jnp.where(row == b, fork[b], forks)
        lens = jnp.where(row == b, length[b], lens)
    is_prefix = lane < PREFIX_IDS
    moved = jnp.maximum(lane - PREFIX_IDS, 0)
    chunk = jnp.where(is_prefix, lane % NPRE, NPRE + moved % NOWN)
    wanted = (is_prefix & (forks == lane // NPRE)) | (~is_prefix & (row == moved // NOWN))
    tokens = jnp.where(wanted, jnp.clip(lens - PAGE * chunk, 0, PAGE), 0)
    place = jnp.where(row == 0, ids % P_DEV, 0)
    table = jnp.concatenate([tokens, place], 0).astype(F32).astype(BF16)
    holder = ids // P_DEV
    holder = (holder % YN) * ZN + holder // YN
    member = jnp.broadcast_to(holder[0:1], (POOL, HD)) == iota((POOL, HD), 0)
    earlier = (iota((HD, HD), 0) < iota((HD, HD), 1)).astype(F32).astype(BF16)
    rank = dot(member.astype(F32).astype(BF16), earlier)
    out = jnp.zeros((POOL, HD), F32)
    for s in range(SLOTS):
        chosen = jnp.where(member & (rank == float(s)), 1.0, 0.0).astype(BF16)
        parts = [table if k == s else jnp.zeros((16, HD), BF16) for k in range(HD // 16)]
        out = out + dot(chosen, jnp.concatenate(parts, 0), NT)
    req[...] = out.astype(I32)


def order_kernel(place, own, far, left, right, out):
    for k, ref in ((0, own), (2, far), (1, left), (3, right)):
        out[(place[0] + ZL - k) % ZL] = ref[...]


def prefetch_kernel(source, out, sems):
    part = out.shape[0] // sems.shape[0]
    copies = [
        pltpu.make_async_copy(source.at[pl.ds(n * part, part)], out.at[pl.ds(n * part, part)], sems.at[n])
        for n in range(sems.shape[0])
    ]
    for copy in copies:
        copy.start()
    for copy in copies:
        copy.wait()


def gather_kernel(places, req, store, out, stage, sems):
    copies = []
    for y in range(YN):
        for z in range(ZN):
            for s in range(SLOTS):
                at = places[y * ZN + z, 16 * s + 8]
                start = z * KEYS + s * PAGE
                stage[y, pl.ds(start, PAGE), :] = store[at, 0]
                stage[y, pl.ds(PAGE_ROWS + start, PAGE), :] = store[at, 1]
        stage[y, pl.ds(2 * PAGE_ROWS, ZN), :] = req[pl.ds(y * ZN, ZN), :].astype(F32).astype(BF16)
        copy = pltpu.make_async_copy(stage.at[y], out.at[y], sems.at[y])
        copy.start()
        copies.append(copy)
    for copy in copies:
        copy.wait()


def local_kernel(own, length, q, fresh_k, fresh_v, store, sums, top, total, keys, values):
    branches = B - MIG
    span = NOWN * PAGE
    for b in range(branches):
        for p in range(NOWN):
            at = own[MIG + b, p] % P_DEV
            start = b * span + p * PAGE
            keys[pl.ds(start, PAGE), :] = store[at, 0]
            values[pl.ds(start, PAGE), :] = store[at, 1]
    rows = q[...]
    branch_of = (iota((ROWS, 1), 0) % 16) // STEPS
    step_of = iota((ROWS, 1), 0) % STEPS
    lane16 = iota((ROWS, 16), 1)
    score = dot(rows, fresh_k[...], NT) * SCALE
    ok = (lane16 // STEPS == branch_of) & (lane16 % STEPS <= step_of)
    blocks = [(jnp.where(ok, score, NEG), ok, fresh_v[...])]
    position = iota((ROWS, span), 1) + NPRE * PAGE
    for b in range(branches):
        score = dot(rows, keys[pl.ds(b * span, span), :], NT) * SCALE
        ok = (branch_of == MIG + b) & (position < length[MIG + b])
        blocks.append((jnp.where(ok, score, NEG), ok, values[pl.ds(b * span, span), :]))
    best = jnp.max(blocks[0][0], 1, keepdims=True)
    for score, _, _ in blocks[1:]:
        best = jnp.maximum(best, jnp.max(score, 1, keepdims=True))
    acc = jnp.zeros((ROWS, HD), F32)
    count = jnp.zeros((ROWS, 1), F32)
    for score, ok, value in blocks:
        weight = jnp.where(ok, jnp.exp(score - best), 0.0).astype(BF16)
        count = count + jnp.sum(weight.astype(F32), 1, keepdims=True)
        acc = acc + dot(weight, value)
    sums[...] = acc
    top[...] = jnp.broadcast_to(best, (ROWS, HD))
    total[...] = jnp.broadcast_to(count, (ROWS, HD))


def partial_kernel(source, queries, out, pages, meta, meta_sem, sems):
    size = PAGE_ROWS // PARTS
    per = ZN // PARTS
    meta_copy = pltpu.make_async_copy(source.at[:, pl.ds(2 * PAGE_ROWS, ZN), :], meta, meta_sem)
    meta_copy.start()
    copies = []
    for part in range(PARTS):
        group = []
        for kv in range(2):
            rows = pl.ds(kv * PAGE_ROWS + part * size, size)
            copy = pltpu.make_async_copy(source.at[:, rows, :], pages.at[:, rows, :], sems.at[part, kv])
            copy.start()
            group.append(copy)
        copies.append(group)
    meta_copy.wait()
    pick = iota((16, HD), 1) % 16 == iota((16, HD), 0) // STEPS
    blocks = []
    for k in range(YN):
        tile = meta[k].astype(F32)
        rows = [jnp.where(pick, jnp.broadcast_to(tile[z : z + 1], (16, HD)), 0.0).astype(BF16) for z in range(ZN)]
        blocks.append(jnp.concatenate(rows, 0))
    width = YN * KEYS
    shape = (YN * HD, width)
    origin, key = iota(shape, 0), iota(shape, 1)
    expand = (origin // HD == key // KEYS) & ((origin % HD) // 16 == (key % KEYS) // PAGE)
    tokens = dot(jnp.concatenate(blocks, 1), expand.astype(F32).astype(BF16))
    number = (iota((ZN * 16, width), 1) % PAGE).astype(F32)
    mask = jnp.where(number < tokens, 0.0, NEG)
    column = iota((ROWS, HD), 1)
    row = iota((8, HD), 0)
    for part in range(PARTS):
        members = range(part * per, (part + 1) * per)
        for copy in copies[part]:
            copy.wait()
        scores = []
        for z in members:
            keys = jnp.concatenate([pages[k, pl.ds(z * KEYS, KEYS), :] for k in range(YN)], 0)
            scores.append(dot(queries[z], keys, NT))
        stats = jnp.zeros((ROWS, HD), F32)
        weights = []
        for n, z in enumerate(members):
            bias = jnp.concatenate([mask[z * 16 : (z + 1) * 16]] * GROUP, 0)
            score = jnp.where(bias < 0.0, NEG, scores[n] * SCALE)
            best = jnp.max(score, 1, keepdims=True).astype(BF16).astype(F32)
            weight = jnp.where(bias < 0.0, 0.0, jnp.exp(score - best)).astype(BF16)
            count = jnp.sum(weight.astype(F32), 1, keepdims=True)
            weights.append(weight)
            stats = jnp.where(column == n, best, jnp.where(column == 8 + n, count, stats))
        turned = jnp.transpose(stats)[0:16]
        turned = jnp.concatenate([turned, jnp.zeros((16, HD - ROWS), F32)], 1)
        tops, counts = turned[0:8], turned[8:16]
        high = counts.astype(BF16).astype(F32)
        low = counts - high
        rows = []
        for n, z in enumerate(members):
            values = jnp.concatenate([pages[k, pl.ds(PAGE_ROWS + z * KEYS, KEYS), :] for k in range(YN)], 0)
            tile = jnp.where(row == 1, high[n : n + 1], jnp.where(row == 2, low[n : n + 1], 0.0))
            rows += [dot(weights[n], values), jnp.where(row == 0, tops[n : n + 1], tile)]
        out[pl.ds(part * per * RES, per * RES), :] = jnp.concatenate(rows, 0).astype(BF16)


def finish_kernel(parts, sums, top, total, early, weight_hbm, out, late, sems):
    ahead = early.shape[0] // HD
    copies = [
        pltpu.make_async_copy(
            weight_hbm.at[pl.ds((ahead + n) * HD, HD), :], late.at[pl.ds(n * HD, HD), :], sems.at[n]
        )
        for n in range(GROUP - ahead)
    ]
    for copy in copies:
        copy.start()
    row = iota((ZN, HD), 0)
    tops = jnp.full((ZN, HD), NEG, F32)
    counts = jnp.zeros((ZN, HD), F32)
    received = []
    for z in range(0, ZN, 2):
        pair = parts[pl.ds(z * RES, 2 * RES), :].astype(F32)
        received += [pair[0:RES], pair[RES : 2 * RES]]
    for z in range(ZN):
        tile = received[z][ROWS:RES]
        tops = jnp.where(row == z, tile[0:1], tops)
        counts = jnp.where(row == z, tile[1:2] + tile[2:3], counts)
    tops = jnp.concatenate([tops, jnp.full((HD - ZN, HD), NEG, F32)], 0)
    counts = jnp.concatenate([counts, jnp.zeros((HD - ZN, HD), F32)], 0)
    tops = jnp.transpose(tops)[0:ROWS]
    counts = jnp.transpose(counts)[0:ROWS]
    own_top = top[...]
    best = jnp.maximum(jnp.max(tops, 1, keepdims=True), own_top)
    factor = jnp.exp(tops - best)
    own_factor = jnp.exp(own_top - best)
    denominator = jnp.sum(factor * counts, 1, keepdims=True) + own_factor * total[...]
    numerator = own_factor * sums[...]
    for z in range(ZN):
        numerator = numerator + factor[:, z : z + 1] * received[z][0:ROWS]
    attended = (numerator / denominator).astype(BF16)
    result = jnp.zeros((16, late.shape[1]), F32)
    for g in range(GROUP):
        if g < ahead:
            rows = early[pl.ds(g * HD, HD), :]
        else:
            copies[g - ahead].wait()
            rows = late[pl.ds((g - ahead) * HD, HD), :]
        result = result + dot(attended[16 * g : 16 * (g + 1)], rows)
    result = result.astype(BF16).astype(F32)
    width = out.shape[2]
    for k in range(TPN):
        out[k] = result[:, k * width : (k + 1) * width].astype(BF16)


def total_kernel(shares, out):
    total = shares[0].astype(F32)
    for k in range(1, TPN):
        total = total + shares[k].astype(F32)
    total = total.astype(BF16).astype(F32)
    for b in range(B):
        out[b] = total[STEPS * b : STEPS * (b + 1)].astype(BF16)


def call(kernel, out_shape, in_specs, name, scratch=(), cost=None, mib=12, out_specs=None):
    return pl.pallas_call(
        kernel,
        out_shape=out_shape,
        in_specs=in_specs,
        out_specs=jax.tree.map(lambda _: VMEM, out_shape) if out_specs is None else out_specs,
        scratch_shapes=scratch,
        cost_estimate=cost,
        compiler_params=pltpu.CompilerParams(vmem_limit_bytes=mib * 2**20),
        name=name,
    )


def hbm(x):
    return pltpu.with_memory_space_constraint(x, pltpu.HBM)


def vmem(x):
    return pltpu.with_memory_space_constraint(x, pltpu.VMEM)


def prefetch(x, name, rows=None):
    return call(
        prefetch_kernel,
        pltpu.VMEM((rows or x.shape[0], *x.shape[1:]), x.dtype),
        [HBM],
        name,
        [pltpu.SemaphoreType.DMA((8,))],
        out_specs=VMEM,
    )(hbm(x))


PARTIAL_SCRATCH = [
    pltpu.VMEM((YN, CHUNK, HD), BF16),
    pltpu.VMEM((YN, ZN, HD), BF16),
    pltpu.SemaphoreType.DMA(()),
    pltpu.SemaphoreType.DMA((PARTS, 2)),
]


def swap(x, axes):
    return lax.all_to_all(x, axes, split_axis=0, concat_axis=0, tiled=True)


def shards(query, new_kv, kv_store, prefix_pages, fork_of, own_pages, lengths, o_weight):
    shape = jax.ShapeDtypeStruct
    store = kv_store.reshape(P_DEV, 2, PAGE, HD)
    request = call(
        request_kernel,
        shape((POOL, HD), I32),
        [HBM] * 4,
        "request",
        [
            pltpu.SMEM(prefix_pages.shape, I32),
            pltpu.SMEM(own_pages.shape, I32),
            pltpu.SMEM(fork_of.shape, I32),
            pltpu.SMEM(lengths.shape, I32),
            pltpu.SemaphoreType.DMA((4,)),
        ],
    )(hbm(prefix_pages), hbm(own_pages), hbm(fork_of), hbm(lengths))
    request = swap(request, ("y", *Z))
    q = query.transpose(2, 0, 1, 3).reshape(ROWS, HD)
    shifted = [lax.ppermute(q, "zl", [(z, (z + k) % ZL) for z in range(ZL)]) for k in (2, 1, 3)]
    place = lax.axis_index("zl").astype(I32).reshape(1)
    near = call(order_kernel, shape((ZL, ROWS, HD), BF16), [SMEM] + [VMEM] * ZL, "order")(place, q, *shifted)
    request, near = lax.optimization_barrier((request, near))
    store = prefetch(store, "store_ahead")
    pages = call(
        gather_kernel,
        pltpu.HBM((YN, CHUNK, HD), BF16),
        [SMEM, VMEM, VMEM],
        "gather_pages",
        [pltpu.VMEM((YN, CHUNK, HD), BF16), pltpu.SemaphoreType.DMA((YN,))],
        out_specs=HBM,
    )(request, request, vmem(store))
    near, pages = lax.optimization_barrier((near, pages))
    pages = swap(pages, "y")
    queries = lax.all_gather(near, "zh").reshape(ZN, ROWS, HD)
    fresh_k = new_kv[:, :, 0, 0].reshape(B * STEPS, HD)
    fresh_v = new_kv[:, :, 1, 0].reshape(B * STEPS, HD)
    local = call(
        local_kernel,
        [shape((ROWS, HD), F32)] * 3,
        [SMEM, SMEM, VMEM, VMEM, VMEM, VMEM],
        "resident",
        [pltpu.VMEM(((B - MIG) * NOWN * PAGE, HD), BF16)] * 2,
        pl.CostEstimate(flops=10**8, bytes_accessed=3 * 2**20, transcendentals=10**5),
    )(own_pages, lengths, q, fresh_k, fresh_v, store)
    parts = call(partial_kernel, shape((ZN * RES, HD), BF16), [HBM, VMEM], "partials", PARTIAL_SCRATCH)(pages, queries)
    parts = swap(parts.reshape(ZN, RES, HD), Z).reshape(ZN * RES, HD)
    width = o_weight.shape[1] // TPN
    early = prefetch(o_weight, "weight_ahead", AHEAD * HD)
    rest = (GROUP - AHEAD) * HD
    shares = call(
        finish_kernel,
        shape((TPN, 16, width), BF16),
        [VMEM] * 5 + [HBM],
        "finish",
        [pltpu.VMEM((rest, o_weight.shape[1]), BF16), pltpu.SemaphoreType.DMA((GROUP - AHEAD,))],
    )(parts, *local, vmem(early), hbm(o_weight))
    shares = swap(shares, ("x", "c"))
    return call(total_kernel, shape((B, STEPS, width), BF16), [VMEM], "total")(shares)


def solution(mesh):
    fine = Mesh(mesh.devices.reshape(ZN // ZL, ZL, YN, XN, CN), ("zh", "zl", "y", "x", "c"))
    pool, tp = ("zh", "zl", "y"), ("x", "c")
    return jax.shard_map(
        shards,
        mesh=fine,
        in_specs=(
            P(pool, None, tp, None),
            P(pool, None, None, tp, None),
            P(pool, None, tp, None, None),
            P(pool, None),
            P(pool),
            P(pool, None),
            P(pool),
            P(tp, None),
        ),
        out_specs=P(pool, None, tp),
        check_vma=False,
    )
```

```python
import math

import jax
import jax.numpy as jnp
from jax import lax
from jax.experimental import pallas as pl
from jax.experimental.pallas import tpu as pltpu
from jax.sharding import Mesh
from jax.sharding import PartitionSpec as P

F32 = jnp.float32
BF16 = jnp.bfloat16
I32 = jnp.int32

HD = 128
PAGE = 16
NPRE = 8
NOWN = 24
ROOTS = 4
B = 8
MIG = 4
STEPS = 2
GROUP = 4
ROWS = B * STEPS * GROUP
SLOTS = 4
P_DEV = 256
NEG = -(2.0**100)
SCALE = 1.0 / math.sqrt(HD)
ZN, YN, XN, CN = 16, 4, 4, 2
ZH, ZM, ZL = 4, 2, 2
PARTS = 2
POOL_AXES = ("zh", "zm", "zl", "y")
NEAR = ("zl", "y")
FAR = ("zh", "zm")
SOURCES = ZL * YN
MEMBERS = ZH * ZM
POOL = ZN * YN
TPN = XN * CN
PREFIX_IDS = ROOTS * NPRE
KEYS = SLOTS * PAGE
PAGE_ROWS = MEMBERS * KEYS
CHUNK = 2 * PAGE_ROWS + 16
RES = ROWS + 8

VMEM = pl.BlockSpec(memory_space=pltpu.VMEM)
SMEM = pl.BlockSpec(memory_space=pltpu.SMEM)
HBM = pl.BlockSpec(memory_space=pltpu.HBM)
ANY = pl.BlockSpec(memory_space=pl.ANY)
NT = (((1,), (1,)), ((), ()))
NN = (((1,), (0,)), ((), ()))


def iota(shape, dim):
    return lax.broadcasted_iota(I32, shape, dim)


def dot(a, b, dims=NN):
    return lax.dot_general(a, b, dims, preferred_element_type=F32)


def request_kernel(prefix_hbm, own_hbm, fork_hbm, length_hbm, req, prefix, own, fork, length, sems):
    pairs = ((prefix_hbm, prefix), (own_hbm, own), (fork_hbm, fork), (length_hbm, length))
    copies = [pltpu.make_async_copy(a, b, sems.at[n]) for n, (a, b) in enumerate(pairs)]
    for copy in copies:
        copy.start()
    for copy in copies:
        copy.wait()
    lane = iota((8, HD), 1)
    row = iota((8, HD), 0)
    ids = jnp.zeros((8, HD), I32)
    for r in range(ROOTS):
        for c in range(NPRE):
            ids = jnp.where(lane == r * NPRE + c, prefix[r, c], ids)
    for r in range(MIG):
        for c in range(NOWN):
            ids = jnp.where(lane == PREFIX_IDS + r * NOWN + c, own[r, c], ids)
    forks = jnp.zeros((8, HD), I32)
    lens = jnp.zeros((8, HD), I32)
    for b in range(B):
        forks = jnp.where(row == b, fork[b], forks)
        lens = jnp.where(row == b, length[b], lens)
    is_prefix = lane < PREFIX_IDS
    moved = jnp.maximum(lane - PREFIX_IDS, 0)
    chunk = jnp.where(is_prefix, lane % NPRE, NPRE + moved % NOWN)
    wanted = (is_prefix & (forks == lane // NPRE)) | (~is_prefix & (row == moved // NOWN))
    tokens = jnp.where(wanted, jnp.clip(lens - PAGE * chunk, 0, PAGE), 0)
    place = jnp.where(row == 0, ids % P_DEV, 0)
    table = jnp.concatenate([tokens, place], 0).astype(F32).astype(BF16)
    holder = ids // P_DEV
    plane, row_y = holder // YN, holder % YN
    holder = ((plane % ZL) * YN + row_y) * MEMBERS + plane // ZL
    member = jnp.broadcast_to(holder[0:1], (POOL, HD)) == iota((POOL, HD), 0)
    earlier = (iota((HD, HD), 0) < iota((HD, HD), 1)).astype(F32).astype(BF16)
    rank = dot(member.astype(F32).astype(BF16), earlier)
    out = jnp.zeros((POOL, HD), F32)
    for s in range(SLOTS):
        chosen = jnp.where(member & (rank == float(s)), 1.0, 0.0).astype(BF16)
        parts = [table if k == s else jnp.zeros((16, HD), BF16) for k in range(HD // 16)]
        out = out + dot(chosen, jnp.concatenate(parts, 0), NT)
    req[...] = out.astype(I32)


def order_kernel(place, own, other, out):
    out[place[0]] = own[...]
    out[1 - place[0]] = other[...]


def prefetch_kernel(source, out, sems):
    part = out.shape[0] // sems.shape[0]
    copies = [
        pltpu.make_async_copy(source.at[pl.ds(n * part, part)], out.at[pl.ds(n * part, part)], sems.at[n])
        for n in range(sems.shape[0])
    ]
    for copy in copies:
        copy.start()
    for copy in copies:
        copy.wait()


def gather_kernel(places, req, store, out, stage, sems):
    copies = []
    for c in range(SOURCES):
        for n in range(MEMBERS):
            for s in range(SLOTS):
                at = places[c * MEMBERS + n, 16 * s + 8]
                start = n * KEYS + s * PAGE
                stage[c, pl.ds(start, PAGE), :] = store[at, 0]
                stage[c, pl.ds(PAGE_ROWS + start, PAGE), :] = store[at, 1]
        rows = req[pl.ds(c * MEMBERS, MEMBERS), :].astype(F32)
        rows = jnp.concatenate([rows, jnp.zeros((16 - MEMBERS, HD), F32)], 0)
        stage[c, pl.ds(2 * PAGE_ROWS, 16), :] = rows.astype(BF16)
        copy = pltpu.make_async_copy(stage.at[c], out.at[c], sems.at[c])
        copy.start()
        copies.append(copy)
    for copy in copies:
        copy.wait()


def local_kernel(own, length, q, fresh_k, fresh_v, store, sums, top, total, keys, values):
    branches = B - MIG
    span = NOWN * PAGE
    for b in range(branches):
        for p in range(NOWN):
            at = own[MIG + b, p] % P_DEV
            start = b * span + p * PAGE
            keys[pl.ds(start, PAGE), :] = store[at, 0]
            values[pl.ds(start, PAGE), :] = store[at, 1]
    rows = q[...]
    branch_of = (iota((ROWS, 1), 0) % 16) // STEPS
    step_of = iota((ROWS, 1), 0) % STEPS
    lane16 = iota((ROWS, 16), 1)
    score = dot(rows, fresh_k[...], NT) * SCALE
    ok = (lane16 // STEPS == branch_of) & (lane16 % STEPS <= step_of)
    blocks = [(jnp.where(ok, score, NEG), ok, fresh_v[...])]
    position = iota((ROWS, span), 1) + NPRE * PAGE
    for b in range(branches):
        score = dot(rows, keys[pl.ds(b * span, span), :], NT) * SCALE
        ok = (branch_of == MIG + b) & (position < length[MIG + b])
        blocks.append((jnp.where(ok, score, NEG), ok, values[pl.ds(b * span, span), :]))
    best = jnp.max(blocks[0][0], 1, keepdims=True)
    for score, _, _ in blocks[1:]:
        best = jnp.maximum(best, jnp.max(score, 1, keepdims=True))
    acc = jnp.zeros((ROWS, HD), F32)
    count = jnp.zeros((ROWS, 1), F32)
    for score, ok, value in blocks:
        weight = jnp.where(ok, jnp.exp(score - best), 0.0).astype(BF16)
        count = count + jnp.sum(weight.astype(F32), 1, keepdims=True)
        acc = acc + dot(weight, value)
    sums[...] = acc
    top[...] = jnp.broadcast_to(best, (ROWS, HD))
    total[...] = jnp.broadcast_to(count, (ROWS, HD))


def partial_kernel(source, queries, out, pages, meta, meta_sem, sems):
    size = PAGE_ROWS // PARTS
    per = MEMBERS // PARTS
    meta_copy = pltpu.make_async_copy(source.at[:, pl.ds(2 * PAGE_ROWS, 16), :], meta, meta_sem)
    meta_copy.start()
    copies = []
    for part in range(PARTS):
        group = []
        for kv in range(2):
            rows = pl.ds(kv * PAGE_ROWS + part * size, size)
            copy = pltpu.make_async_copy(source.at[:, rows, :], pages.at[:, rows, :], sems.at[part, kv])
            copy.start()
            group.append(copy)
        copies.append(group)
    meta_copy.wait()
    pick = iota((16, HD), 1) % 16 == iota((16, HD), 0) // STEPS
    stacks = []
    for k in range(SOURCES):
        tile = meta[k].astype(F32)
        rows = [jnp.where(pick, jnp.broadcast_to(tile[n : n + 1], (16, HD)), 0.0).astype(BF16) for n in range(MEMBERS)]
        stacks.append(jnp.concatenate(rows, 0))
    pairs = [jnp.concatenate(stacks[k : k + 2], 1) for k in range(0, SOURCES, 2)]
    shape = (2 * HD, 2 * KEYS)
    expand = iota(shape, 0) // HD * KEYS + (iota(shape, 0) % HD) // 16 * PAGE == iota(shape, 1) // PAGE * PAGE
    expand = expand & (iota(shape, 0) % HD < KEYS)
    tokens = dot(jnp.concatenate(pairs, 0), expand.astype(F32).astype(BF16))
    number = (iota((tokens.shape[0], 2 * KEYS), 1) % PAGE).astype(F32)
    mask = jnp.where(number < tokens, 0.0, NEG)
    column = iota((ROWS, HD), 1)
    row = iota((8, HD), 0)
    for part in range(PARTS):
        members = range(part * per, (part + 1) * per)
        for copy in copies[part]:
            copy.wait()
        scores = []
        for z in members:
            keys = jnp.concatenate([pages[k, pl.ds(z * KEYS, KEYS), :] for k in range(SOURCES)], 0)
            scores.append(dot(queries[z], keys, NT))
        stats = jnp.zeros((ROWS, HD), F32)
        weights = []
        for n, z in enumerate(members):
            rows = range(z * 16, SOURCES // 2 * MEMBERS * 16, MEMBERS * 16)
            bias = jnp.concatenate([mask[r : r + 16] for r in rows], 1)
            bias = jnp.concatenate([bias] * GROUP, 0)
            score = jnp.where(bias < 0.0, NEG, scores[n] * SCALE)
            best = jnp.max(score, 1, keepdims=True).astype(BF16).astype(F32)
            weight = jnp.where(bias < 0.0, 0.0, jnp.exp(score - best)).astype(BF16)
            count = jnp.sum(weight.astype(F32), 1, keepdims=True)
            weights.append(weight)
            stats = jnp.where(column == n, best, jnp.where(column == 8 + n, count, stats))
        turned = jnp.transpose(stats)[0:16]
        turned = jnp.concatenate([turned, jnp.zeros((16, HD - ROWS), F32)], 1)
        tops, counts = turned[0:8], turned[8:16]
        high = counts.astype(BF16).astype(F32)
        low = counts - high
        rows = []
        for n, z in enumerate(members):
            values = jnp.concatenate([pages[k, pl.ds(PAGE_ROWS + z * KEYS, KEYS), :] for k in range(SOURCES)], 0)
            tile = jnp.where(row == 1, high[n : n + 1], jnp.where(row == 2, low[n : n + 1], 0.0))
            rows += [dot(weights[n], values), jnp.where(row == 0, tops[n : n + 1], tile)]
        out[pl.ds(part * per * RES, per * RES), :] = jnp.concatenate(rows, 0).astype(BF16)


def finish_kernel(parts, sums, top, total, weight_hbm, out, weight, sems):
    copies = [
        pltpu.make_async_copy(weight_hbm.at[pl.ds(g * HD, HD), :], weight.at[pl.ds(g * HD, HD), :], sems.at[g])
        for g in range(GROUP)
    ]
    for copy in copies:
        copy.start()
    row = iota((8, HD), 0)
    tops = jnp.full((8, HD), NEG, F32)
    counts = jnp.zeros((8, HD), F32)
    received = []
    for z in range(0, MEMBERS, 2):
        pair = parts[pl.ds(z * RES, 2 * RES), :].astype(F32)
        received += [pair[0:RES], pair[RES : 2 * RES]]
    for z in range(MEMBERS):
        tile = received[z][ROWS:RES]
        tops = jnp.where(row == z, tile[0:1], tops)
        counts = jnp.where(row == z, tile[1:2] + tile[2:3], counts)
    tops = jnp.concatenate([tops, jnp.full((HD - 8, HD), NEG, F32)], 0)
    counts = jnp.concatenate([counts, jnp.zeros((HD - 8, HD), F32)], 0)
    tops = jnp.transpose(tops)[0:ROWS]
    counts = jnp.transpose(counts)[0:ROWS]
    own_top = top[...]
    best = jnp.maximum(jnp.max(tops, 1, keepdims=True), own_top)
    factor = jnp.exp(tops - best)
    own_factor = jnp.exp(own_top - best)
    denominator = jnp.sum(factor * counts, 1, keepdims=True) + own_factor * total[...]
    numerator = own_factor * sums[...]
    for z in range(MEMBERS):
        numerator = numerator + factor[:, z : z + 1] * received[z][0:ROWS]
    attended = (numerator / denominator).astype(BF16)
    result = jnp.zeros((16, weight.shape[1]), F32)
    for g in range(GROUP):
        copies[g].wait()
        result = result + dot(attended[16 * g : 16 * (g + 1)], weight[pl.ds(g * HD, HD), :])
    result = result.astype(BF16).astype(F32)
    width = out.shape[2]
    for k in range(TPN):
        out[k] = result[:, k * width : (k + 1) * width].astype(BF16)


def total_kernel(shares, out):
    total = shares[0].astype(F32)
    for k in range(1, TPN):
        total = total + shares[k].astype(F32)
    total = total.astype(BF16).astype(F32)
    for b in range(B):
        out[b] = total[STEPS * b : STEPS * (b + 1)].astype(BF16)


def call(kernel, out_shape, in_specs, name, scratch=(), cost=None, mib=12, out_specs=None):
    return pl.pallas_call(
        kernel,
        out_shape=out_shape,
        in_specs=in_specs,
        out_specs=jax.tree.map(lambda _: VMEM, out_shape) if out_specs is None else out_specs,
        scratch_shapes=scratch,
        cost_estimate=cost,
        compiler_params=pltpu.CompilerParams(vmem_limit_bytes=mib * 2**20),
        name=name,
    )


def hbm(x):
    return pltpu.with_memory_space_constraint(x, pltpu.HBM)


def vmem(x):
    return pltpu.with_memory_space_constraint(x, pltpu.VMEM)


def prefetch(x, name):
    return call(
        prefetch_kernel,
        pltpu.VMEM(x.shape, x.dtype),
        [HBM],
        name,
        [pltpu.SemaphoreType.DMA((8,))],
        out_specs=VMEM,
    )(hbm(x))


PARTIAL_SCRATCH = [
    pltpu.VMEM((SOURCES, CHUNK, HD), BF16),
    pltpu.VMEM((SOURCES, 16, HD), BF16),
    pltpu.SemaphoreType.DMA(()),
    pltpu.SemaphoreType.DMA((PARTS, 2)),
]


def swap(x, axes):
    return lax.all_to_all(x, axes, split_axis=0, concat_axis=0, tiled=True)


def shards(query, new_kv, kv_store, prefix_pages, fork_of, own_pages, lengths, o_weight):
    shape = jax.ShapeDtypeStruct
    store = kv_store.reshape(P_DEV, 2, PAGE, HD)
    request = call(
        request_kernel,
        shape((POOL, HD), I32),
        [HBM] * 4,
        "request",
        [
            pltpu.SMEM(prefix_pages.shape, I32),
            pltpu.SMEM(own_pages.shape, I32),
            pltpu.SMEM(fork_of.shape, I32),
            pltpu.SMEM(lengths.shape, I32),
            pltpu.SemaphoreType.DMA((4,)),
        ],
    )(hbm(prefix_pages), hbm(own_pages), hbm(fork_of), hbm(lengths))
    request = swap(request, NEAR + FAR)
    q = query.transpose(2, 0, 1, 3).reshape(ROWS, HD)
    other = lax.ppermute(q, "zm", [(0, 1), (1, 0)])
    place = lax.axis_index("zm").astype(I32).reshape(1)
    near = call(order_kernel, shape((ZM, ROWS, HD), BF16), [SMEM, VMEM, VMEM], "order")(place, q, other)
    request, near = lax.optimization_barrier((request, near))
    store = prefetch(store, "store_ahead")
    pages = call(
        gather_kernel,
        pltpu.HBM((SOURCES, CHUNK, HD), BF16),
        [SMEM, VMEM, VMEM],
        "gather_pages",
        [pltpu.VMEM((SOURCES, CHUNK, HD), BF16), pltpu.SemaphoreType.DMA((SOURCES,))],
        out_specs=HBM,
    )(request, request, vmem(store))
    near, pages = lax.optimization_barrier((near, pages))
    pages = swap(pages, NEAR)
    queries = lax.all_gather(near, "zh").reshape(MEMBERS, ROWS, HD)
    fresh_k = new_kv[:, :, 0, 0].reshape(B * STEPS, HD)
    fresh_v = new_kv[:, :, 1, 0].reshape(B * STEPS, HD)
    local = call(
        local_kernel,
        [shape((ROWS, HD), F32)] * 3,
        [SMEM, SMEM, VMEM, VMEM, VMEM, VMEM],
        "resident",
        [pltpu.VMEM(((B - MIG) * NOWN * PAGE, HD), BF16)] * 2,
        pl.CostEstimate(flops=10**8, bytes_accessed=3 * 2**20, transcendentals=10**5),
    )(own_pages, lengths, q, fresh_k, fresh_v, store)
    parts = call(partial_kernel, shape((MEMBERS * RES, HD), BF16), [HBM, VMEM], "partials", PARTIAL_SCRATCH)(
        pages, queries
    )
    parts = swap(parts.reshape(MEMBERS, RES, HD), FAR).reshape(MEMBERS * RES, HD)
    width = o_weight.shape[1] // TPN
    shares = call(
        finish_kernel,
        shape((TPN, 16, width), BF16),
        [VMEM] * 4 + [HBM],
        "finish",
        [pltpu.VMEM(o_weight.shape, BF16), pltpu.SemaphoreType.DMA((GROUP,))],
    )(parts, *local, hbm(o_weight))
    shares = swap(shares, ("x", "c"))
    return call(total_kernel, shape((B, STEPS, width), BF16), [VMEM], "total")(shares)


def solution(mesh):
    fine = Mesh(mesh.devices.reshape(ZH, ZM, ZL, YN, XN, CN), POOL_AXES + ("x", "c"))
    pool, tp = POOL_AXES, ("x", "c")
    return jax.shard_map(
        shards,
        mesh=fine,
        in_specs=(
            P(pool, None, tp, None),
            P(pool, None, None, tp, None),
            P(pool, None, tp, None, None),
            P(pool, None),
            P(pool),
            P(pool, None),
            P(pool),
            P(tp, None),
        ),
        out_specs=P(pool, None, tp),
        check_vma=False,
    )
```

```python
import math

import jax
import jax.numpy as jnp
from jax import lax
from jax.experimental import pallas as pl
from jax.experimental.pallas import tpu as pltpu
from jax.sharding import Mesh
from jax.sharding import PartitionSpec as P

F32 = jnp.float32
BF16 = jnp.bfloat16
I32 = jnp.int32

HD = 128
PAGE = 16
NPRE = 8
NOWN = 24
ROOTS = 4
B = 8
MIG = 4
STEPS = 2
GROUP = 4
ROWS = B * STEPS * GROUP
SLOTS = 4
P_DEV = 256
NEG = -(2.0**100)
SCALE = 1.0 / math.sqrt(HD)
ZN, YN, XN, CN = 16, 4, 4, 2
ZH, ZM, ZL = 4, 2, 2
PARTS = 2
POOL_AXES = ("zh", "zm", "zl", "y")
NEAR = ("zl", "y")
FAR = ("zh", "zm")
SOURCES = ZL * YN
MEMBERS = ZH * ZM
POOL = ZN * YN
TPN = XN * CN
PREFIX_IDS = ROOTS * NPRE
KEYS = SLOTS * PAGE
PAGE_ROWS = MEMBERS * KEYS
CHUNK = 2 * PAGE_ROWS + 16
RES = ROWS + 8

VMEM = pl.BlockSpec(memory_space=pltpu.VMEM)
SMEM = pl.BlockSpec(memory_space=pltpu.SMEM)
HBM = pl.BlockSpec(memory_space=pltpu.HBM)
ANY = pl.BlockSpec(memory_space=pl.ANY)
NT = (((1,), (1,)), ((), ()))
NN = (((1,), (0,)), ((), ()))


def iota(shape, dim):
    return lax.broadcasted_iota(I32, shape, dim)


def dot(a, b, dims=NN):
    return lax.dot_general(a, b, dims, preferred_element_type=F32)


def request_kernel(prefix_hbm, own_hbm, fork_hbm, length_hbm, req, prefix, own, fork, length, sems):
    pairs = ((prefix_hbm, prefix), (own_hbm, own), (fork_hbm, fork), (length_hbm, length))
    copies = [pltpu.make_async_copy(a, b, sems.at[n]) for n, (a, b) in enumerate(pairs)]
    for copy in copies:
        copy.start()
    for copy in copies:
        copy.wait()
    lane = iota((8, HD), 1)
    row = iota((8, HD), 0)
    ids = jnp.zeros((8, HD), I32)
    for r in range(ROOTS):
        for c in range(NPRE):
            ids = jnp.where(lane == r * NPRE + c, prefix[r, c], ids)
    for r in range(MIG):
        for c in range(NOWN):
            ids = jnp.where(lane == PREFIX_IDS + r * NOWN + c, own[r, c], ids)
    forks = jnp.zeros((8, HD), I32)
    lens = jnp.zeros((8, HD), I32)
    for b in range(B):
        forks = jnp.where(row == b, fork[b], forks)
        lens = jnp.where(row == b, length[b], lens)
    is_prefix = lane < PREFIX_IDS
    moved = jnp.maximum(lane - PREFIX_IDS, 0)
    chunk = jnp.where(is_prefix, lane % NPRE, NPRE + moved % NOWN)
    wanted = (is_prefix & (forks == lane // NPRE)) | (~is_prefix & (row == moved // NOWN))
    tokens = jnp.where(wanted, jnp.clip(lens - PAGE * chunk, 0, PAGE), 0)
    place = jnp.where(row == 0, ids % P_DEV, 0)
    table = jnp.concatenate([tokens, place], 0).astype(F32).astype(BF16)
    holder = ids // P_DEV
    plane, row_y = holder // YN, holder % YN
    holder = ((plane % ZL) * YN + row_y) * MEMBERS + plane // ZL
    member = jnp.broadcast_to(holder[0:1], (POOL, HD)) == iota((POOL, HD), 0)
    earlier = (iota((HD, HD), 0) < iota((HD, HD), 1)).astype(F32).astype(BF16)
    rank = dot(member.astype(F32).astype(BF16), earlier)
    out = jnp.zeros((POOL, HD), F32)
    for s in range(SLOTS):
        chosen = jnp.where(member & (rank == float(s)), 1.0, 0.0).astype(BF16)
        parts = [table if k == s else jnp.zeros((16, HD), BF16) for k in range(HD // 16)]
        out = out + dot(chosen, jnp.concatenate(parts, 0), NT)
    req[...] = out.astype(I32)


def stack_kernel(own, other, out):
    half = own.shape[0]
    out[pl.ds(0, half)] = own[...]
    out[pl.ds(half, half)] = other[...]


def prefetch_kernel(source, out, sems):
    part = out.shape[0] // sems.shape[0]
    copies = [
        pltpu.make_async_copy(source.at[pl.ds(n * part, part)], out.at[pl.ds(n * part, part)], sems.at[n])
        for n in range(sems.shape[0])
    ]
    for copy in copies:
        copy.start()
    for copy in copies:
        copy.wait()


def gather_kernel(places, req, store, out, stage, sems):
    copies = []
    for c in range(SOURCES):
        for n in range(MEMBERS):
            for s in range(SLOTS):
                at = places[c * MEMBERS + n, 16 * s + 8]
                start = n * KEYS + s * PAGE
                stage[c, pl.ds(start, PAGE), :] = store[at, 0]
                stage[c, pl.ds(PAGE_ROWS + start, PAGE), :] = store[at, 1]
        rows = req[pl.ds(c * MEMBERS, MEMBERS), :].astype(F32)
        rows = jnp.concatenate([rows, jnp.zeros((16 - MEMBERS, HD), F32)], 0)
        stage[c, pl.ds(2 * PAGE_ROWS, 16), :] = rows.astype(BF16)
        copy = pltpu.make_async_copy(stage.at[c], out.at[c], sems.at[c])
        copy.start()
        copies.append(copy)
    for copy in copies:
        copy.wait()


def local_kernel(own, length, q, fresh_k, fresh_v, store, sums, top, total, keys, values):
    branches = B - MIG
    span = NOWN * PAGE
    for b in range(branches):
        for p in range(NOWN):
            at = own[MIG + b, p] % P_DEV
            start = b * span + p * PAGE
            keys[pl.ds(start, PAGE), :] = store[at, 0]
            values[pl.ds(start, PAGE), :] = store[at, 1]
    rows = q[...]
    branch_of = (iota((ROWS, 1), 0) % 16) // STEPS
    step_of = iota((ROWS, 1), 0) % STEPS
    lane16 = iota((ROWS, 16), 1)
    score = dot(rows, fresh_k[...], NT) * SCALE
    ok = (lane16 // STEPS == branch_of) & (lane16 % STEPS <= step_of)
    blocks = [(jnp.where(ok, score, NEG), ok, fresh_v[...])]
    position = iota((ROWS, span), 1) + NPRE * PAGE
    for b in range(branches):
        score = dot(rows, keys[pl.ds(b * span, span), :], NT) * SCALE
        ok = (branch_of == MIG + b) & (position < length[MIG + b])
        blocks.append((jnp.where(ok, score, NEG), ok, values[pl.ds(b * span, span), :]))
    best = jnp.max(blocks[0][0], 1, keepdims=True)
    for score, _, _ in blocks[1:]:
        best = jnp.maximum(best, jnp.max(score, 1, keepdims=True))
    acc = jnp.zeros((ROWS, HD), F32)
    count = jnp.zeros((ROWS, 1), F32)
    for score, ok, value in blocks:
        weight = jnp.where(ok, jnp.exp(score - best), 0.0).astype(BF16)
        count = count + jnp.sum(weight.astype(F32), 1, keepdims=True)
        acc = acc + dot(weight, value)
    sums[...] = acc
    top[...] = jnp.broadcast_to(best, (ROWS, HD))
    total[...] = jnp.broadcast_to(count, (ROWS, HD))


def partial_kernel(me, source, near, far, out, pages, meta, queries, meta_sem, sems):
    size = PAGE_ROWS // PARTS
    per = MEMBERS // PARTS
    meta_copy = pltpu.make_async_copy(source.at[:, pl.ds(2 * PAGE_ROWS, 16), :], meta, meta_sem)
    meta_copy.start()
    copies = []
    for part in range(PARTS):
        group = []
        for kv in range(2):
            rows = pl.ds(kv * PAGE_ROWS + part * size, size)
            copy = pltpu.make_async_copy(source.at[:, rows, :], pages.at[:, rows, :], sems.at[part, kv])
            copy.start()
            group.append(copy)
        copies.append(group)
    for r in range(MEMBERS):
        half = near if r < MEMBERS // 2 else far
        queries[me[0] ^ r] = half[r % (MEMBERS // 2)]
    meta_copy.wait()
    pick = iota((16, HD), 1) % 16 == iota((16, HD), 0) // STEPS
    stacks = []
    for k in range(SOURCES):
        tile = meta[k].astype(F32)
        rows = [jnp.where(pick, jnp.broadcast_to(tile[n : n + 1], (16, HD)), 0.0).astype(BF16) for n in range(MEMBERS)]
        stacks.append(jnp.concatenate(rows, 0))
    pairs = [jnp.concatenate(stacks[k : k + 2], 1) for k in range(0, SOURCES, 2)]
    shape = (2 * HD, 2 * KEYS)
    expand = iota(shape, 0) // HD * KEYS + (iota(shape, 0) % HD) // 16 * PAGE == iota(shape, 1) // PAGE * PAGE
    expand = expand & (iota(shape, 0) % HD < KEYS)
    tokens = dot(jnp.concatenate(pairs, 0), expand.astype(F32).astype(BF16))
    number = (iota((tokens.shape[0], 2 * KEYS), 1) % PAGE).astype(F32)
    mask = jnp.where(number < tokens, 0.0, NEG)
    column = iota((ROWS, HD), 1)
    row = iota((8, HD), 0)
    for part in range(PARTS):
        members = range(part * per, (part + 1) * per)
        for copy in copies[part]:
            copy.wait()
        scores = []
        for z in members:
            keys = jnp.concatenate([pages[k, pl.ds(z * KEYS, KEYS), :] for k in range(SOURCES)], 0)
            scores.append(dot(queries[z], keys, NT))
        stats = jnp.zeros((ROWS, HD), F32)
        weights = []
        for n, z in enumerate(members):
            rows = range(z * 16, SOURCES // 2 * MEMBERS * 16, MEMBERS * 16)
            bias = jnp.concatenate([mask[r : r + 16] for r in rows], 1)
            bias = jnp.concatenate([bias] * GROUP, 0)
            score = jnp.where(bias < 0.0, NEG, scores[n] * SCALE)
            best = jnp.max(score, 1, keepdims=True).astype(BF16).astype(F32)
            weight = jnp.where(bias < 0.0, 0.0, jnp.exp(score - best)).astype(BF16)
            count = jnp.sum(weight.astype(F32), 1, keepdims=True)
            weights.append(weight)
            stats = jnp.where(column == n, best, jnp.where(column == 8 + n, count, stats))
        turned = jnp.transpose(stats)[0:16]
        turned = jnp.concatenate([turned, jnp.zeros((16, HD - ROWS), F32)], 1)
        tops, counts = turned[0:8], turned[8:16]
        high = counts.astype(BF16).astype(F32)
        low = counts - high
        rows = []
        for n, z in enumerate(members):
            values = jnp.concatenate([pages[k, pl.ds(PAGE_ROWS + z * KEYS, KEYS), :] for k in range(SOURCES)], 0)
            tile = jnp.where(row == 1, high[n : n + 1], jnp.where(row == 2, low[n : n + 1], 0.0))
            rows += [dot(weights[n], values), jnp.where(row == 0, tops[n : n + 1], tile)]
        out[pl.ds(part * per * RES, per * RES), :] = jnp.concatenate(rows, 0).astype(BF16)


def finish_kernel(parts, sums, top, total, weight_hbm, out, weight, sems):
    copies = [
        pltpu.make_async_copy(weight_hbm.at[pl.ds(g * HD, HD), :], weight.at[pl.ds(g * HD, HD), :], sems.at[g])
        for g in range(GROUP)
    ]
    for copy in copies:
        copy.start()
    row = iota((8, HD), 0)
    tops = jnp.full((8, HD), NEG, F32)
    counts = jnp.zeros((8, HD), F32)
    received = []
    for z in range(0, MEMBERS, 2):
        pair = parts[pl.ds(z * RES, 2 * RES), :].astype(F32)
        received += [pair[0:RES], pair[RES : 2 * RES]]
    for z in range(MEMBERS):
        tile = received[z][ROWS:RES]
        tops = jnp.where(row == z, tile[0:1], tops)
        counts = jnp.where(row == z, tile[1:2] + tile[2:3], counts)
    tops = jnp.concatenate([tops, jnp.full((HD - 8, HD), NEG, F32)], 0)
    counts = jnp.concatenate([counts, jnp.zeros((HD - 8, HD), F32)], 0)
    tops = jnp.transpose(tops)[0:ROWS]
    counts = jnp.transpose(counts)[0:ROWS]
    own_top = top[...]
    best = jnp.maximum(jnp.max(tops, 1, keepdims=True), own_top)
    factor = jnp.exp(tops - best)
    own_factor = jnp.exp(own_top - best)
    denominator = jnp.sum(factor * counts, 1, keepdims=True) + own_factor * total[...]
    numerator = own_factor * sums[...]
    for z in range(MEMBERS):
        numerator = numerator + factor[:, z : z + 1] * received[z][0:ROWS]
    attended = (numerator / denominator).astype(BF16)
    result = jnp.zeros((16, weight.shape[1]), F32)
    for g in range(GROUP):
        copies[g].wait()
        result = result + dot(attended[16 * g : 16 * (g + 1)], weight[pl.ds(g * HD, HD), :])
    result = result.astype(BF16).astype(F32)
    width = out.shape[2]
    for k in range(TPN):
        out[k] = result[:, k * width : (k + 1) * width].astype(BF16)


def total_kernel(shares, out):
    total = shares[0].astype(F32)
    for k in range(1, TPN):
        total = total + shares[k].astype(F32)
    total = total.astype(BF16).astype(F32)
    for b in range(B):
        out[b] = total[STEPS * b : STEPS * (b + 1)].astype(BF16)


def call(kernel, out_shape, in_specs, name, scratch=(), cost=None, mib=12, out_specs=None):
    return pl.pallas_call(
        kernel,
        out_shape=out_shape,
        in_specs=in_specs,
        out_specs=jax.tree.map(lambda _: VMEM, out_shape) if out_specs is None else out_specs,
        scratch_shapes=scratch,
        cost_estimate=cost,
        compiler_params=pltpu.CompilerParams(vmem_limit_bytes=mib * 2**20),
        name=name,
    )


def hbm(x):
    return pltpu.with_memory_space_constraint(x, pltpu.HBM)


def vmem(x):
    return pltpu.with_memory_space_constraint(x, pltpu.VMEM)


def prefetch(x, name):
    return call(
        prefetch_kernel,
        pltpu.VMEM(x.shape, x.dtype),
        [HBM],
        name,
        [pltpu.SemaphoreType.DMA((8,))],
        out_specs=VMEM,
    )(hbm(x))


PARTIAL_SCRATCH = [
    pltpu.VMEM((SOURCES, CHUNK, HD), BF16),
    pltpu.VMEM((SOURCES, 16, HD), BF16),
    pltpu.VMEM((MEMBERS, ROWS, HD), BF16),
    pltpu.SemaphoreType.DMA(()),
    pltpu.SemaphoreType.DMA((PARTS, 2)),
]


def swap(x, axes):
    return lax.all_to_all(x, axes, split_axis=0, concat_axis=0, tiled=True)


def shards(query, new_kv, kv_store, prefix_pages, fork_of, own_pages, lengths, o_weight):
    shape = jax.ShapeDtypeStruct
    store = kv_store.reshape(P_DEV, 2, PAGE, HD)
    request = call(
        request_kernel,
        shape((POOL, HD), I32),
        [HBM] * 4,
        "request",
        [
            pltpu.SMEM(prefix_pages.shape, I32),
            pltpu.SMEM(own_pages.shape, I32),
            pltpu.SMEM(fork_of.shape, I32),
            pltpu.SMEM(lengths.shape, I32),
            pltpu.SemaphoreType.DMA((4,)),
        ],
    )(hbm(prefix_pages), hbm(own_pages), hbm(fork_of), hbm(lengths))
    request = swap(request, NEAR + FAR)
    q = query.transpose(2, 0, 1, 3).reshape(ROWS, HD)
    near = q[None]
    for axis, pairs in (("zm", [(0, 1), (1, 0)]), ("zh", [(0, 1), (1, 0), (2, 3), (3, 2)])):
        other = lax.ppermute(near, axis, pairs)
        near = call(stack_kernel, shape((2 * near.shape[0], ROWS, HD), BF16), [VMEM, VMEM], "stack")(near, other)
    request, near = lax.optimization_barrier((request, near))
    store = prefetch(store, "store_ahead")
    pages = call(
        gather_kernel,
        pltpu.HBM((SOURCES, CHUNK, HD), BF16),
        [SMEM, VMEM, VMEM],
        "gather_pages",
        [pltpu.VMEM((SOURCES, CHUNK, HD), BF16), pltpu.SemaphoreType.DMA((SOURCES,))],
        out_specs=HBM,
    )(request, request, vmem(store))
    near, pages = lax.optimization_barrier((near, pages))
    pages = swap(pages, NEAR)
    far = lax.ppermute(near, "zh", [(0, 2), (1, 3), (2, 0), (3, 1)])
    me = (lax.axis_index("zh") * ZM + lax.axis_index("zm")).astype(I32).reshape(1)
    fresh_k = new_kv[:, :, 0, 0].reshape(B * STEPS, HD)
    fresh_v = new_kv[:, :, 1, 0].reshape(B * STEPS, HD)
    local = call(
        local_kernel,
        [shape((ROWS, HD), F32)] * 3,
        [SMEM, SMEM, VMEM, VMEM, VMEM, VMEM],
        "resident",
        [pltpu.VMEM(((B - MIG) * NOWN * PAGE, HD), BF16)] * 2,
        pl.CostEstimate(flops=10**8, bytes_accessed=3 * 2**20, transcendentals=10**5),
    )(own_pages, lengths, q, fresh_k, fresh_v, store)
    parts = call(
        partial_kernel, shape((MEMBERS * RES, HD), BF16), [SMEM, HBM, VMEM, VMEM], "partials", PARTIAL_SCRATCH
    )(me, pages, near, far)
    parts = swap(parts.reshape(MEMBERS, RES, HD), FAR).reshape(MEMBERS * RES, HD)
    width = o_weight.shape[1] // TPN
    shares = call(
        finish_kernel,
        shape((TPN, 16, width), BF16),
        [VMEM] * 4 + [HBM],
        "finish",
        [pltpu.VMEM(o_weight.shape, BF16), pltpu.SemaphoreType.DMA((GROUP,))],
    )(parts, *local, hbm(o_weight))
    shares = swap(shares, ("x", "c"))
    return call(total_kernel, shape((B, STEPS, width), BF16), [VMEM], "total")(shares)


def solution(mesh):
    fine = Mesh(mesh.devices.reshape(ZH, ZM, ZL, YN, XN, CN), POOL_AXES + ("x", "c"))
    pool, tp = POOL_AXES, ("x", "c")
    return jax.shard_map(
        shards,
        mesh=fine,
        in_specs=(
            P(pool, None, tp, None),
            P(pool, None, None, tp, None),
            P(pool, None, tp, None, None),
            P(pool, None),
            P(pool),
            P(pool, None),
            P(pool),
            P(tp, None),
        ),
        out_specs=P(pool, None, tp),
        check_vma=False,
    )
```

```python
import math

import jax
import jax.numpy as jnp
from jax import lax
from jax.experimental import pallas as pl
from jax.experimental.pallas import tpu as pltpu
from jax.sharding import Mesh
from jax.sharding import PartitionSpec as P

F32 = jnp.float32
BF16 = jnp.bfloat16
I32 = jnp.int32

HD = 128
PAGE = 16
NPRE = 8
NOWN = 24
ROOTS = 4
B = 8
MIG = 4
STEPS = 2
GROUP = 4
ROWS = B * STEPS * GROUP
SLOTS = 4
P_DEV = 256
NEG = -(2.0**100)
SCALE = 1.0 / math.sqrt(HD)
ZN, YN, XN, CN = 16, 4, 4, 2
ZH, ZM, ZL = 4, 2, 2
PARTS = 1
POOL_AXES = ("zh", "zm", "zl", "y")
NEAR = ("zl", "y")
FAR = ("zh", "zm")
SOURCES = ZL * YN
MEMBERS = ZH * ZM
POOL = ZN * YN
TPN = XN * CN
PREFIX_IDS = ROOTS * NPRE
KEYS = SLOTS * PAGE
PAGE_ROWS = MEMBERS * KEYS
QROWS = STEPS * GROUP
TAIL = MEMBERS * QROWS + 16
CHUNK = 2 * PAGE_ROWS + TAIL
RES = ROWS + 8

VMEM = pl.BlockSpec(memory_space=pltpu.VMEM)
SMEM = pl.BlockSpec(memory_space=pltpu.SMEM)
HBM = pl.BlockSpec(memory_space=pltpu.HBM)
ANY = pl.BlockSpec(memory_space=pl.ANY)
NT = (((1,), (1,)), ((), ()))
NN = (((1,), (0,)), ((), ()))


def iota(shape, dim):
    return lax.broadcasted_iota(I32, shape, dim)


def dot(a, b, dims=NN):
    return lax.dot_general(a, b, dims, preferred_element_type=F32)


def request_kernel(prefix_hbm, own_hbm, fork_hbm, length_hbm, query, req, q, prefix, own, fork, length, sems):
    pairs = ((prefix_hbm, prefix), (own_hbm, own), (fork_hbm, fork), (length_hbm, length))
    copies = [pltpu.make_async_copy(a, b, sems.at[n]) for n, (a, b) in enumerate(pairs)]
    for copy in copies:
        copy.start()
    for copy in copies:
        copy.wait()
    lane = iota((8, HD), 1)
    row = iota((8, HD), 0)
    ids = jnp.zeros((8, HD), I32)
    for r in range(ROOTS):
        for c in range(NPRE):
            ids = jnp.where(lane == r * NPRE + c, prefix[r, c], ids)
    for r in range(MIG):
        for c in range(NOWN):
            ids = jnp.where(lane == PREFIX_IDS + r * NOWN + c, own[r, c], ids)
    forks = jnp.zeros((8, HD), I32)
    lens = jnp.zeros((8, HD), I32)
    for b in range(B):
        forks = jnp.where(row == b, fork[b], forks)
        lens = jnp.where(row == b, length[b], lens)
    is_prefix = lane < PREFIX_IDS
    moved = jnp.maximum(lane - PREFIX_IDS, 0)
    chunk = jnp.where(is_prefix, lane % NPRE, NPRE + moved % NOWN)
    wanted = (is_prefix & (forks == lane // NPRE)) | (~is_prefix & (row == moved // NOWN))
    tokens = jnp.where(wanted, jnp.clip(lens - PAGE * chunk, 0, PAGE), 0)
    place = jnp.where(row == 0, ids % P_DEV, 0)
    table = jnp.concatenate([tokens, place], 0).astype(F32).astype(BF16)
    holder = ids // P_DEV
    plane, row_y = holder // YN, holder % YN
    holder = ((plane % ZL) * YN + row_y) * MEMBERS + plane // ZL
    member = jnp.broadcast_to(holder[0:1], (POOL, HD)) == iota((POOL, HD), 0)
    earlier = (iota((HD, HD), 0) < iota((HD, HD), 1)).astype(F32).astype(BF16)
    rank = dot(member.astype(F32).astype(BF16), earlier)
    out = jnp.zeros((POOL, HD), F32)
    for s in range(SLOTS):
        chosen = jnp.where(member & (rank == float(s)), 1.0, 0.0).astype(BF16)
        parts = [table if k == s else jnp.zeros((16, HD), BF16) for k in range(HD // 16)]
        out = out + dot(chosen, jnp.concatenate(parts, 0), NT)
    for b in range(B):
        rows = jnp.concatenate([query[b, t].astype(F32) for t in range(STEPS)], 0)
        for m in range(MEMBERS):
            d = b * MEMBERS + m
            req[d] = jnp.concatenate([rows, jnp.broadcast_to(out[d : d + 1], (8, HD))], 0).astype(BF16)
    for b in range(0, B, 2):
        rows = [query[n, t].astype(F32) for n in (b, b + 1) for t in range(STEPS)]
        q[pl.ds(b * QROWS, 2 * QROWS), :] = jnp.concatenate(rows, 0).astype(BF16)


def prefetch_kernel(source, out, sems):
    part = out.shape[0] // sems.shape[0]
    copies = [
        pltpu.make_async_copy(source.at[pl.ds(n * part, part)], out.at[pl.ds(n * part, part)], sems.at[n])
        for n in range(sems.shape[0])
    ]
    for copy in copies:
        copy.start()
    for copy in copies:
        copy.wait()


def gather_kernel(req, store, out, stage, wanted, places, place_sem, sems):
    row = iota((MEMBERS, HD), 0)
    tails = []
    for c in range(SOURCES):
        tiles = [req[c * MEMBERS + n].astype(F32) for n in range(MEMBERS)]
        asked = tiles[0][8:16]
        for n in range(1, MEMBERS):
            asked = jnp.where(row == n, tiles[n][8:16], asked)
        wanted[pl.ds(c * MEMBERS, MEMBERS), :] = asked.astype(I32)
        tails.append([tile[0:8] for tile in tiles] + [asked, jnp.zeros((16 - MEMBERS, HD), F32)])
    copy = pltpu.make_async_copy(wanted, places, place_sem)
    copy.start()
    for c in range(SOURCES):
        stage[c, pl.ds(2 * PAGE_ROWS, TAIL), :] = jnp.concatenate(tails[c], 0).astype(BF16)
    copy.wait()
    copies = []
    for c in range(SOURCES):
        for n in range(MEMBERS):
            for s in range(SLOTS):
                at = places[c * MEMBERS + n, 16 * s + 8]
                start = n * KEYS + s * PAGE
                stage[c, pl.ds(start, PAGE), :] = store[at, 0]
                stage[c, pl.ds(PAGE_ROWS + start, PAGE), :] = store[at, 1]
        copy = pltpu.make_async_copy(stage.at[c], out.at[c], sems.at[c])
        copy.start()
        copies.append(copy)
    for copy in copies:
        copy.wait()


def local_kernel(own, length, q, fresh_k, fresh_v, store, sums, top, total, keys, values):
    branches = B - MIG
    span = NOWN * PAGE
    for b in range(branches):
        for p in range(NOWN):
            at = own[MIG + b, p] % P_DEV
            start = b * span + p * PAGE
            keys[pl.ds(start, PAGE), :] = store[at, 0]
            values[pl.ds(start, PAGE), :] = store[at, 1]
    rows = q[...]
    branch_of = iota((ROWS, 1), 0) // QROWS
    step_of = iota((ROWS, 1), 0) // GROUP % STEPS
    lane16 = iota((ROWS, 16), 1)
    score = dot(rows, fresh_k[...], NT) * SCALE
    ok = (lane16 // STEPS == branch_of) & (lane16 % STEPS <= step_of)
    blocks = [(jnp.where(ok, score, NEG), ok, fresh_v[...])]
    position = iota((ROWS, span), 1) + NPRE * PAGE
    for b in range(branches):
        score = dot(rows, keys[pl.ds(b * span, span), :], NT) * SCALE
        ok = (branch_of == MIG + b) & (position < length[MIG + b])
        blocks.append((jnp.where(ok, score, NEG), ok, values[pl.ds(b * span, span), :]))
    best = jnp.max(blocks[0][0], 1, keepdims=True)
    for score, _, _ in blocks[1:]:
        best = jnp.maximum(best, jnp.max(score, 1, keepdims=True))
    acc = jnp.zeros((ROWS, HD), F32)
    count = jnp.zeros((ROWS, 1), F32)
    for score, ok, value in blocks:
        weight = jnp.where(ok, jnp.exp(score - best), 0.0).astype(BF16)
        count = count + jnp.sum(weight.astype(F32), 1, keepdims=True)
        acc = acc + dot(weight, value)
    sums[...] = acc
    top[...] = jnp.broadcast_to(best, (ROWS, HD))
    total[...] = jnp.broadcast_to(count, (ROWS, HD))


def partial_kernel(pages, out):
    per = MEMBERS // PARTS
    pick = iota((B, HD), 1) % 16 == iota((B, HD), 0)
    stacks = []
    asking = []
    for k in range(SOURCES):
        tail = pages[k, pl.ds(2 * PAGE_ROWS, TAIL), :].astype(F32)
        asking.append(tail)
        tile = tail[MEMBERS * QROWS : MEMBERS * QROWS + MEMBERS]
        rows = [jnp.where(pick, jnp.broadcast_to(tile[n : n + 1], (B, HD)), 0.0) for n in range(MEMBERS)]
        stacks.append(jnp.concatenate(rows, 0).astype(BF16))
    pairs = [jnp.concatenate(stacks[k : k + 2], 1) for k in range(0, SOURCES, 2)]
    shape = (2 * HD, 2 * KEYS)
    expand = iota(shape, 0) // HD * KEYS + (iota(shape, 0) % HD) // 16 * PAGE == iota(shape, 1) // PAGE * PAGE
    expand = expand & (iota(shape, 0) % HD < KEYS)
    tokens = dot(jnp.concatenate(pairs, 0), expand.astype(F32).astype(BF16))
    number = (iota((tokens.shape[0], 2 * KEYS), 1) % PAGE).astype(F32)
    mask = jnp.where(number < tokens, 0.0, NEG)
    column = iota((ROWS, HD), 1)
    row = iota((8, HD), 0)
    for part in range(PARTS):
        members = range(part * per, (part + 1) * per)
        scores = []
        for z in members:
            keys = jnp.concatenate([pages[k, pl.ds(z * KEYS, KEYS), :] for k in range(SOURCES)], 0)
            queries = jnp.concatenate([tail[z * QROWS : (z + 1) * QROWS] for tail in asking], 0).astype(BF16)
            scores.append(dot(queries, keys, NT))
        stats = jnp.zeros((ROWS, HD), F32)
        weights = []
        for n, z in enumerate(members):
            rows = range(z * B, SOURCES // 2 * MEMBERS * B, MEMBERS * B)
            bias = jnp.concatenate([mask[r : r + B] for r in rows], 1)
            bias = jnp.concatenate([jnp.broadcast_to(bias[b : b + 1], (QROWS, bias.shape[1])) for b in range(B)], 0)
            score = jnp.where(bias < 0.0, NEG, scores[n] * SCALE)
            best = jnp.max(score, 1, keepdims=True).astype(BF16).astype(F32)
            weight = jnp.where(bias < 0.0, 0.0, jnp.exp(score - best)).astype(BF16)
            count = jnp.sum(weight.astype(F32), 1, keepdims=True)
            weights.append(weight)
            stats = jnp.where(column == n, best, jnp.where(column == 8 + n, count, stats))
        turned = jnp.transpose(stats)[0:16]
        turned = jnp.concatenate([turned, jnp.zeros((16, HD - ROWS), F32)], 1)
        tops, counts = turned[0:8], turned[8:16]
        high = counts.astype(BF16).astype(F32)
        low = counts - high
        rows = []
        for n, z in enumerate(members):
            values = jnp.concatenate([pages[k, pl.ds(PAGE_ROWS + z * KEYS, KEYS), :] for k in range(SOURCES)], 0)
            tile = jnp.where(row == 1, high[n : n + 1], jnp.where(row == 2, low[n : n + 1], 0.0))
            rows += [dot(weights[n], values), jnp.where(row == 0, tops[n : n + 1], tile)]
        out[pl.ds(part * per * RES, per * RES), :] = jnp.concatenate(rows, 0).astype(BF16)


def finish_kernel(parts, sums, top, total, weight_hbm, out, weight, rows, sems):
    copies = [
        pltpu.make_async_copy(weight_hbm.at[pl.ds(g * HD, HD), :], weight.at[pl.ds(g * HD, HD), :], sems.at[g])
        for g in range(GROUP)
    ]
    for copy in copies:
        copy.start()
    row = iota((8, HD), 0)
    tops = jnp.full((8, HD), NEG, F32)
    counts = jnp.zeros((8, HD), F32)
    received = []
    for z in range(0, MEMBERS, 2):
        pair = parts[pl.ds(z * RES, 2 * RES), :].astype(F32)
        received += [pair[0:RES], pair[RES : 2 * RES]]
    for z in range(MEMBERS):
        tile = received[z][ROWS:RES]
        tops = jnp.where(row == z, tile[0:1], tops)
        counts = jnp.where(row == z, tile[1:2] + tile[2:3], counts)
    tops = jnp.concatenate([tops, jnp.full((HD - 8, HD), NEG, F32)], 0)
    counts = jnp.concatenate([counts, jnp.zeros((HD - 8, HD), F32)], 0)
    tops = jnp.transpose(tops)[0:ROWS]
    counts = jnp.transpose(counts)[0:ROWS]
    own_top = top[...]
    best = jnp.maximum(jnp.max(tops, 1, keepdims=True), own_top)
    factor = jnp.exp(tops - best)
    own_factor = jnp.exp(own_top - best)
    denominator = jnp.sum(factor * counts, 1, keepdims=True) + own_factor * total[...]
    numerator = own_factor * sums[...]
    for z in range(MEMBERS):
        numerator = numerator + factor[:, z : z + 1] * received[z][0:ROWS]
    rows[...] = numerator / denominator
    result = jnp.zeros((16, weight.shape[1]), F32)
    for g in range(GROUP):
        copies[g].wait()
        attended = rows[pl.ds(g, 16, stride=GROUP), :].astype(BF16)
        result = result + dot(attended, weight[pl.ds(g * HD, HD), :])
    result = result.astype(BF16).astype(F32)
    width = out.shape[2]
    for k in range(TPN):
        out[k] = result[:, k * width : (k + 1) * width].astype(BF16)


def total_kernel(shares, out):
    total = shares[0].astype(F32)
    for k in range(1, TPN):
        total = total + shares[k].astype(F32)
    total = total.astype(BF16).astype(F32)
    for b in range(B):
        out[b] = total[STEPS * b : STEPS * (b + 1)].astype(BF16)


def call(kernel, out_shape, in_specs, name, scratch=(), cost=None, mib=12, out_specs=None):
    return pl.pallas_call(
        kernel,
        out_shape=out_shape,
        in_specs=in_specs,
        out_specs=jax.tree.map(lambda _: VMEM, out_shape) if out_specs is None else out_specs,
        scratch_shapes=scratch,
        cost_estimate=cost,
        compiler_params=pltpu.CompilerParams(vmem_limit_bytes=mib * 2**20),
        name=name,
    )


def hbm(x):
    return pltpu.with_memory_space_constraint(x, pltpu.HBM)


def vmem(x):
    return pltpu.with_memory_space_constraint(x, pltpu.VMEM)


def prefetch(x, name):
    return call(
        prefetch_kernel,
        pltpu.VMEM(x.shape, x.dtype),
        [HBM],
        name,
        [pltpu.SemaphoreType.DMA((8,))],
        out_specs=VMEM,
    )(hbm(x))


def swap(x, axes):
    return lax.all_to_all(x, axes, split_axis=0, concat_axis=0, tiled=True)


def shards(query, new_kv, kv_store, prefix_pages, fork_of, own_pages, lengths, o_weight):
    shape = jax.ShapeDtypeStruct
    store = kv_store.reshape(P_DEV, 2, PAGE, HD)
    request, q = call(
        request_kernel,
        [shape((POOL, 16, HD), BF16), shape((ROWS, HD), BF16)],
        [HBM] * 4 + [VMEM],
        "request",
        [
            pltpu.SMEM(prefix_pages.shape, I32),
            pltpu.SMEM(own_pages.shape, I32),
            pltpu.SMEM(fork_of.shape, I32),
            pltpu.SMEM(lengths.shape, I32),
            pltpu.SemaphoreType.DMA((4,)),
        ],
    )(hbm(prefix_pages), hbm(own_pages), hbm(fork_of), hbm(lengths), query)
    request = swap(request, NEAR + FAR)
    store = prefetch(store, "store_ahead")
    pages = call(
        gather_kernel,
        pltpu.HBM((SOURCES, CHUNK, HD), BF16),
        [VMEM, VMEM],
        "gather_pages",
        [
            pltpu.VMEM((SOURCES, CHUNK, HD), BF16),
            pltpu.VMEM((POOL, HD), I32),
            pltpu.SMEM((POOL, HD), I32),
            pltpu.SemaphoreType.DMA(()),
            pltpu.SemaphoreType.DMA((SOURCES,)),
        ],
        out_specs=HBM,
    )(request, vmem(store))
    pages = swap(pages, NEAR)
    fresh_k = new_kv[:, :, 0, 0].reshape(B * STEPS, HD)
    fresh_v = new_kv[:, :, 1, 0].reshape(B * STEPS, HD)
    local = call(
        local_kernel,
        [shape((ROWS, HD), F32)] * 3,
        [SMEM, SMEM, VMEM, VMEM, VMEM, VMEM],
        "resident",
        [pltpu.VMEM(((B - MIG) * NOWN * PAGE, HD), BF16)] * 2,
        pl.CostEstimate(flops=10**8, bytes_accessed=3 * 2**20, transcendentals=10**5),
    )(own_pages, lengths, q, fresh_k, fresh_v, store)
    parts = call(partial_kernel, shape((MEMBERS * RES, HD), BF16), [VMEM], "partials")(vmem(pages))
    parts = swap(parts.reshape(MEMBERS, RES, HD), FAR).reshape(MEMBERS * RES, HD)
    width = o_weight.shape[1] // TPN
    shares = call(
        finish_kernel,
        shape((TPN, 16, width), BF16),
        [VMEM] * 4 + [HBM],
        "finish",
        [pltpu.VMEM(o_weight.shape, BF16), pltpu.VMEM((ROWS, HD), F32), pltpu.SemaphoreType.DMA((GROUP,))],
    )(parts, *local, hbm(o_weight))
    shares = swap(shares, ("x", "c"))
    return call(total_kernel, shape((B, STEPS, width), BF16), [VMEM], "total")(shares)


def solution(mesh):
    fine = Mesh(mesh.devices.reshape(ZH, ZM, ZL, YN, XN, CN), POOL_AXES + ("x", "c"))
    pool, tp = POOL_AXES, ("x", "c")
    return jax.shard_map(
        shards,
        mesh=fine,
        in_specs=(
            P(pool, None, tp, None),
            P(pool, None, None, tp, None),
            P(pool, None, tp, None, None),
            P(pool, None),
            P(pool),
            P(pool, None),
            P(pool),
            P(tp, None),
        ),
        out_specs=P(pool, None, tp),
        check_vma=False,
    )
```

```python
import math

import jax
import jax.numpy as jnp
from jax import lax
from jax.experimental import pallas as pl
from jax.experimental.pallas import tpu as pltpu
from jax.sharding import Mesh
from jax.sharding import PartitionSpec as P

F32 = jnp.float32
BF16 = jnp.bfloat16
I32 = jnp.int32

HD = 128
PAGE = 16
NPRE = 8
NOWN = 24
ROOTS = 4
B = 8
MIG = 4
STEPS = 2
GROUP = 4
ROWS = B * STEPS * GROUP
SLOTS = 4
P_DEV = 256
NEG = -(2.0**100)
SCALE = 1.0 / math.sqrt(HD)
ZN, YN, XN, CN = 16, 4, 4, 2
ZH, ZM, ZL = 4, 2, 2
PARTS = 1
POOL_AXES = ("zh", "zm", "zl", "y")
NEAR = ("zl", "y")
FAR = ("zh", "zm")
SOURCES = ZL * YN
MEMBERS = ZH * ZM
POOL = ZN * YN
TPN = XN * CN
PREFIX_IDS = ROOTS * NPRE
KEYS = SLOTS * PAGE
PAGE_ROWS = MEMBERS * KEYS
QROWS = STEPS * GROUP
TAIL = MEMBERS * QROWS + 16
CHUNK = 2 * PAGE_ROWS + TAIL
RES = ROWS + 8

VMEM = pl.BlockSpec(memory_space=pltpu.VMEM)
SMEM = pl.BlockSpec(memory_space=pltpu.SMEM)
HBM = pl.BlockSpec(memory_space=pltpu.HBM)
ANY = pl.BlockSpec(memory_space=pl.ANY)
NT = (((1,), (1,)), ((), ()))
NN = (((1,), (0,)), ((), ()))


def iota(shape, dim):
    return lax.broadcasted_iota(I32, shape, dim)


def dot(a, b, dims=NN):
    return lax.dot_general(a, b, dims, preferred_element_type=F32)


def request_kernel(
    prefix_hbm, own_hbm, fork_hbm, length_hbm, query_hbm, req, prefix, own, fork, length, query, sems
):
    pairs = ((prefix_hbm, prefix), (own_hbm, own), (fork_hbm, fork), (length_hbm, length), (query_hbm, query))
    copies = [pltpu.make_async_copy(a, b, sems.at[n]) for n, (a, b) in enumerate(pairs)]
    for copy in copies:
        copy.start()
    for copy in copies:
        copy.wait()
    lane = iota((8, HD), 1)
    row = iota((8, HD), 0)
    ids = jnp.zeros((8, HD), I32)
    for r in range(ROOTS):
        for c in range(NPRE):
            ids = jnp.where(lane == r * NPRE + c, prefix[r, c], ids)
    for r in range(MIG):
        for c in range(NOWN):
            ids = jnp.where(lane == PREFIX_IDS + r * NOWN + c, own[r, c], ids)
    forks = jnp.zeros((8, HD), I32)
    lens = jnp.zeros((8, HD), I32)
    for b in range(B):
        forks = jnp.where(row == b, fork[b], forks)
        lens = jnp.where(row == b, length[b], lens)
    is_prefix = lane < PREFIX_IDS
    moved = jnp.maximum(lane - PREFIX_IDS, 0)
    chunk = jnp.where(is_prefix, lane % NPRE, NPRE + moved % NOWN)
    wanted = (is_prefix & (forks == lane // NPRE)) | (~is_prefix & (row == moved // NOWN))
    tokens = jnp.where(wanted, jnp.clip(lens - PAGE * chunk, 0, PAGE), 0)
    place = jnp.where(row == 0, ids % P_DEV, 0)
    table = jnp.concatenate([tokens, place], 0).astype(F32).astype(BF16)
    holder = ids // P_DEV
    plane, row_y = holder // YN, holder % YN
    holder = ((plane % ZL) * YN + row_y) * MEMBERS + plane // ZL
    member = jnp.broadcast_to(holder[0:1], (POOL, HD)) == iota((POOL, HD), 0)
    earlier = (iota((HD, HD), 0) < iota((HD, HD), 1)).astype(F32).astype(BF16)
    rank = dot(member.astype(F32).astype(BF16), earlier)
    out = jnp.zeros((POOL, HD), F32)
    for s in range(SLOTS):
        chosen = jnp.where(member & (rank == float(s)), 1.0, 0.0).astype(BF16)
        parts = [table if k == s else jnp.zeros((16, HD), BF16) for k in range(HD // 16)]
        out = out + dot(chosen, jnp.concatenate(parts, 0), NT)
    for b in range(B):
        for n in range(QROWS // 2):
            rows = query[b, n]
            for m in range(MEMBERS):
                req[b * MEMBERS + m, n] = rows
    for d in range(POOL):
        req[d, QROWS // 2] = jnp.broadcast_to(out[d : d + 1], (2, HD)).astype(BF16)


def prefetch_kernel(source, out, sems):
    part = out.shape[0] // sems.shape[0]
    copies = [
        pltpu.make_async_copy(source.at[pl.ds(n * part, part)], out.at[pl.ds(n * part, part)], sems.at[n])
        for n in range(sems.shape[0])
    ]
    for copy in copies:
        copy.start()
    for copy in copies:
        copy.wait()


def gather_kernel(req, store, out, stage, wanted, places, place_sem, sems):
    row = iota((MEMBERS, HD), 0)
    tails = []
    for c in range(SOURCES):
        asked = jnp.zeros((MEMBERS, HD), F32)
        rows = []
        for n in range(MEMBERS):
            block = req[c * MEMBERS + n].astype(F32)
            rows += [block[k] for k in range(QROWS // 2)]
            asked = jnp.where(row == n, block[QROWS // 2, 0:1], asked)
        wanted[pl.ds(c * MEMBERS, MEMBERS), :] = asked.astype(I32)
        tails.append(rows + [asked, jnp.zeros((16 - MEMBERS, HD), F32)])
    copy = pltpu.make_async_copy(wanted, places, place_sem)
    copy.start()
    for c in range(SOURCES):
        stage[c, pl.ds(2 * PAGE_ROWS, TAIL), :] = jnp.concatenate(tails[c], 0).astype(BF16)
    copy.wait()
    copies = []
    for c in range(SOURCES):
        for n in range(MEMBERS):
            for s in range(SLOTS):
                at = places[c * MEMBERS + n, 16 * s + 8]
                start = n * KEYS + s * PAGE
                stage[c, pl.ds(start, PAGE), :] = store[at, 0]
                stage[c, pl.ds(PAGE_ROWS + start, PAGE), :] = store[at, 1]
        copy = pltpu.make_async_copy(stage.at[c], out.at[c], sems.at[c])
        copy.start()
        copies.append(copy)
    for copy in copies:
        copy.wait()


def local_kernel(own, length, q, fresh_k, fresh_v, store, sums, top, total, keys, values):
    branches = B - MIG
    span = NOWN * PAGE
    for b in range(branches):
        for p in range(NOWN):
            at = own[MIG + b, p] % P_DEV
            start = b * span + p * PAGE
            keys[pl.ds(start, PAGE), :] = store[at, 0]
            values[pl.ds(start, PAGE), :] = store[at, 1]
    rows = q[...]
    branch_of = iota((ROWS, 1), 0) // QROWS
    step_of = iota((ROWS, 1), 0) // GROUP % STEPS
    lane16 = iota((ROWS, 16), 1)
    score = dot(rows, fresh_k[...], NT) * SCALE
    ok = (lane16 // STEPS == branch_of) & (lane16 % STEPS <= step_of)
    blocks = [(jnp.where(ok, score, NEG), ok, fresh_v[...])]
    position = iota((ROWS, span), 1) + NPRE * PAGE
    for b in range(branches):
        score = dot(rows, keys[pl.ds(b * span, span), :], NT) * SCALE
        ok = (branch_of == MIG + b) & (position < length[MIG + b])
        blocks.append((jnp.where(ok, score, NEG), ok, values[pl.ds(b * span, span), :]))
    best = jnp.max(blocks[0][0], 1, keepdims=True)
    for score, _, _ in blocks[1:]:
        best = jnp.maximum(best, jnp.max(score, 1, keepdims=True))
    acc = jnp.zeros((ROWS, HD), F32)
    count = jnp.zeros((ROWS, 1), F32)
    for score, ok, value in blocks:
        weight = jnp.where(ok, jnp.exp(score - best), 0.0).astype(BF16)
        count = count + jnp.sum(weight.astype(F32), 1, keepdims=True)
        acc = acc + dot(weight, value)
    sums[...] = acc
    top[...] = jnp.broadcast_to(best, (ROWS, HD))
    total[...] = jnp.broadcast_to(count, (ROWS, HD))


def partial_kernel(pages, out):
    per = MEMBERS // PARTS
    pick = iota((B, HD), 1) % 16 == iota((B, HD), 0)
    stacks = []
    asking = []
    for k in range(SOURCES):
        tail = pages[k, pl.ds(2 * PAGE_ROWS, TAIL), :].astype(F32)
        asking.append(tail)
        tile = tail[MEMBERS * QROWS : MEMBERS * QROWS + MEMBERS]
        rows = [jnp.where(pick, jnp.broadcast_to(tile[n : n + 1], (B, HD)), 0.0) for n in range(MEMBERS)]
        stacks.append(jnp.concatenate(rows, 0).astype(BF16))
    pairs = [jnp.concatenate(stacks[k : k + 2], 1) for k in range(0, SOURCES, 2)]
    shape = (2 * HD, 2 * KEYS)
    expand = iota(shape, 0) // HD * KEYS + (iota(shape, 0) % HD) // 16 * PAGE == iota(shape, 1) // PAGE * PAGE
    expand = expand & (iota(shape, 0) % HD < KEYS)
    tokens = dot(jnp.concatenate(pairs, 0), expand.astype(F32).astype(BF16))
    number = (iota((tokens.shape[0], 2 * KEYS), 1) % PAGE).astype(F32)
    mask = jnp.where(number < tokens, 0.0, NEG)
    column = iota((ROWS, HD), 1)
    row = iota((8, HD), 0)
    for part in range(PARTS):
        members = range(part * per, (part + 1) * per)
        scores = []
        for z in members:
            keys = jnp.concatenate([pages[k, pl.ds(z * KEYS, KEYS), :] for k in range(SOURCES)], 0)
            queries = jnp.concatenate([tail[z * QROWS : (z + 1) * QROWS] for tail in asking], 0).astype(BF16)
            scores.append(dot(queries, keys, NT))
        stats = jnp.zeros((ROWS, HD), F32)
        weights = []
        for n, z in enumerate(members):
            rows = range(z * B, SOURCES // 2 * MEMBERS * B, MEMBERS * B)
            bias = jnp.concatenate([mask[r : r + B] for r in rows], 1)
            bias = jnp.concatenate([jnp.broadcast_to(bias[b : b + 1], (QROWS, bias.shape[1])) for b in range(B)], 0)
            score = jnp.where(bias < 0.0, NEG, scores[n] * SCALE)
            best = jnp.max(score, 1, keepdims=True).astype(BF16).astype(F32)
            weight = jnp.where(bias < 0.0, 0.0, jnp.exp(score - best)).astype(BF16)
            count = jnp.sum(weight.astype(F32), 1, keepdims=True)
            weights.append(weight)
            stats = jnp.where(column == n, best, jnp.where(column == 8 + n, count, stats))
        turned = jnp.transpose(stats)[0:16]
        turned = jnp.concatenate([turned, jnp.zeros((16, HD - ROWS), F32)], 1)
        tops, counts = turned[0:8], turned[8:16]
        high = counts.astype(BF16).astype(F32)
        low = counts - high
        rows = []
        for n, z in enumerate(members):
            values = jnp.concatenate([pages[k, pl.ds(PAGE_ROWS + z * KEYS, KEYS), :] for k in range(SOURCES)], 0)
            tile = jnp.where(row == 1, high[n : n + 1], jnp.where(row == 2, low[n : n + 1], 0.0))
            rows += [dot(weights[n], values), jnp.where(row == 0, tops[n : n + 1], tile)]
        out[pl.ds(part * per * RES, per * RES), :] = jnp.concatenate(rows, 0).astype(BF16)


def finish_kernel(parts, sums, top, total, weight_hbm, out, weight, rows, sems):
    copies = [
        pltpu.make_async_copy(weight_hbm.at[pl.ds(g * HD, HD), :], weight.at[pl.ds(g * HD, HD), :], sems.at[g])
        for g in range(GROUP)
    ]
    for copy in copies:
        copy.start()
    row = iota((8, HD), 0)
    tops = jnp.full((8, HD), NEG, F32)
    counts = jnp.zeros((8, HD), F32)
    received = []
    for z in range(0, MEMBERS, 2):
        pair = parts[pl.ds(z * RES, 2 * RES), :].astype(F32)
        received += [pair[0:RES], pair[RES : 2 * RES]]
    for z in range(MEMBERS):
        tile = received[z][ROWS:RES]
        tops = jnp.where(row == z, tile[0:1], tops)
        counts = jnp.where(row == z, tile[1:2] + tile[2:3], counts)
    tops = jnp.concatenate([tops, jnp.full((HD - 8, HD), NEG, F32)], 0)
    counts = jnp.concatenate([counts, jnp.zeros((HD - 8, HD), F32)], 0)
    tops = jnp.transpose(tops)[0:ROWS]
    counts = jnp.transpose(counts)[0:ROWS]
    own_top = top[...]
    best = jnp.maximum(jnp.max(tops, 1, keepdims=True), own_top)
    factor = jnp.exp(tops - best)
    own_factor = jnp.exp(own_top - best)
    denominator = jnp.sum(factor * counts, 1, keepdims=True) + own_factor * total[...]
    numerator = own_factor * sums[...]
    for z in range(MEMBERS):
        numerator = numerator + factor[:, z : z + 1] * received[z][0:ROWS]
    rows[...] = numerator / denominator
    result = jnp.zeros((16, weight.shape[1]), F32)
    for g in range(GROUP):
        copies[g].wait()
        attended = rows[pl.ds(g, 16, stride=GROUP), :].astype(BF16)
        result = result + dot(attended, weight[pl.ds(g * HD, HD), :])
    result = result.astype(BF16).astype(F32)
    width = out.shape[2]
    for k in range(TPN):
        out[k] = result[:, k * width : (k + 1) * width].astype(BF16)


def total_kernel(shares, out):
    total = shares[0].astype(F32)
    for k in range(1, TPN):
        total = total + shares[k].astype(F32)
    total = total.astype(BF16).astype(F32)
    for b in range(B):
        out[b] = total[STEPS * b : STEPS * (b + 1)].astype(BF16)


def call(kernel, out_shape, in_specs, name, scratch=(), cost=None, mib=12, out_specs=None):
    return pl.pallas_call(
        kernel,
        out_shape=out_shape,
        in_specs=in_specs,
        out_specs=jax.tree.map(lambda _: VMEM, out_shape) if out_specs is None else out_specs,
        scratch_shapes=scratch,
        cost_estimate=cost,
        compiler_params=pltpu.CompilerParams(vmem_limit_bytes=mib * 2**20),
        name=name,
    )


def hbm(x):
    return pltpu.with_memory_space_constraint(x, pltpu.HBM)


def vmem(x):
    return pltpu.with_memory_space_constraint(x, pltpu.VMEM)


def prefetch(x, name):
    return call(
        prefetch_kernel,
        pltpu.VMEM(x.shape, x.dtype),
        [HBM],
        name,
        [pltpu.SemaphoreType.DMA((8,))],
        out_specs=VMEM,
    )(hbm(x))


def swap(x, axes):
    return lax.all_to_all(x, axes, split_axis=0, concat_axis=0, tiled=True)


def shards(query, new_kv, kv_store, prefix_pages, fork_of, own_pages, lengths, o_weight):
    shape = jax.ShapeDtypeStruct
    store = kv_store.reshape(P_DEV, 2, PAGE, HD)
    pairs = query.reshape(B, QROWS // 2, 2, HD)
    request = call(
        request_kernel,
        shape((POOL, QROWS // 2 + 1, 2, HD), BF16),
        [HBM] * 5,
        "request",
        [
            pltpu.SMEM(prefix_pages.shape, I32),
            pltpu.SMEM(own_pages.shape, I32),
            pltpu.SMEM(fork_of.shape, I32),
            pltpu.SMEM(lengths.shape, I32),
            pltpu.VMEM(pairs.shape, BF16),
            pltpu.SemaphoreType.DMA((5,)),
        ],
    )(hbm(prefix_pages), hbm(own_pages), hbm(fork_of), hbm(lengths), hbm(pairs))
    request = swap(request, NEAR + FAR)
    store = prefetch(store, "store_ahead")
    pages = call(
        gather_kernel,
        pltpu.HBM((SOURCES, CHUNK, HD), BF16),
        [VMEM, VMEM],
        "gather_pages",
        [
            pltpu.VMEM((SOURCES, CHUNK, HD), BF16),
            pltpu.VMEM((POOL, HD), I32),
            pltpu.SMEM((POOL, HD), I32),
            pltpu.SemaphoreType.DMA(()),
            pltpu.SemaphoreType.DMA((SOURCES,)),
        ],
        out_specs=HBM,
    )(request, vmem(store))
    pages = swap(pages, NEAR)
    q = query.reshape(ROWS, HD)
    fresh_k = new_kv[:, :, 0, 0].reshape(B * STEPS, HD)
    fresh_v = new_kv[:, :, 1, 0].reshape(B * STEPS, HD)
    local = call(
        local_kernel,
        [shape((ROWS, HD), F32)] * 3,
        [SMEM, SMEM, VMEM, VMEM, VMEM, VMEM],
        "resident",
        [pltpu.VMEM(((B - MIG) * NOWN * PAGE, HD), BF16)] * 2,
        pl.CostEstimate(flops=10**8, bytes_accessed=3 * 2**20, transcendentals=10**5),
    )(own_pages, lengths, q, fresh_k, fresh_v, store)
    parts = call(partial_kernel, shape((MEMBERS * RES, HD), BF16), [VMEM], "partials")(vmem(pages))
    parts = swap(parts.reshape(MEMBERS, RES, HD), FAR).reshape(MEMBERS * RES, HD)
    width = o_weight.shape[1] // TPN
    shares = call(
        finish_kernel,
        shape((TPN, 16, width), BF16),
        [VMEM] * 4 + [HBM],
        "finish",
        [pltpu.VMEM(o_weight.shape, BF16), pltpu.VMEM((ROWS, HD), F32), pltpu.SemaphoreType.DMA((GROUP,))],
    )(parts, *local, hbm(o_weight))
    shares = swap(shares, ("x", "c"))
    return call(total_kernel, shape((B, STEPS, width), BF16), [VMEM], "total")(shares)


def solution(mesh):
    fine = Mesh(mesh.devices.reshape(ZH, ZM, ZL, YN, XN, CN), POOL_AXES + ("x", "c"))
    pool, tp = POOL_AXES, ("x", "c")
    return jax.shard_map(
        shards,
        mesh=fine,
        in_specs=(
            P(pool, None, tp, None),
            P(pool, None, None, tp, None),
            P(pool, None, tp, None, None),
            P(pool, None),
            P(pool),
            P(pool, None),
            P(pool),
            P(tp, None),
        ),
        out_specs=P(pool, None, tp),
        check_vma=False,
    )
```

```python
import math

import jax
import jax.numpy as jnp
from jax import lax
from jax.experimental import pallas as pl
from jax.experimental.pallas import tpu as pltpu
from jax.sharding import Mesh
from jax.sharding import PartitionSpec as P

F32 = jnp.float32
BF16 = jnp.bfloat16
I32 = jnp.int32

HD = 128
PAGE = 16
NPRE = 8
NOWN = 24
ROOTS = 4
B = 8
MIG = 4
STEPS = 2
GROUP = 4
ROWS = B * STEPS * GROUP
SLOTS = 4
P_DEV = 256
NEG = -(2.0**100)
SCALE = 1.0 / math.sqrt(HD)
ZN, YN, XN, CN = 16, 4, 4, 2
ZH, ZM, ZL = 4, 2, 2
PARTS = 1
POOL_AXES = ("zh", "zm", "zl", "y")
NEAR = ("zl", "y")
FAR = ("zh", "zm")
SOURCES = ZL * YN
MEMBERS = ZH * ZM
POOL = ZN * YN
TPN = XN * CN
PREFIX_IDS = ROOTS * NPRE
KEYS = SLOTS * PAGE
PAGE_ROWS = MEMBERS * KEYS
QROWS = STEPS * GROUP
TAIL = MEMBERS * QROWS + 16
CHUNK = 2 * PAGE_ROWS + TAIL
RES = ROWS + 8

VMEM = pl.BlockSpec(memory_space=pltpu.VMEM)
SMEM = pl.BlockSpec(memory_space=pltpu.SMEM)
HBM = pl.BlockSpec(memory_space=pltpu.HBM)
ANY = pl.BlockSpec(memory_space=pl.ANY)
NT = (((1,), (1,)), ((), ()))
NN = (((1,), (0,)), ((), ()))


def iota(shape, dim):
    return lax.broadcasted_iota(I32, shape, dim)


def dot(a, b, dims=NN):
    return lax.dot_general(a, b, dims, preferred_element_type=F32)


def request_kernel(
    prefix_hbm, own_hbm, fork_hbm, length_hbm, query_hbm, req, prefix, own, fork, length, query, sems
):
    pairs = ((prefix_hbm, prefix), (own_hbm, own), (fork_hbm, fork), (length_hbm, length), (query_hbm, query))
    copies = [pltpu.make_async_copy(a, b, sems.at[n]) for n, (a, b) in enumerate(pairs)]
    for copy in copies:
        copy.start()
    for copy in copies:
        copy.wait()
    for b in range(B):
        for n in range(QROWS // 2):
            rows = query[b, n]
            for m in range(MEMBERS):
                req[b * MEMBERS + m, n] = rows
    lane = iota((8, HD), 1)
    row = iota((8, HD), 0)
    ids = jnp.zeros((8, HD), I32)
    for r in range(ROOTS):
        for c in range(NPRE):
            ids = jnp.where(lane == r * NPRE + c, prefix[r, c], ids)
    for r in range(MIG):
        for c in range(NOWN):
            ids = jnp.where(lane == PREFIX_IDS + r * NOWN + c, own[r, c], ids)
    forks = jnp.zeros((8, HD), I32)
    lens = jnp.zeros((8, HD), I32)
    for b in range(B):
        forks = jnp.where(row == b, fork[b], forks)
        lens = jnp.where(row == b, length[b], lens)
    is_prefix = lane < PREFIX_IDS
    moved = jnp.maximum(lane - PREFIX_IDS, 0)
    chunk = jnp.where(is_prefix, lane % NPRE, NPRE + moved % NOWN)
    wanted = (is_prefix & (forks == lane // NPRE)) | (~is_prefix & (row == moved // NOWN))
    tokens = jnp.where(wanted, jnp.clip(lens - PAGE * chunk, 0, PAGE), 0)
    place = jnp.where(row == 0, ids % P_DEV, 0)
    table = jnp.concatenate([tokens, place], 0).astype(F32).astype(BF16)
    holder = ids // P_DEV
    plane, row_y = holder // YN, holder % YN
    holder = ((plane % ZL) * YN + row_y) * MEMBERS + plane // ZL
    member = jnp.broadcast_to(holder[0:1], (POOL, HD)) == iota((POOL, HD), 0)
    earlier = (iota((HD, HD), 0) < iota((HD, HD), 1)).astype(F32).astype(BF16)
    rank = dot(member.astype(F32).astype(BF16), earlier)
    out = jnp.zeros((POOL, HD), F32)
    for s in range(SLOTS):
        chosen = jnp.where(member & (rank == float(s)), 1.0, 0.0).astype(BF16)
        parts = [table if k == s else jnp.zeros((16, HD), BF16) for k in range(HD // 16)]
        out = out + dot(chosen, jnp.concatenate(parts, 0), NT)
    for d in range(POOL):
        req[d, QROWS // 2] = jnp.broadcast_to(out[d : d + 1], (2, HD)).astype(BF16)


def prefetch_kernel(source, out, sems):
    part = out.shape[0] // sems.shape[0]
    copies = [
        pltpu.make_async_copy(source.at[pl.ds(n * part, part)], out.at[pl.ds(n * part, part)], sems.at[n])
        for n in range(sems.shape[0])
    ]
    for copy in copies:
        copy.start()
    for copy in copies:
        copy.wait()


def gather_kernel(req, store, out, wanted, places, place_sem):
    row = iota((MEMBERS, HD), 0)
    tails = []
    for c in range(SOURCES):
        asked = jnp.zeros((MEMBERS, HD), F32)
        rows = []
        for n in range(MEMBERS):
            block = req[c * MEMBERS + n].astype(F32)
            rows += [block[k] for k in range(QROWS // 2)]
            asked = jnp.where(row == n, block[QROWS // 2, 0:1], asked)
        wanted[pl.ds(c * MEMBERS, MEMBERS), :] = asked.astype(I32)
        tails.append(rows + [asked, jnp.zeros((16 - MEMBERS, HD), F32)])
    copy = pltpu.make_async_copy(wanted, places, place_sem)
    copy.start()
    for c in range(SOURCES):
        out[c, pl.ds(2 * PAGE_ROWS, TAIL), :] = jnp.concatenate(tails[c], 0).astype(BF16)
    copy.wait()
    for c in range(SOURCES):
        for n in range(MEMBERS):
            for s in range(SLOTS):
                at = places[c * MEMBERS + n, 16 * s + 8]
                start = n * KEYS + s * PAGE
                out[c, pl.ds(start, PAGE), :] = store[at, 0]
                out[c, pl.ds(PAGE_ROWS + start, PAGE), :] = store[at, 1]


def local_kernel(own, length, q, fresh_k, fresh_v, store, sums, top, total, keys, values):
    branches = B - MIG
    span = NOWN * PAGE
    for b in range(branches):
        for p in range(NOWN):
            at = own[MIG + b, p] % P_DEV
            start = b * span + p * PAGE
            keys[pl.ds(start, PAGE), :] = store[at, 0]
            values[pl.ds(start, PAGE), :] = store[at, 1]
    rows = q[...]
    branch_of = iota((ROWS, 1), 0) // QROWS
    step_of = iota((ROWS, 1), 0) // GROUP % STEPS
    lane16 = iota((ROWS, 16), 1)
    score = dot(rows, fresh_k[...], NT) * SCALE
    ok = (lane16 // STEPS == branch_of) & (lane16 % STEPS <= step_of)
    blocks = [(jnp.where(ok, score, NEG), ok, fresh_v[...])]
    position = iota((ROWS, span), 1) + NPRE * PAGE
    for b in range(branches):
        score = dot(rows, keys[pl.ds(b * span, span), :], NT) * SCALE
        ok = (branch_of == MIG + b) & (position < length[MIG + b])
        blocks.append((jnp.where(ok, score, NEG), ok, values[pl.ds(b * span, span), :]))
    best = jnp.max(blocks[0][0], 1, keepdims=True)
    for score, _, _ in blocks[1:]:
        best = jnp.maximum(best, jnp.max(score, 1, keepdims=True))
    acc = jnp.zeros((ROWS, HD), F32)
    count = jnp.zeros((ROWS, 1), F32)
    for score, ok, value in blocks:
        weight = jnp.where(ok, jnp.exp(score - best), 0.0).astype(BF16)
        count = count + jnp.sum(weight.astype(F32), 1, keepdims=True)
        acc = acc + dot(weight, value)
    sums[...] = acc
    top[...] = jnp.broadcast_to(best, (ROWS, HD))
    total[...] = jnp.broadcast_to(count, (ROWS, HD))


def partial_kernel(pages, out):
    per = MEMBERS // PARTS
    pick = iota((B, HD), 1) % 16 == iota((B, HD), 0)
    stacks = []
    asking = []
    for k in range(SOURCES):
        tail = pages[k, pl.ds(2 * PAGE_ROWS, TAIL), :].astype(F32)
        asking.append(tail)
        tile = tail[MEMBERS * QROWS : MEMBERS * QROWS + MEMBERS]
        rows = [jnp.where(pick, jnp.broadcast_to(tile[n : n + 1], (B, HD)), 0.0) for n in range(MEMBERS)]
        stacks.append(jnp.concatenate(rows, 0).astype(BF16))
    pairs = [jnp.concatenate(stacks[k : k + 2], 1) for k in range(0, SOURCES, 2)]
    shape = (2 * HD, 2 * KEYS)
    expand = iota(shape, 0) // HD * KEYS + (iota(shape, 0) % HD) // 16 * PAGE == iota(shape, 1) // PAGE * PAGE
    expand = expand & (iota(shape, 0) % HD < KEYS)
    tokens = dot(jnp.concatenate(pairs, 0), expand.astype(F32).astype(BF16))
    number = (iota((tokens.shape[0], 2 * KEYS), 1) % PAGE).astype(F32)
    mask = jnp.where(number < tokens, 0.0, NEG)
    column = iota((ROWS, HD), 1)
    row = iota((8, HD), 0)
    for part in range(PARTS):
        members = range(part * per, (part + 1) * per)
        scores = []
        for z in members:
            keys = jnp.concatenate([pages[k, pl.ds(z * KEYS, KEYS), :] for k in range(SOURCES)], 0)
            queries = jnp.concatenate([tail[z * QROWS : (z + 1) * QROWS] for tail in asking], 0).astype(BF16)
            scores.append(dot(queries, keys, NT))
        stats = jnp.zeros((ROWS, HD), F32)
        weights = []
        for n, z in enumerate(members):
            rows = range(z * B, SOURCES // 2 * MEMBERS * B, MEMBERS * B)
            bias = jnp.concatenate([mask[r : r + B] for r in rows], 1)
            bias = jnp.concatenate([jnp.broadcast_to(bias[b : b + 1], (QROWS, bias.shape[1])) for b in range(B)], 0)
            score = jnp.where(bias < 0.0, NEG, scores[n] * SCALE)
            best = jnp.max(score, 1, keepdims=True).astype(BF16).astype(F32)
            weight = jnp.where(bias < 0.0, 0.0, jnp.exp(score - best)).astype(BF16)
            count = jnp.sum(weight.astype(F32), 1, keepdims=True)
            weights.append(weight)
            stats = jnp.where(column == n, best, jnp.where(column == 8 + n, count, stats))
        turned = jnp.transpose(stats)[0:16]
        turned = jnp.concatenate([turned, jnp.zeros((16, HD - ROWS), F32)], 1)
        tops, counts = turned[0:8], turned[8:16]
        high = counts.astype(BF16).astype(F32)
        low = counts - high
        rows = []
        for n, z in enumerate(members):
            values = jnp.concatenate([pages[k, pl.ds(PAGE_ROWS + z * KEYS, KEYS), :] for k in range(SOURCES)], 0)
            tile = jnp.where(row == 1, high[n : n + 1], jnp.where(row == 2, low[n : n + 1], 0.0))
            rows += [dot(weights[n], values), jnp.where(row == 0, tops[n : n + 1], tile)]
        out[pl.ds(part * per * RES, per * RES), :] = jnp.concatenate(rows, 0).astype(BF16)


def finish_kernel(parts, sums, top, total, weight_hbm, out, weight, rows, sems):
    copies = [
        pltpu.make_async_copy(weight_hbm.at[pl.ds(g * HD, HD), :], weight.at[pl.ds(g * HD, HD), :], sems.at[g])
        for g in range(GROUP)
    ]
    for copy in copies:
        copy.start()
    row = iota((8, HD), 0)
    tops = jnp.full((8, HD), NEG, F32)
    counts = jnp.zeros((8, HD), F32)
    received = []
    for z in range(0, MEMBERS, 2):
        pair = parts[pl.ds(z * RES, 2 * RES), :].astype(F32)
        received += [pair[0:RES], pair[RES : 2 * RES]]
    for z in range(MEMBERS):
        tile = received[z][ROWS:RES]
        tops = jnp.where(row == z, tile[0:1], tops)
        counts = jnp.where(row == z, tile[1:2] + tile[2:3], counts)
    tops = jnp.concatenate([tops, jnp.full((HD - 8, HD), NEG, F32)], 0)
    counts = jnp.concatenate([counts, jnp.zeros((HD - 8, HD), F32)], 0)
    tops = jnp.transpose(tops)[0:ROWS]
    counts = jnp.transpose(counts)[0:ROWS]
    own_top = top[...]
    best = jnp.maximum(jnp.max(tops, 1, keepdims=True), own_top)
    factor = jnp.exp(tops - best)
    own_factor = jnp.exp(own_top - best)
    denominator = jnp.sum(factor * counts, 1, keepdims=True) + own_factor * total[...]
    numerator = own_factor * sums[...]
    for z in range(MEMBERS):
        numerator = numerator + factor[:, z : z + 1] * received[z][0:ROWS]
    rows[...] = numerator / denominator
    result = jnp.zeros((16, weight.shape[1]), F32)
    for g in range(GROUP):
        copies[g].wait()
        attended = rows[pl.ds(g, 16, stride=GROUP), :].astype(BF16)
        result = result + dot(attended, weight[pl.ds(g * HD, HD), :])
    result = result.astype(BF16).astype(F32)
    width = out.shape[2]
    for k in range(TPN):
        out[k] = result[:, k * width : (k + 1) * width].astype(BF16)


def total_kernel(shares, out):
    total = shares[0].astype(F32)
    for k in range(1, TPN):
        total = total + shares[k].astype(F32)
    total = total.astype(BF16).astype(F32)
    for b in range(B):
        out[b] = total[STEPS * b : STEPS * (b + 1)].astype(BF16)


def call(kernel, out_shape, in_specs, name, scratch=(), cost=None, mib=12, out_specs=None):
    return pl.pallas_call(
        kernel,
        out_shape=out_shape,
        in_specs=in_specs,
        out_specs=jax.tree.map(lambda _: VMEM, out_shape) if out_specs is None else out_specs,
        scratch_shapes=scratch,
        cost_estimate=cost,
        compiler_params=pltpu.CompilerParams(vmem_limit_bytes=mib * 2**20),
        name=name,
    )


def hbm(x):
    return pltpu.with_memory_space_constraint(x, pltpu.HBM)


def vmem(x):
    return pltpu.with_memory_space_constraint(x, pltpu.VMEM)


def prefetch(x, name):
    return call(
        prefetch_kernel,
        pltpu.VMEM(x.shape, x.dtype),
        [HBM],
        name,
        [pltpu.SemaphoreType.DMA((8,))],
        out_specs=VMEM,
    )(hbm(x))


def swap(x, axes):
    return lax.all_to_all(x, axes, split_axis=0, concat_axis=0, tiled=True)


def shards(query, new_kv, kv_store, prefix_pages, fork_of, own_pages, lengths, o_weight):
    shape = jax.ShapeDtypeStruct
    store = kv_store.reshape(P_DEV, 2, PAGE, HD)
    pairs = query.reshape(B, QROWS // 2, 2, HD)
    request = call(
        request_kernel,
        shape((POOL, QROWS // 2 + 1, 2, HD), BF16),
        [HBM] * 5,
        "request",
        [
            pltpu.SMEM(prefix_pages.shape, I32),
            pltpu.SMEM(own_pages.shape, I32),
            pltpu.SMEM(fork_of.shape, I32),
            pltpu.SMEM(lengths.shape, I32),
            pltpu.VMEM(pairs.shape, BF16),
            pltpu.SemaphoreType.DMA((5,)),
        ],
    )(hbm(prefix_pages), hbm(own_pages), hbm(fork_of), hbm(lengths), hbm(pairs))
    request = swap(request, NEAR + FAR)
    store = prefetch(store, "store_ahead")
    pages = call(
        gather_kernel,
        pltpu.VMEM((SOURCES, CHUNK, HD), BF16),
        [VMEM, VMEM],
        "gather_pages",
        [pltpu.VMEM((POOL, HD), I32), pltpu.SMEM((POOL, HD), I32), pltpu.SemaphoreType.DMA(())],
        out_specs=VMEM,
    )(request, vmem(store))
    pages = swap(pages, NEAR)
    q = query.reshape(ROWS, HD)
    fresh_k = new_kv[:, :, 0, 0].reshape(B * STEPS, HD)
    fresh_v = new_kv[:, :, 1, 0].reshape(B * STEPS, HD)
    local = call(
        local_kernel,
        [shape((ROWS, HD), F32)] * 3,
        [SMEM, SMEM, VMEM, VMEM, VMEM, VMEM],
        "resident",
        [pltpu.VMEM(((B - MIG) * NOWN * PAGE, HD), BF16)] * 2,
        pl.CostEstimate(flops=10**8, bytes_accessed=3 * 2**20, transcendentals=10**5),
    )(own_pages, lengths, q, fresh_k, fresh_v, store)
    parts = call(partial_kernel, shape((MEMBERS * RES, HD), BF16), [VMEM], "partials")(vmem(pages))
    parts = swap(parts.reshape(MEMBERS, RES, HD), FAR).reshape(MEMBERS * RES, HD)
    width = o_weight.shape[1] // TPN
    shares = call(
        finish_kernel,
        shape((TPN, 16, width), BF16),
        [VMEM] * 4 + [HBM],
        "finish",
        [pltpu.VMEM(o_weight.shape, BF16), pltpu.VMEM((ROWS, HD), F32), pltpu.SemaphoreType.DMA((GROUP,))],
    )(parts, *local, hbm(o_weight))
    shares = swap(shares, ("x", "c"))
    return call(total_kernel, shape((B, STEPS, width), BF16), [VMEM], "total")(shares)


def solution(mesh):
    fine = Mesh(mesh.devices.reshape(ZH, ZM, ZL, YN, XN, CN), POOL_AXES + ("x", "c"))
    pool, tp = POOL_AXES, ("x", "c")
    return jax.shard_map(
        shards,
        mesh=fine,
        in_specs=(
            P(pool, None, tp, None),
            P(pool, None, None, tp, None),
            P(pool, None, tp, None, None),
            P(pool, None),
            P(pool),
            P(pool, None),
            P(pool),
            P(tp, None),
        ),
        out_specs=P(pool, None, tp),
        check_vma=False,
    )
```

```python
import math

import jax
import jax.numpy as jnp
from jax import lax
from jax.experimental import pallas as pl
from jax.experimental.pallas import tpu as pltpu
from jax.sharding import Mesh
from jax.sharding import PartitionSpec as P

F32 = jnp.float32
BF16 = jnp.bfloat16
I32 = jnp.int32

HD = 128
PAGE = 16
NPRE = 8
NOWN = 24
ROOTS = 4
B = 8
MIG = 4
STEPS = 2
GROUP = 4
ROWS = B * STEPS * GROUP
SLOTS = 4
P_DEV = 256
NEG = -(2.0**100)
SCALE = 1.0 / math.sqrt(HD)
ZN, YN, XN, CN = 16, 4, 4, 2
ZH, ZM, ZL = 4, 2, 2
PARTS = 1
POOL_AXES = ("zh", "zm", "zl", "y")
NEAR = ("zl", "y")
FAR = ("zm", "zh")
SOURCES = ZL * YN
MEMBERS = ZH * ZM
POOL = ZN * YN
TPN = XN * CN
PREFIX_IDS = ROOTS * NPRE
KEYS = SLOTS * PAGE
PAGE_ROWS = MEMBERS * KEYS
QROWS = STEPS * GROUP
TAIL = MEMBERS * QROWS + 16
CHUNK = 2 * PAGE_ROWS + TAIL
RES = ROWS + 8

VMEM = pl.BlockSpec(memory_space=pltpu.VMEM)
SMEM = pl.BlockSpec(memory_space=pltpu.SMEM)
HBM = pl.BlockSpec(memory_space=pltpu.HBM)
ANY = pl.BlockSpec(memory_space=pl.ANY)
NT = (((1,), (1,)), ((), ()))
NN = (((1,), (0,)), ((), ()))


def iota(shape, dim):
    return lax.broadcasted_iota(I32, shape, dim)


def dot(a, b, dims=NN):
    return lax.dot_general(a, b, dims, preferred_element_type=F32)


def request_kernel(
    prefix_hbm, own_hbm, fork_hbm, length_hbm, query_hbm, req, prefix, own, fork, length, query, sems
):
    pairs = ((prefix_hbm, prefix), (own_hbm, own), (fork_hbm, fork), (length_hbm, length), (query_hbm, query))
    copies = [pltpu.make_async_copy(a, b, sems.at[n]) for n, (a, b) in enumerate(pairs)]
    for copy in copies:
        copy.start()
    for copy in copies:
        copy.wait()
    for b in range(B):
        for n in range(QROWS // 2):
            rows = query[b, n]
            for m in range(MEMBERS):
                req[b * MEMBERS + m, n] = rows
    lane = iota((8, HD), 1)
    row = iota((8, HD), 0)
    ids = jnp.zeros((8, HD), I32)
    for r in range(ROOTS):
        for c in range(NPRE):
            ids = jnp.where(lane == r * NPRE + c, prefix[r, c], ids)
    for r in range(MIG):
        for c in range(NOWN):
            ids = jnp.where(lane == PREFIX_IDS + r * NOWN + c, own[r, c], ids)
    forks = jnp.zeros((8, HD), I32)
    lens = jnp.zeros((8, HD), I32)
    for b in range(B):
        forks = jnp.where(row == b, fork[b], forks)
        lens = jnp.where(row == b, length[b], lens)
    is_prefix = lane < PREFIX_IDS
    moved = jnp.maximum(lane - PREFIX_IDS, 0)
    chunk = jnp.where(is_prefix, lane % NPRE, NPRE + moved % NOWN)
    wanted = (is_prefix & (forks == lane // NPRE)) | (~is_prefix & (row == moved // NOWN))
    tokens = jnp.where(wanted, jnp.clip(lens - PAGE * chunk, 0, PAGE), 0)
    place = jnp.where(row == 0, ids % P_DEV, 0)
    table = jnp.concatenate([tokens, place], 0).astype(F32).astype(BF16)
    holder = ids // P_DEV
    plane, row_y = holder // YN, holder % YN
    member = plane // ZL % ZM * ZH + plane // (ZL * ZM)
    holder = ((plane % ZL) * YN + row_y) * MEMBERS + member
    member = jnp.broadcast_to(holder[0:1], (POOL, HD)) == iota((POOL, HD), 0)
    earlier = (iota((HD, HD), 0) < iota((HD, HD), 1)).astype(F32).astype(BF16)
    rank = dot(member.astype(F32).astype(BF16), earlier)
    out = jnp.zeros((POOL, HD), F32)
    for s in range(SLOTS):
        chosen = jnp.where(member & (rank == float(s)), 1.0, 0.0).astype(BF16)
        parts = [table if k == s else jnp.zeros((16, HD), BF16) for k in range(HD // 16)]
        out = out + dot(chosen, jnp.concatenate(parts, 0), NT)
    for d in range(POOL):
        req[d, QROWS // 2] = jnp.broadcast_to(out[d : d + 1], (2, HD)).astype(BF16)


def prefetch_kernel(source, out, sems):
    part = out.shape[0] // sems.shape[0]
    copies = [
        pltpu.make_async_copy(source.at[pl.ds(n * part, part)], out.at[pl.ds(n * part, part)], sems.at[n])
        for n in range(sems.shape[0])
    ]
    for copy in copies:
        copy.start()
    for copy in copies:
        copy.wait()


def gather_kernel(req, store, out, wanted, places, place_sem):
    row = iota((MEMBERS, HD), 0)
    tails = []
    for c in range(SOURCES):
        asked = jnp.zeros((MEMBERS, HD), F32)
        rows = []
        for n in range(MEMBERS):
            block = req[c * MEMBERS + n].astype(F32)
            rows += [block[k] for k in range(QROWS // 2)]
            asked = jnp.where(row == n, block[QROWS // 2, 0:1], asked)
        wanted[pl.ds(c * MEMBERS, MEMBERS), :] = asked.astype(I32)
        tails.append(rows + [asked, jnp.zeros((16 - MEMBERS, HD), F32)])
    copy = pltpu.make_async_copy(wanted, places, place_sem)
    copy.start()
    for c in range(SOURCES):
        out[c, pl.ds(2 * PAGE_ROWS, TAIL), :] = jnp.concatenate(tails[c], 0).astype(BF16)
    copy.wait()
    for c in range(SOURCES):
        for n in range(MEMBERS):
            for s in range(SLOTS):
                at = places[c * MEMBERS + n, 16 * s + 8]
                start = n * KEYS + s * PAGE
                out[c, pl.ds(start, PAGE), :] = store[at, 0]
                out[c, pl.ds(PAGE_ROWS + start, PAGE), :] = store[at, 1]


def local_kernel(own, length, q, fresh_k, fresh_v, store, sums, top, total, keys, values):
    branches = B - MIG
    span = NOWN * PAGE
    for b in range(branches):
        for p in range(NOWN):
            at = own[MIG + b, p] % P_DEV
            start = b * span + p * PAGE
            keys[pl.ds(start, PAGE), :] = store[at, 0]
            values[pl.ds(start, PAGE), :] = store[at, 1]
    rows = q[...]
    branch_of = iota((ROWS, 1), 0) // QROWS
    step_of = iota((ROWS, 1), 0) // GROUP % STEPS
    lane16 = iota((ROWS, 16), 1)
    score = dot(rows, fresh_k[...], NT) * SCALE
    ok = (lane16 // STEPS == branch_of) & (lane16 % STEPS <= step_of)
    blocks = [(jnp.where(ok, score, NEG), ok, fresh_v[...])]
    position = iota((ROWS, span), 1) + NPRE * PAGE
    for b in range(branches):
        score = dot(rows, keys[pl.ds(b * span, span), :], NT) * SCALE
        ok = (branch_of == MIG + b) & (position < length[MIG + b])
        blocks.append((jnp.where(ok, score, NEG), ok, values[pl.ds(b * span, span), :]))
    best = jnp.max(blocks[0][0], 1, keepdims=True)
    for score, _, _ in blocks[1:]:
        best = jnp.maximum(best, jnp.max(score, 1, keepdims=True))
    acc = jnp.zeros((ROWS, HD), F32)
    count = jnp.zeros((ROWS, 1), F32)
    for score, ok, value in blocks:
        weight = jnp.where(ok, jnp.exp(score - best), 0.0).astype(BF16)
        count = count + jnp.sum(weight.astype(F32), 1, keepdims=True)
        acc = acc + dot(weight, value)
    sums[...] = acc
    top[...] = jnp.broadcast_to(best, (ROWS, HD))
    total[...] = jnp.broadcast_to(count, (ROWS, HD))


def partial_kernel(pages, out):
    per = MEMBERS // PARTS
    pick = iota((B, HD), 1) % 16 == iota((B, HD), 0)
    stacks = []
    asking = []
    for k in range(SOURCES):
        tail = pages[k, pl.ds(2 * PAGE_ROWS, TAIL), :].astype(F32)
        asking.append(tail)
        tile = tail[MEMBERS * QROWS : MEMBERS * QROWS + MEMBERS]
        rows = [jnp.where(pick, jnp.broadcast_to(tile[n : n + 1], (B, HD)), 0.0) for n in range(MEMBERS)]
        stacks.append(jnp.concatenate(rows, 0).astype(BF16))
    pairs = [jnp.concatenate(stacks[k : k + 2], 1) for k in range(0, SOURCES, 2)]
    shape = (2 * HD, 2 * KEYS)
    expand = iota(shape, 0) // HD * KEYS + (iota(shape, 0) % HD) // 16 * PAGE == iota(shape, 1) // PAGE * PAGE
    expand = expand & (iota(shape, 0) % HD < KEYS)
    tokens = dot(jnp.concatenate(pairs, 0), expand.astype(F32).astype(BF16))
    number = (iota((tokens.shape[0], 2 * KEYS), 1) % PAGE).astype(F32)
    mask = jnp.where(number < tokens, 0.0, NEG)
    column = iota((ROWS, HD), 1)
    row = iota((8, HD), 0)
    for part in range(PARTS):
        members = range(part * per, (part + 1) * per)
        scores = []
        for z in members:
            keys = jnp.concatenate([pages[k, pl.ds(z * KEYS, KEYS), :] for k in range(SOURCES)], 0)
            queries = jnp.concatenate([tail[z * QROWS : (z + 1) * QROWS] for tail in asking], 0).astype(BF16)
            scores.append(dot(queries, keys, NT))
        stats = jnp.zeros((ROWS, HD), F32)
        weights = []
        for n, z in enumerate(members):
            rows = range(z * B, SOURCES // 2 * MEMBERS * B, MEMBERS * B)
            bias = jnp.concatenate([mask[r : r + B] for r in rows], 1)
            bias = jnp.concatenate([jnp.broadcast_to(bias[b : b + 1], (QROWS, bias.shape[1])) for b in range(B)], 0)
            score = jnp.where(bias < 0.0, NEG, scores[n] * SCALE)
            best = jnp.max(score, 1, keepdims=True).astype(BF16).astype(F32)
            weight = jnp.where(bias < 0.0, 0.0, jnp.exp(score - best)).astype(BF16)
            count = jnp.sum(weight.astype(F32), 1, keepdims=True)
            weights.append(weight)
            stats = jnp.where(column == n, best, jnp.where(column == 8 + n, count, stats))
        turned = jnp.transpose(stats)[0:16]
        turned = jnp.concatenate([turned, jnp.zeros((16, HD - ROWS), F32)], 1)
        tops, counts = turned[0:8], turned[8:16]
        high = counts.astype(BF16).astype(F32)
        low = counts - high
        rows = []
        for n, z in enumerate(members):
            values = jnp.concatenate([pages[k, pl.ds(PAGE_ROWS + z * KEYS, KEYS), :] for k in range(SOURCES)], 0)
            tile = jnp.where(row == 1, high[n : n + 1], jnp.where(row == 2, low[n : n + 1], 0.0))
            rows += [dot(weights[n], values), jnp.where(row == 0, tops[n : n + 1], tile)]
        out[pl.ds(part * per * RES, per * RES), :] = jnp.concatenate(rows, 0).astype(BF16)


def finish_kernel(parts, sums, top, total, weight_hbm, out, weight, rows, sems):
    copies = [
        pltpu.make_async_copy(weight_hbm.at[pl.ds(g * HD, HD), :], weight.at[pl.ds(g * HD, HD), :], sems.at[g])
        for g in range(GROUP)
    ]
    for copy in copies:
        copy.start()
    row = iota((8, HD), 0)
    tops = jnp.full((8, HD), NEG, F32)
    counts = jnp.zeros((8, HD), F32)
    received = []
    for z in range(0, MEMBERS, 2):
        pair = parts[pl.ds(z * RES, 2 * RES), :].astype(F32)
        received += [pair[0:RES], pair[RES : 2 * RES]]
    for z in range(MEMBERS):
        tile = received[z][ROWS:RES]
        tops = jnp.where(row == z, tile[0:1], tops)
        counts = jnp.where(row == z, tile[1:2] + tile[2:3], counts)
    tops = jnp.concatenate([tops, jnp.full((HD - 8, HD), NEG, F32)], 0)
    counts = jnp.concatenate([counts, jnp.zeros((HD - 8, HD), F32)], 0)
    tops = jnp.transpose(tops)[0:ROWS]
    counts = jnp.transpose(counts)[0:ROWS]
    own_top = top[...]
    best = jnp.maximum(jnp.max(tops, 1, keepdims=True), own_top)
    factor = jnp.exp(tops - best)
    own_factor = jnp.exp(own_top - best)
    denominator = jnp.sum(factor * counts, 1, keepdims=True) + own_factor * total[...]
    numerator = own_factor * sums[...]
    for z in range(MEMBERS):
        numerator = numerator + factor[:, z : z + 1] * received[z][0:ROWS]
    rows[...] = numerator / denominator
    result = jnp.zeros((16, weight.shape[1]), F32)
    for g in range(GROUP):
        copies[g].wait()
        attended = rows[pl.ds(g, 16, stride=GROUP), :].astype(BF16)
        result = result + dot(attended, weight[pl.ds(g * HD, HD), :])
    result = result.astype(BF16).astype(F32)
    width = out.shape[2]
    for k in range(TPN):
        out[k] = result[:, k * width : (k + 1) * width].astype(BF16)


def total_kernel(shares, out):
    total = shares[0].astype(F32)
    for k in range(1, TPN):
        total = total + shares[k].astype(F32)
    total = total.astype(BF16).astype(F32)
    for b in range(B):
        out[b] = total[STEPS * b : STEPS * (b + 1)].astype(BF16)


def call(kernel, out_shape, in_specs, name, scratch=(), cost=None, mib=12, out_specs=None):
    return pl.pallas_call(
        kernel,
        out_shape=out_shape,
        in_specs=in_specs,
        out_specs=jax.tree.map(lambda _: VMEM, out_shape) if out_specs is None else out_specs,
        scratch_shapes=scratch,
        cost_estimate=cost,
        compiler_params=pltpu.CompilerParams(vmem_limit_bytes=mib * 2**20),
        name=name,
    )


def hbm(x):
    return pltpu.with_memory_space_constraint(x, pltpu.HBM)


def vmem(x):
    return pltpu.with_memory_space_constraint(x, pltpu.VMEM)


def prefetch(x, name):
    return call(
        prefetch_kernel,
        pltpu.VMEM(x.shape, x.dtype),
        [HBM],
        name,
        [pltpu.SemaphoreType.DMA((8,))],
        out_specs=VMEM,
    )(hbm(x))


def swap(x, axes):
    return lax.all_to_all(x, axes, split_axis=0, concat_axis=0, tiled=True)


def shards(query, new_kv, kv_store, prefix_pages, fork_of, own_pages, lengths, o_weight):
    shape = jax.ShapeDtypeStruct
    store = kv_store.reshape(P_DEV, 2, PAGE, HD)
    pairs = query.reshape(B, QROWS // 2, 2, HD)
    request = call(
        request_kernel,
        shape((POOL, QROWS // 2 + 1, 2, HD), BF16),
        [HBM] * 5,
        "request",
        [
            pltpu.SMEM(prefix_pages.shape, I32),
            pltpu.SMEM(own_pages.shape, I32),
            pltpu.SMEM(fork_of.shape, I32),
            pltpu.SMEM(lengths.shape, I32),
            pltpu.VMEM(pairs.shape, BF16),
            pltpu.SemaphoreType.DMA((5,)),
        ],
    )(hbm(prefix_pages), hbm(own_pages), hbm(fork_of), hbm(lengths), hbm(pairs))
    request = swap(request, NEAR + FAR)
    store = prefetch(store, "store_ahead")
    pages = call(
        gather_kernel,
        pltpu.VMEM((SOURCES, CHUNK, HD), BF16),
        [VMEM, VMEM],
        "gather_pages",
        [pltpu.VMEM((POOL, HD), I32), pltpu.SMEM((POOL, HD), I32), pltpu.SemaphoreType.DMA(())],
        out_specs=VMEM,
    )(request, vmem(store))
    pages = swap(pages, NEAR)
    q = query.reshape(ROWS, HD)
    fresh_k = new_kv[:, :, 0, 0].reshape(B * STEPS, HD)
    fresh_v = new_kv[:, :, 1, 0].reshape(B * STEPS, HD)
    local = call(
        local_kernel,
        [shape((ROWS, HD), F32)] * 3,
        [SMEM, SMEM, VMEM, VMEM, VMEM, VMEM],
        "resident",
        [pltpu.VMEM(((B - MIG) * NOWN * PAGE, HD), BF16)] * 2,
        pl.CostEstimate(flops=10**8, bytes_accessed=3 * 2**20, transcendentals=10**5),
    )(own_pages, lengths, q, fresh_k, fresh_v, store)
    parts = call(partial_kernel, shape((MEMBERS * RES, HD), BF16), [VMEM], "partials")(vmem(pages))
    parts = swap(parts.reshape(MEMBERS, RES, HD), FAR).reshape(MEMBERS * RES, HD)
    width = o_weight.shape[1] // TPN
    shares = call(
        finish_kernel,
        shape((TPN, 16, width), BF16),
        [VMEM] * 4 + [HBM],
        "finish",
        [pltpu.VMEM(o_weight.shape, BF16), pltpu.VMEM((ROWS, HD), F32), pltpu.SemaphoreType.DMA((GROUP,))],
    )(parts, *local, hbm(o_weight))
    shares = swap(shares, ("x", "c"))
    return call(total_kernel, shape((B, STEPS, width), BF16), [VMEM], "total")(shares)


def solution(mesh):
    fine = Mesh(mesh.devices.reshape(ZH, ZM, ZL, YN, XN, CN), POOL_AXES + ("x", "c"))
    pool, tp = POOL_AXES, ("x", "c")
    return jax.shard_map(
        shards,
        mesh=fine,
        in_specs=(
            P(pool, None, tp, None),
            P(pool, None, None, tp, None),
            P(pool, None, tp, None, None),
            P(pool, None),
            P(pool),
            P(pool, None),
            P(pool),
            P(tp, None),
        ),
        out_specs=P(pool, None, tp),
        check_vma=False,
    )
```

```python
import math

import jax
import jax.numpy as jnp
from jax import lax
from jax.experimental import pallas as pl
from jax.experimental.pallas import tpu as pltpu
from jax.sharding import Mesh
from jax.sharding import PartitionSpec as P

F32 = jnp.float32
BF16 = jnp.bfloat16
I32 = jnp.int32

HD = 128
PAGE = 16
NPRE = 8
NOWN = 24
ROOTS = 4
B = 8
MIG = 4
STEPS = 2
GROUP = 4
ROWS = B * STEPS * GROUP
SLOTS = 4
P_DEV = 256
NEG = -(2.0**100)
SCALE = 1.0 / math.sqrt(HD)
ZN, YN, XN, CN = 16, 4, 4, 2
ZH, ZM, ZL = 4, 2, 2
PARTS = 1
POOL_AXES = ("zh", "zm", "zl", "y")
NEAR = ("zl", "y")
FAR = ("zm", "zh")
SOURCES = ZL * YN
MEMBERS = ZH * ZM
POOL = ZN * YN
TPN = XN * CN
PREFIX_IDS = ROOTS * NPRE
KEYS = SLOTS * PAGE
PAGE_ROWS = MEMBERS * KEYS
QROWS = STEPS * GROUP
TAIL = MEMBERS * QROWS + 16
CHUNK = 2 * PAGE_ROWS + TAIL
RES = ROWS + 8

VMEM = pl.BlockSpec(memory_space=pltpu.VMEM)
SMEM = pl.BlockSpec(memory_space=pltpu.SMEM)
HBM = pl.BlockSpec(memory_space=pltpu.HBM)
ANY = pl.BlockSpec(memory_space=pl.ANY)
NT = (((1,), (1,)), ((), ()))
NN = (((1,), (0,)), ((), ()))


def iota(shape, dim):
    return lax.broadcasted_iota(I32, shape, dim)


def dot(a, b, dims=NN):
    return lax.dot_general(a, b, dims, preferred_element_type=F32)


def request_kernel(
    prefix_hbm, own_hbm, fork_hbm, length_hbm, query_hbm, req, prefix, own, fork, length, query, sems
):
    pairs = ((prefix_hbm, prefix), (own_hbm, own), (fork_hbm, fork), (length_hbm, length), (query_hbm, query))
    copies = [pltpu.make_async_copy(a, b, sems.at[n]) for n, (a, b) in enumerate(pairs)]
    for copy in copies:
        copy.start()
    for copy in copies:
        copy.wait()
    for b in range(B):
        for n in range(QROWS // 2):
            rows = query[b, n]
            for m in range(MEMBERS):
                req[b * MEMBERS + m, n] = rows
    lane = iota((8, HD), 1)
    row = iota((8, HD), 0)
    ids = jnp.zeros((8, HD), I32)
    for r in range(ROOTS):
        for c in range(NPRE):
            ids = jnp.where(lane == r * NPRE + c, prefix[r, c], ids)
    for r in range(MIG):
        for c in range(NOWN):
            ids = jnp.where(lane == PREFIX_IDS + r * NOWN + c, own[r, c], ids)
    forks = jnp.zeros((8, HD), I32)
    lens = jnp.zeros((8, HD), I32)
    for b in range(B):
        forks = jnp.where(row == b, fork[b], forks)
        lens = jnp.where(row == b, length[b], lens)
    is_prefix = lane < PREFIX_IDS
    moved = jnp.maximum(lane - PREFIX_IDS, 0)
    chunk = jnp.where(is_prefix, lane % NPRE, NPRE + moved % NOWN)
    wanted = (is_prefix & (forks == lane // NPRE)) | (~is_prefix & (row == moved // NOWN))
    tokens = jnp.where(wanted, jnp.clip(lens - PAGE * chunk, 0, PAGE), 0)
    place = jnp.where(row == 0, ids % P_DEV, 0)
    table = jnp.concatenate([tokens, place], 0).astype(F32).astype(BF16)
    holder = ids // P_DEV
    plane, row_y = holder // YN, holder % YN
    member = plane // ZL % ZM * ZH + plane // (ZL * ZM)
    holder = ((plane % ZL) * YN + row_y) * MEMBERS + member
    member = jnp.broadcast_to(holder[0:1], (POOL, HD)) == iota((POOL, HD), 0)
    earlier = (iota((HD, HD), 0) < iota((HD, HD), 1)).astype(F32).astype(BF16)
    rank = dot(member.astype(F32).astype(BF16), earlier)
    out = jnp.zeros((POOL, HD), F32)
    for s in range(SLOTS):
        chosen = jnp.where(member & (rank == float(s)), 1.0, 0.0).astype(BF16)
        parts = [table if k == s else jnp.zeros((16, HD), BF16) for k in range(HD // 16)]
        out = out + dot(chosen, jnp.concatenate(parts, 0), NT)
    for d in range(POOL):
        req[d, QROWS // 2] = jnp.broadcast_to(out[d : d + 1], (2, HD)).astype(BF16)


def prefetch_kernel(source, out, sems):
    part = out.shape[0] // sems.shape[0]
    copies = [
        pltpu.make_async_copy(source.at[pl.ds(n * part, part)], out.at[pl.ds(n * part, part)], sems.at[n])
        for n in range(sems.shape[0])
    ]
    for copy in copies:
        copy.start()
    for copy in copies:
        copy.wait()


def gather_kernel(req, store, out, wanted, places, place_sem):
    row = iota((MEMBERS, HD), 0)
    tails = []
    for c in range(SOURCES):
        asked = jnp.zeros((MEMBERS, HD), F32)
        rows = []
        for n in range(MEMBERS):
            block = req[c * MEMBERS + n].astype(F32)
            rows += [block[k] for k in range(QROWS // 2)]
            asked = jnp.where(row == n, block[QROWS // 2, 0:1], asked)
        wanted[pl.ds(c * MEMBERS, MEMBERS), :] = asked.astype(I32)
        tails.append(rows + [asked, jnp.zeros((16 - MEMBERS, HD), F32)])
    copy = pltpu.make_async_copy(wanted, places, place_sem)
    copy.start()
    for c in range(SOURCES):
        out[c, pl.ds(2 * PAGE_ROWS, TAIL), :] = jnp.concatenate(tails[c], 0).astype(BF16)
    copy.wait()
    for c in range(SOURCES):
        for n in range(MEMBERS):
            for s in range(SLOTS):
                at = places[c * MEMBERS + n, 16 * s + 8]
                start = n * KEYS + s * PAGE
                out[c, pl.ds(start, PAGE), :] = store[at, 0]
                out[c, pl.ds(PAGE_ROWS + start, PAGE), :] = store[at, 1]


def local_kernel(own, length, q, fresh_k, fresh_v, store, sums, top, total, keys, values):
    branches = B - MIG
    span = NOWN * PAGE
    for b in range(branches):
        for p in range(NOWN):
            at = own[MIG + b, p] % P_DEV
            start = b * span + p * PAGE
            keys[pl.ds(start, PAGE), :] = store[at, 0]
            values[pl.ds(start, PAGE), :] = store[at, 1]
    rows = q[...]
    branch_of = iota((ROWS, 1), 0) // QROWS
    step_of = iota((ROWS, 1), 0) // GROUP % STEPS
    lane16 = iota((ROWS, 16), 1)
    score = dot(rows, fresh_k[...], NT) * SCALE
    ok = (lane16 // STEPS == branch_of) & (lane16 % STEPS <= step_of)
    blocks = [(jnp.where(ok, score, NEG), ok, fresh_v[...])]
    position = iota((ROWS, span), 1) + NPRE * PAGE
    for b in range(branches):
        score = dot(rows, keys[pl.ds(b * span, span), :], NT) * SCALE
        ok = (branch_of == MIG + b) & (position < length[MIG + b])
        blocks.append((jnp.where(ok, score, NEG), ok, values[pl.ds(b * span, span), :]))
    best = jnp.max(blocks[0][0], 1, keepdims=True)
    for score, _, _ in blocks[1:]:
        best = jnp.maximum(best, jnp.max(score, 1, keepdims=True))
    acc = jnp.zeros((ROWS, HD), F32)
    count = jnp.zeros((ROWS, 1), F32)
    for score, ok, value in blocks:
        weight = jnp.where(ok, jnp.exp(score - best), 0.0).astype(BF16)
        count = count + jnp.sum(weight.astype(F32), 1, keepdims=True)
        acc = acc + dot(weight, value)
    sums[...] = acc
    top[...] = jnp.broadcast_to(best, (ROWS, HD))
    total[...] = jnp.broadcast_to(count, (ROWS, HD))


def partial_kernel(pages, out):
    per = MEMBERS // PARTS
    pick = iota((B, HD), 1) % 16 == iota((B, HD), 0)
    stacks = []
    asking = []
    for k in range(SOURCES):
        tail = pages[k, pl.ds(2 * PAGE_ROWS, TAIL), :].astype(F32)
        asking.append(tail)
        tile = tail[MEMBERS * QROWS : MEMBERS * QROWS + MEMBERS]
        rows = [jnp.where(pick, jnp.broadcast_to(tile[n : n + 1], (B, HD)), 0.0) for n in range(MEMBERS)]
        stacks.append(jnp.concatenate(rows, 0).astype(BF16))
    pairs = [jnp.concatenate(stacks[k : k + 2], 1) for k in range(0, SOURCES, 2)]
    shape = (2 * HD, 2 * KEYS)
    expand = iota(shape, 0) // HD * KEYS + (iota(shape, 0) % HD) // 16 * PAGE == iota(shape, 1) // PAGE * PAGE
    expand = expand & (iota(shape, 0) % HD < KEYS)
    tokens = dot(jnp.concatenate(pairs, 0), expand.astype(F32).astype(BF16))
    number = (iota((tokens.shape[0], 2 * KEYS), 1) % PAGE).astype(F32)
    mask = jnp.where(number < tokens, 0.0, NEG)
    column = iota((ROWS, HD), 1)
    row = iota((8, HD), 0)
    for part in range(PARTS):
        members = range(part * per, (part + 1) * per)
        scores = []
        for z in members:
            keys = jnp.concatenate([pages[k, pl.ds(z * KEYS, KEYS), :] for k in range(SOURCES)], 0)
            queries = jnp.concatenate([tail[z * QROWS : (z + 1) * QROWS] for tail in asking], 0).astype(BF16)
            scores.append(dot(queries, keys, NT))
        stats = jnp.zeros((ROWS, HD), F32)
        weights = []
        for n, z in enumerate(members):
            rows = range(z * B, SOURCES // 2 * MEMBERS * B, MEMBERS * B)
            bias = jnp.concatenate([mask[r : r + B] for r in rows], 1)
            bias = jnp.concatenate([jnp.broadcast_to(bias[b : b + 1], (QROWS, bias.shape[1])) for b in range(B)], 0)
            score = jnp.where(bias < 0.0, NEG, scores[n] * SCALE)
            best = jnp.max(score, 1, keepdims=True).astype(BF16).astype(F32)
            weight = jnp.where(bias < 0.0, 0.0, jnp.exp(score - best)).astype(BF16)
            count = jnp.sum(weight.astype(F32), 1, keepdims=True)
            weights.append(weight)
            stats = jnp.where(column == n, best, jnp.where(column == 8 + n, count, stats))
        turned = jnp.transpose(stats)[0:16]
        turned = jnp.concatenate([turned, jnp.zeros((16, HD - ROWS), F32)], 1)
        tops, counts = turned[0:8], turned[8:16]
        high = counts.astype(BF16).astype(F32)
        low = counts - high
        rows = []
        for n, z in enumerate(members):
            values = jnp.concatenate([pages[k, pl.ds(PAGE_ROWS + z * KEYS, KEYS), :] for k in range(SOURCES)], 0)
            tile = jnp.where(row == 1, high[n : n + 1], jnp.where(row == 2, low[n : n + 1], 0.0))
            rows += [dot(weights[n], values), jnp.where(row == 0, tops[n : n + 1], tile)]
        out[pl.ds(part * per * RES, per * RES), :] = jnp.concatenate(rows, 0).astype(BF16)


def finish_kernel(parts, sums, top, total, weight_hbm, out, weight, rows, sems):
    copies = [
        pltpu.make_async_copy(weight_hbm.at[pl.ds(g * HD, HD), :], weight.at[pl.ds(g * HD, HD), :], sems.at[g])
        for g in range(GROUP)
    ]
    for copy in copies:
        copy.start()
    row = iota((8, HD), 0)
    tops = jnp.full((8, HD), NEG, F32)
    counts = jnp.zeros((8, HD), F32)
    received = []
    for z in range(0, MEMBERS, 2):
        pair = parts[pl.ds(z * RES, 2 * RES), :].astype(F32)
        received += [pair[0:RES], pair[RES : 2 * RES]]
    for z in range(MEMBERS):
        tile = received[z][ROWS:RES]
        tops = jnp.where(row == z, tile[0:1], tops)
        counts = jnp.where(row == z, tile[1:2] + tile[2:3], counts)
    tops = jnp.concatenate([tops, jnp.full((HD - 8, HD), NEG, F32)], 0)
    counts = jnp.concatenate([counts, jnp.zeros((HD - 8, HD), F32)], 0)
    tops = jnp.transpose(tops)[0:ROWS]
    counts = jnp.transpose(counts)[0:ROWS]
    own_top = top[...]
    best = jnp.maximum(jnp.max(tops, 1, keepdims=True), own_top)
    factor = jnp.exp(tops - best)
    own_factor = jnp.exp(own_top - best)
    denominator = jnp.sum(factor * counts, 1, keepdims=True) + own_factor * total[...]
    numerator = own_factor * sums[...]
    for z in range(MEMBERS):
        numerator = numerator + factor[:, z : z + 1] * received[z][0:ROWS]
    rows[...] = numerator / denominator
    result = jnp.zeros((16, weight.shape[1]), F32)
    for g in range(GROUP):
        copies[g].wait()
        attended = rows[pl.ds(g, 16, stride=GROUP), :].astype(BF16)
        result = result + dot(attended, weight[pl.ds(g * HD, HD), :])
    result = result.astype(BF16).astype(F32)
    width = out.shape[2]
    for k in range(TPN):
        out[k] = result[:, k * width : (k + 1) * width].astype(BF16)


def total_kernel(shares, out):
    total = shares[0].astype(F32)
    for k in range(1, TPN):
        total = total + shares[k].astype(F32)
    total = total.astype(BF16).astype(F32)
    for b in range(B):
        out[b] = total[STEPS * b : STEPS * (b + 1)].astype(BF16)


def call(kernel, out_shape, in_specs, name, scratch=(), cost=None, mib=12, out_specs=None):
    return pl.pallas_call(
        kernel,
        out_shape=out_shape,
        in_specs=in_specs,
        out_specs=jax.tree.map(lambda _: VMEM, out_shape) if out_specs is None else out_specs,
        scratch_shapes=scratch,
        cost_estimate=cost,
        compiler_params=pltpu.CompilerParams(vmem_limit_bytes=mib * 2**20),
        name=name,
    )


def hbm(x):
    return pltpu.with_memory_space_constraint(x, pltpu.HBM)


def vmem(x):
    return pltpu.with_memory_space_constraint(x, pltpu.VMEM)


def prefetch(x, name):
    return call(
        prefetch_kernel,
        pltpu.VMEM(x.shape, x.dtype),
        [HBM],
        name,
        [pltpu.SemaphoreType.DMA((8,))],
        out_specs=VMEM,
    )(hbm(x))


def swap(x, axes):
    return lax.all_to_all(x, axes, split_axis=0, concat_axis=0, tiled=True)


def shards(query, new_kv, kv_store, prefix_pages, fork_of, own_pages, lengths, o_weight):
    shape = jax.ShapeDtypeStruct
    store = kv_store.reshape(P_DEV, 2, PAGE, HD)
    pairs = query.reshape(B, QROWS // 2, 2, HD)
    request = call(
        request_kernel,
        shape((POOL, QROWS // 2 + 1, 2, HD), BF16),
        [HBM] * 5,
        "request",
        [
            pltpu.SMEM(prefix_pages.shape, I32),
            pltpu.SMEM(own_pages.shape, I32),
            pltpu.SMEM(fork_of.shape, I32),
            pltpu.SMEM(lengths.shape, I32),
            pltpu.VMEM(pairs.shape, BF16),
            pltpu.SemaphoreType.DMA((5,)),
        ],
    )(hbm(prefix_pages), hbm(own_pages), hbm(fork_of), hbm(lengths), hbm(pairs))
    request = swap(request, NEAR + FAR)
    store = prefetch(store, "store_ahead")
    q = query.reshape(ROWS, HD)
    fresh_k = new_kv[:, :, 0, 0].reshape(B * STEPS, HD)
    fresh_v = new_kv[:, :, 1, 0].reshape(B * STEPS, HD)
    local = call(
        local_kernel,
        [shape((ROWS, HD), F32)] * 3,
        [SMEM, SMEM, VMEM, VMEM, VMEM, VMEM],
        "resident",
        [pltpu.VMEM(((B - MIG) * NOWN * PAGE, HD), BF16)] * 2,
        pl.CostEstimate(flops=10**8, bytes_accessed=3 * 2**20, transcendentals=10**5),
    )(own_pages, lengths, q, fresh_k, fresh_v, store)
    request, *local = lax.optimization_barrier((request, *local))
    pages = call(
        gather_kernel,
        pltpu.VMEM((SOURCES, CHUNK, HD), BF16),
        [VMEM, VMEM],
        "gather_pages",
        [pltpu.VMEM((POOL, HD), I32), pltpu.SMEM((POOL, HD), I32), pltpu.SemaphoreType.DMA(())],
        out_specs=VMEM,
    )(request, vmem(store))
    pages = swap(pages, NEAR)
    parts = call(partial_kernel, shape((MEMBERS * RES, HD), BF16), [VMEM], "partials")(vmem(pages))
    parts = swap(parts.reshape(MEMBERS, RES, HD), FAR).reshape(MEMBERS * RES, HD)
    width = o_weight.shape[1] // TPN
    shares = call(
        finish_kernel,
        shape((TPN, 16, width), BF16),
        [VMEM] * 4 + [HBM],
        "finish",
        [pltpu.VMEM(o_weight.shape, BF16), pltpu.VMEM((ROWS, HD), F32), pltpu.SemaphoreType.DMA((GROUP,))],
    )(parts, *local, hbm(o_weight))
    shares = swap(shares, ("x", "c"))
    return call(total_kernel, shape((B, STEPS, width), BF16), [VMEM], "total")(shares)


def solution(mesh):
    fine = Mesh(mesh.devices.reshape(ZH, ZM, ZL, YN, XN, CN), POOL_AXES + ("x", "c"))
    pool, tp = POOL_AXES, ("x", "c")
    return jax.shard_map(
        shards,
        mesh=fine,
        in_specs=(
            P(pool, None, tp, None),
            P(pool, None, None, tp, None),
            P(pool, None, tp, None, None),
            P(pool, None),
            P(pool),
            P(pool, None),
            P(pool),
            P(tp, None),
        ),
        out_specs=P(pool, None, tp),
        check_vma=False,
    )
```

```python
import math

import jax
import jax.numpy as jnp
from jax import lax
from jax.experimental import pallas as pl
from jax.experimental.pallas import tpu as pltpu
from jax.sharding import Mesh
from jax.sharding import PartitionSpec as P

F32 = jnp.float32
BF16 = jnp.bfloat16
I32 = jnp.int32

HD = 128
PAGE = 16
NPRE = 8
NOWN = 24
ROOTS = 4
B = 8
MIG = 4
STEPS = 2
GROUP = 4
ROWS = B * STEPS * GROUP
SLOTS = 4
P_DEV = 256
NEG = -(2.0**100)
SCALE = 1.0 / math.sqrt(HD)
ZN, YN, XN, CN = 16, 4, 4, 2
ZH, ZM, ZL = 4, 2, 2
PARTS = 1
POOL_AXES = ("zh", "zm", "zl", "y")
NEAR = ("zl", "y")
FAR = ("zm", "zh")
SOURCES = ZL * YN
MEMBERS = ZH * ZM
POOL = ZN * YN
TPN = XN * CN
PREFIX_IDS = ROOTS * NPRE
KEYS = SLOTS * PAGE
PAGE_ROWS = MEMBERS * KEYS
QROWS = STEPS * GROUP
TAIL = MEMBERS * QROWS + 16
CHUNK = 2 * PAGE_ROWS + TAIL
RES = ROWS + 8

VMEM = pl.BlockSpec(memory_space=pltpu.VMEM)
SMEM = pl.BlockSpec(memory_space=pltpu.SMEM)
HBM = pl.BlockSpec(memory_space=pltpu.HBM)
ANY = pl.BlockSpec(memory_space=pl.ANY)
NT = (((1,), (1,)), ((), ()))
NN = (((1,), (0,)), ((), ()))


def iota(shape, dim):
    return lax.broadcasted_iota(I32, shape, dim)


def dot(a, b, dims=NN):
    return lax.dot_general(a, b, dims, preferred_element_type=F32)


def request_kernel(
    prefix_hbm, own_hbm, fork_hbm, length_hbm, query_hbm, req, prefix, own, fork, length, query, sems
):
    pairs = ((prefix_hbm, prefix), (own_hbm, own), (fork_hbm, fork), (length_hbm, length), (query_hbm, query))
    copies = [pltpu.make_async_copy(a, b, sems.at[n]) for n, (a, b) in enumerate(pairs)]
    for copy in copies:
        copy.start()
    for copy in copies:
        copy.wait()
    for b in range(B):
        for n in range(QROWS // 2):
            rows = query[b, n]
            for m in range(MEMBERS):
                req[m * SOURCES + b, n] = rows
    lane = iota((8, HD), 1)
    row = iota((8, HD), 0)
    ids = jnp.zeros((8, HD), I32)
    for r in range(ROOTS):
        for c in range(NPRE):
            ids = jnp.where(lane == r * NPRE + c, prefix[r, c], ids)
    for r in range(MIG):
        for c in range(NOWN):
            ids = jnp.where(lane == PREFIX_IDS + r * NOWN + c, own[r, c], ids)
    forks = jnp.zeros((8, HD), I32)
    lens = jnp.zeros((8, HD), I32)
    for b in range(B):
        forks = jnp.where(row == b, fork[b], forks)
        lens = jnp.where(row == b, length[b], lens)
    is_prefix = lane < PREFIX_IDS
    moved = jnp.maximum(lane - PREFIX_IDS, 0)
    chunk = jnp.where(is_prefix, lane % NPRE, NPRE + moved % NOWN)
    wanted = (is_prefix & (forks == lane // NPRE)) | (~is_prefix & (row == moved // NOWN))
    tokens = jnp.where(wanted, jnp.clip(lens - PAGE * chunk, 0, PAGE), 0)
    place = jnp.where(row == 0, ids % P_DEV, 0)
    table = jnp.concatenate([tokens, place], 0).astype(F32).astype(BF16)
    holder = ids // P_DEV
    plane, row_y = holder // YN, holder % YN
    member = plane // ZL % ZM * ZH + plane // (ZL * ZM)
    holder = member * SOURCES + (plane % ZL) * YN + row_y
    member = jnp.broadcast_to(holder[0:1], (POOL, HD)) == iota((POOL, HD), 0)
    earlier = (iota((HD, HD), 0) < iota((HD, HD), 1)).astype(F32).astype(BF16)
    rank = dot(member.astype(F32).astype(BF16), earlier)
    out = jnp.zeros((POOL, HD), F32)
    for s in range(SLOTS):
        chosen = jnp.where(member & (rank == float(s)), 1.0, 0.0).astype(BF16)
        parts = [table if k == s else jnp.zeros((16, HD), BF16) for k in range(HD // 16)]
        out = out + dot(chosen, jnp.concatenate(parts, 0), NT)
    for d in range(POOL):
        req[d, QROWS // 2] = jnp.broadcast_to(out[d : d + 1], (2, HD)).astype(BF16)


def prefetch_kernel(source, out, sems):
    part = out.shape[0] // sems.shape[0]
    copies = [
        pltpu.make_async_copy(source.at[pl.ds(n * part, part)], out.at[pl.ds(n * part, part)], sems.at[n])
        for n in range(sems.shape[0])
    ]
    for copy in copies:
        copy.start()
    for copy in copies:
        copy.wait()


def gather_kernel(req, store, out, wanted, places, place_sem):
    row = iota((MEMBERS, HD), 0)
    tails = []
    for c in range(SOURCES):
        asked = jnp.zeros((MEMBERS, HD), F32)
        rows = []
        for n in range(MEMBERS):
            block = req[n * SOURCES + c].astype(F32)
            rows += [block[k] for k in range(QROWS // 2)]
            asked = jnp.where(row == n, block[QROWS // 2, 0:1], asked)
        wanted[pl.ds(c * MEMBERS, MEMBERS), :] = asked.astype(I32)
        tails.append(rows + [asked, jnp.zeros((16 - MEMBERS, HD), F32)])
    copy = pltpu.make_async_copy(wanted, places, place_sem)
    copy.start()
    for c in range(SOURCES):
        out[c, pl.ds(2 * PAGE_ROWS, TAIL), :] = jnp.concatenate(tails[c], 0).astype(BF16)
    copy.wait()
    for c in range(SOURCES):
        for n in range(MEMBERS):
            for s in range(SLOTS):
                at = places[c * MEMBERS + n, 16 * s + 8]
                start = n * KEYS + s * PAGE
                out[c, pl.ds(start, PAGE), :] = store[at, 0]
                out[c, pl.ds(PAGE_ROWS + start, PAGE), :] = store[at, 1]


def local_kernel(own, length, q, fresh_k, fresh_v, store, sums, top, total, keys, values):
    branches = B - MIG
    span = NOWN * PAGE
    for b in range(branches):
        for p in range(NOWN):
            at = own[MIG + b, p] % P_DEV
            start = b * span + p * PAGE
            keys[pl.ds(start, PAGE), :] = store[at, 0]
            values[pl.ds(start, PAGE), :] = store[at, 1]
    rows = q[...]
    branch_of = iota((ROWS, 1), 0) // QROWS
    step_of = iota((ROWS, 1), 0) // GROUP % STEPS
    lane16 = iota((ROWS, 16), 1)
    score = dot(rows, fresh_k[...], NT) * SCALE
    ok = (lane16 // STEPS == branch_of) & (lane16 % STEPS <= step_of)
    blocks = [(jnp.where(ok, score, NEG), ok, fresh_v[...])]
    position = iota((ROWS, span), 1) + NPRE * PAGE
    for b in range(branches):
        score = dot(rows, keys[pl.ds(b * span, span), :], NT) * SCALE
        ok = (branch_of == MIG + b) & (position < length[MIG + b])
        blocks.append((jnp.where(ok, score, NEG), ok, values[pl.ds(b * span, span), :]))
    best = jnp.max(blocks[0][0], 1, keepdims=True)
    for score, _, _ in blocks[1:]:
        best = jnp.maximum(best, jnp.max(score, 1, keepdims=True))
    acc = jnp.zeros((ROWS, HD), F32)
    count = jnp.zeros((ROWS, 1), F32)
    for score, ok, value in blocks:
        weight = jnp.where(ok, jnp.exp(score - best), 0.0).astype(BF16)
        count = count + jnp.sum(weight.astype(F32), 1, keepdims=True)
        acc = acc + dot(weight, value)
    sums[...] = acc
    top[...] = jnp.broadcast_to(best, (ROWS, HD))
    total[...] = jnp.broadcast_to(count, (ROWS, HD))


def partial_kernel(pages, out):
    per = MEMBERS // PARTS
    pick = iota((B, HD), 1) % 16 == iota((B, HD), 0)
    stacks = []
    asking = []
    for k in range(SOURCES):
        tail = pages[k, pl.ds(2 * PAGE_ROWS, TAIL), :].astype(F32)
        asking.append(tail)
        tile = tail[MEMBERS * QROWS : MEMBERS * QROWS + MEMBERS]
        rows = [jnp.where(pick, jnp.broadcast_to(tile[n : n + 1], (B, HD)), 0.0) for n in range(MEMBERS)]
        stacks.append(jnp.concatenate(rows, 0).astype(BF16))
    pairs = [jnp.concatenate(stacks[k : k + 2], 1) for k in range(0, SOURCES, 2)]
    shape = (2 * HD, 2 * KEYS)
    expand = iota(shape, 0) // HD * KEYS + (iota(shape, 0) % HD) // 16 * PAGE == iota(shape, 1) // PAGE * PAGE
    expand = expand & (iota(shape, 0) % HD < KEYS)
    tokens = dot(jnp.concatenate(pairs, 0), expand.astype(F32).astype(BF16))
    number = (iota((tokens.shape[0], 2 * KEYS), 1) % PAGE).astype(F32)
    mask = jnp.where(number < tokens, 0.0, NEG)
    column = iota((ROWS, HD), 1)
    row = iota((8, HD), 0)
    for part in range(PARTS):
        members = range(part * per, (part + 1) * per)
        scores = []
        for z in members:
            keys = jnp.concatenate([pages[k, pl.ds(z * KEYS, KEYS), :] for k in range(SOURCES)], 0)
            queries = jnp.concatenate([tail[z * QROWS : (z + 1) * QROWS] for tail in asking], 0).astype(BF16)
            scores.append(dot(queries, keys, NT))
        stats = jnp.zeros((ROWS, HD), F32)
        weights = []
        for n, z in enumerate(members):
            rows = range(z * B, SOURCES // 2 * MEMBERS * B, MEMBERS * B)
            bias = jnp.concatenate([mask[r : r + B] for r in rows], 1)
            bias = jnp.concatenate([jnp.broadcast_to(bias[b : b + 1], (QROWS, bias.shape[1])) for b in range(B)], 0)
            score = jnp.where(bias < 0.0, NEG, scores[n] * SCALE)
            best = jnp.max(score, 1, keepdims=True).astype(BF16).astype(F32)
            weight = jnp.where(bias < 0.0, 0.0, jnp.exp(score - best)).astype(BF16)
            count = jnp.sum(weight.astype(F32), 1, keepdims=True)
            weights.append(weight)
            stats = jnp.where(column == n, best, jnp.where(column == 8 + n, count, stats))
        turned = jnp.transpose(stats)[0:16]
        turned = jnp.concatenate([turned, jnp.zeros((16, HD - ROWS), F32)], 1)
        tops, counts = turned[0:8], turned[8:16]
        high = counts.astype(BF16).astype(F32)
        low = counts - high
        rows = []
        for n, z in enumerate(members):
            values = jnp.concatenate([pages[k, pl.ds(PAGE_ROWS + z * KEYS, KEYS), :] for k in range(SOURCES)], 0)
            tile = jnp.where(row == 1, high[n : n + 1], jnp.where(row == 2, low[n : n + 1], 0.0))
            rows += [dot(weights[n], values), jnp.where(row == 0, tops[n : n + 1], tile)]
        out[pl.ds(part * per * RES, per * RES), :] = jnp.concatenate(rows, 0).astype(BF16)


def finish_kernel(parts, sums, top, total, weight_hbm, out, weight, rows, sems):
    copies = [
        pltpu.make_async_copy(weight_hbm.at[pl.ds(g * HD, HD), :], weight.at[pl.ds(g * HD, HD), :], sems.at[g])
        for g in range(GROUP)
    ]
    for copy in copies:
        copy.start()
    row = iota((8, HD), 0)
    tops = jnp.full((8, HD), NEG, F32)
    counts = jnp.zeros((8, HD), F32)
    received = []
    for z in range(0, MEMBERS, 2):
        pair = parts[pl.ds(z * RES, 2 * RES), :].astype(F32)
        received += [pair[0:RES], pair[RES : 2 * RES]]
    for z in range(MEMBERS):
        tile = received[z][ROWS:RES]
        tops = jnp.where(row == z, tile[0:1], tops)
        counts = jnp.where(row == z, tile[1:2] + tile[2:3], counts)
    tops = jnp.concatenate([tops, jnp.full((HD - 8, HD), NEG, F32)], 0)
    counts = jnp.concatenate([counts, jnp.zeros((HD - 8, HD), F32)], 0)
    tops = jnp.transpose(tops)[0:ROWS]
    counts = jnp.transpose(counts)[0:ROWS]
    own_top = top[...]
    best = jnp.maximum(jnp.max(tops, 1, keepdims=True), own_top)
    factor = jnp.exp(tops - best)
    own_factor = jnp.exp(own_top - best)
    denominator = jnp.sum(factor * counts, 1, keepdims=True) + own_factor * total[...]
    numerator = own_factor * sums[...]
    for z in range(MEMBERS):
        numerator = numerator + factor[:, z : z + 1] * received[z][0:ROWS]
    rows[...] = numerator / denominator
    result = jnp.zeros((16, weight.shape[1]), F32)
    for g in range(GROUP):
        copies[g].wait()
        attended = rows[pl.ds(g, 16, stride=GROUP), :].astype(BF16)
        result = result + dot(attended, weight[pl.ds(g * HD, HD), :])
    result = result.astype(BF16).astype(F32)
    width = out.shape[2]
    for k in range(TPN):
        out[k] = result[:, k * width : (k + 1) * width].astype(BF16)


def total_kernel(shares, out):
    total = shares[0].astype(F32)
    for k in range(1, TPN):
        total = total + shares[k].astype(F32)
    total = total.astype(BF16).astype(F32)
    for b in range(B):
        out[b] = total[STEPS * b : STEPS * (b + 1)].astype(BF16)


def call(kernel, out_shape, in_specs, name, scratch=(), cost=None, mib=12, out_specs=None):
    return pl.pallas_call(
        kernel,
        out_shape=out_shape,
        in_specs=in_specs,
        out_specs=jax.tree.map(lambda _: VMEM, out_shape) if out_specs is None else out_specs,
        scratch_shapes=scratch,
        cost_estimate=cost,
        compiler_params=pltpu.CompilerParams(vmem_limit_bytes=mib * 2**20),
        name=name,
    )


def hbm(x):
    return pltpu.with_memory_space_constraint(x, pltpu.HBM)


def vmem(x):
    return pltpu.with_memory_space_constraint(x, pltpu.VMEM)


def prefetch(x, name):
    return call(
        prefetch_kernel,
        pltpu.VMEM(x.shape, x.dtype),
        [HBM],
        name,
        [pltpu.SemaphoreType.DMA((8,))],
        out_specs=VMEM,
    )(hbm(x))


def swap(x, axes):
    return lax.all_to_all(x, axes, split_axis=0, concat_axis=0, tiled=True)


def shards(query, new_kv, kv_store, prefix_pages, fork_of, own_pages, lengths, o_weight):
    shape = jax.ShapeDtypeStruct
    store = kv_store.reshape(P_DEV, 2, PAGE, HD)
    pairs = query.reshape(B, QROWS // 2, 2, HD)
    request = call(
        request_kernel,
        shape((POOL, QROWS // 2 + 1, 2, HD), BF16),
        [HBM] * 5,
        "request",
        [
            pltpu.SMEM(prefix_pages.shape, I32),
            pltpu.SMEM(own_pages.shape, I32),
            pltpu.SMEM(fork_of.shape, I32),
            pltpu.SMEM(lengths.shape, I32),
            pltpu.VMEM(pairs.shape, BF16),
            pltpu.SemaphoreType.DMA((5,)),
        ],
    )(hbm(prefix_pages), hbm(own_pages), hbm(fork_of), hbm(lengths), hbm(pairs))
    request = swap(request, FAR + NEAR)
    store = prefetch(store, "store_ahead")
    q = query.reshape(ROWS, HD)
    fresh_k = new_kv[:, :, 0, 0].reshape(B * STEPS, HD)
    fresh_v = new_kv[:, :, 1, 0].reshape(B * STEPS, HD)
    local = call(
        local_kernel,
        [shape((ROWS, HD), F32)] * 3,
        [SMEM, SMEM, VMEM, VMEM, VMEM, VMEM],
        "resident",
        [pltpu.VMEM(((B - MIG) * NOWN * PAGE, HD), BF16)] * 2,
        pl.CostEstimate(flops=10**8, bytes_accessed=3 * 2**20, transcendentals=10**5),
    )(own_pages, lengths, q, fresh_k, fresh_v, store)
    request, *local = lax.optimization_barrier((request, *local))
    pages = call(
        gather_kernel,
        pltpu.VMEM((SOURCES, CHUNK, HD), BF16),
        [VMEM, VMEM],
        "gather_pages",
        [pltpu.VMEM((POOL, HD), I32), pltpu.SMEM((POOL, HD), I32), pltpu.SemaphoreType.DMA(())],
        out_specs=VMEM,
    )(request, vmem(store))
    pages = swap(pages, NEAR)
    parts = call(partial_kernel, shape((MEMBERS * RES, HD), BF16), [VMEM], "partials")(vmem(pages))
    parts = swap(parts.reshape(MEMBERS, RES, HD), FAR).reshape(MEMBERS * RES, HD)
    width = o_weight.shape[1] // TPN
    shares = call(
        finish_kernel,
        shape((TPN, 16, width), BF16),
        [VMEM] * 4 + [HBM],
        "finish",
        [pltpu.VMEM(o_weight.shape, BF16), pltpu.VMEM((ROWS, HD), F32), pltpu.SemaphoreType.DMA((GROUP,))],
    )(parts, *local, hbm(o_weight))
    shares = swap(shares, ("x", "c"))
    return call(total_kernel, shape((B, STEPS, width), BF16), [VMEM], "total")(shares)


def solution(mesh):
    fine = Mesh(mesh.devices.reshape(ZH, ZM, ZL, YN, XN, CN), POOL_AXES + ("x", "c"))
    pool, tp = POOL_AXES, ("x", "c")
    return jax.shard_map(
        shards,
        mesh=fine,
        in_specs=(
            P(pool, None, tp, None),
            P(pool, None, None, tp, None),
            P(pool, None, tp, None, None),
            P(pool, None),
            P(pool),
            P(pool, None),
            P(pool),
            P(tp, None),
        ),
        out_specs=P(pool, None, tp),
        check_vma=False,
    )
```
